32 devices in a mesh: dp: 2 (over y), fsdp: 16 (over z, x, core).
Axes of the slice: x: 2, y: 2, z: 4, core: 2. Of those that a mesh axis runs over, the one named last changes fastest.
Arguments:
- act_short: bfloat16 [8192, 768], P(('dp', 'fsdp')), may hold values from -6 to 6
- act_long: bfloat16 [16384, 768], P(('dp', 'fsdp')), may hold values from -6 to 6
- cot_short: bfloat16 [8192, 768], P(('dp', 'fsdp')), may hold values from -6 to 6
- cot_long: bfloat16 [16384, 768], P(('dp', 'fsdp')), may hold values from -6 to 6
- len_short: int32 [32], P(('dp', 'fsdp')), may hold values from 128 to 256, as said below
- len_long: int32 [32], P(('dp', 'fsdp')), may hold values from 256 to 512, as said below
- attn_in: bfloat16 [3, 768, 768], P(None, ('dp', 'fsdp')), may hold values from -0.21875 to 0.21875
- conv_taps: bfloat16 [3, 3, 768], P(None, None, ('dp', 'fsdp')), may hold values from -3 to 3
- w_out: bfloat16 [768, 768], P(('dp', 'fsdp')), may hold values from -1.25 to 1.25
- w_up: bfloat16 [768, 3072], P(('dp', 'fsdp')), may hold values from -0.21875 to 0.21875
- w_down: bfloat16 [3072, 768], P(('dp', 'fsdp')), may hold values from -0.109375 to 0.109375
- gains: bfloat16 [2, 768], P(None, ('dp', 'fsdp')), may hold values from 0.5 to 1.5
- mom_attn_in: float32 [3, 768, 768], P(None, ('dp', 'fsdp')), may hold values from -512 to 512
- mom_conv_taps: float32 [3, 3, 768], P(None, None, ('dp', 'fsdp')), may hold values from -512 to 512
- mom_w_out: float32 [768, 768], P(('dp', 'fsdp')), may hold values from -160 to 160
- mom_w_up: float32 [768, 3072], P(('dp', 'fsdp')), may hold values from -768 to 768
- mom_w_down: float32 [3072, 768], P(('dp', 'fsdp')), may hold values from -1280 to 1280
- mom_gains: float32 [2, 768], P(None, ('dp', 'fsdp')), may hold values from -1024 to 1024
- avg_attn_in: float32 [3, 768, 768], P(None, ('dp', 'fsdp')), may hold values from -0.21875 to 0.21875
- avg_conv_taps: float32 [3, 3, 768], P(None, None, ('dp', 'fsdp')), may hold values from -3 to 3
- avg_w_out: float32 [768, 768], P(('dp', 'fsdp')), may hold values from -1.25 to 1.25
- avg_w_up: float32 [768, 3072], P(('dp', 'fsdp')), may hold values from -0.21875 to 0.21875
- avg_w_down: float32 [3072, 768], P(('dp', 'fsdp')), may hold values from -0.109375 to 0.109375
- avg_gains: float32 [2, 768], P(None, ('dp', 'fsdp')), may hold values from 0.5 to 1.5
Outputs:
- block_short: bfloat16 [8192, 768], P(('dp', 'fsdp'))
- block_long: bfloat16 [16384, 768], P(('dp', 'fsdp'))
- back_short: float32 [8192, 768], P(('dp', 'fsdp'))
- back_long: float32 [16384, 768], P(('dp', 'fsdp'))
- grad_attn_in: float32 [3, 768, 768], P(None, ('dp', 'fsdp'))
- moment_attn_in: float32 [3, 768, 768], P(None, ('dp', 'fsdp'))
- new_attn_in: float32 [3, 768, 768], P(None, ('dp', 'fsdp'))
- average_attn_in: float32 [3, 768, 768], P(None, ('dp', 'fsdp'))
- grad_conv_taps: float32 [3, 3, 768], P(None, None, ('dp', 'fsdp'))
- moment_conv_taps: float32 [3, 3, 768], P(None, None, ('dp', 'fsdp'))
- new_conv_taps: float32 [3, 3, 768], P(None, None, ('dp', 'fsdp'))
- average_conv_taps: float32 [3, 3, 768], P(None, None, ('dp', 'fsdp'))
- grad_w_out: float32 [768, 768], P(('dp', 'fsdp'))
- moment_w_out: float32 [768, 768], P(('dp', 'fsdp'))
- new_w_out: float32 [768, 768], P(('dp', 'fsdp'))
- average_w_out: float32 [768, 768], P(('dp', 'fsdp'))
- grad_w_up: float32 [768, 3072], P(('dp', 'fsdp'))
- moment_w_up: float32 [768, 3072], P(('dp', 'fsdp'))
- new_w_up: float32 [768, 3072], P(('dp', 'fsdp'))
- average_w_up: float32 [768, 3072], P(('dp', 'fsdp'))
- grad_w_down: float32 [3072, 768], P(('dp', 'fsdp'))
- moment_w_down: float32 [3072, 768], P(('dp', 'fsdp'))
- new_w_down: float32 [3072, 768], P(('dp', 'fsdp'))
- average_w_down: float32 [3072, 768], P(('dp', 'fsdp'))
- grad_gains: float32 [2, 768], P(None, ('dp', 'fsdp'))
- moment_gains: float32 [2, 768], P(None, ('dp', 'fsdp'))
- new_gains: float32 [2, 768], P(None, ('dp', 'fsdp'))
- average_gains: float32 [2, 768], P(None, ('dp', 'fsdp'))
The draws below stay inside these ranges and needn't reach their ends.
Inputs may be any that keep to these rules, and one draw needn't show every extreme that they name: `len_short`: entry i is the count of real tokens in the sequence of rows i * 256 onward of the short group; some sequence has exactly 256. `len_long`: entry i is the count of real tokens in the sequence of rows i * 512 onward of the long group; some sequence has exactly 512.
All inputs are finite; a program needn't handle non-finite values.
Results may differ from the reference program's by a relative error of at most 0.014.
The reference program's roundings to bfloat16 on the way count: a program that leaves them out, or rounds other values in their place, can miss the bound.
Values may be sent and summed in bfloat16 or wider, within the bound.
No kernel may reach another device: no remote copies, remote signals or barrier semaphores. Data moves between devices by JAX's collectives and lax.ppermute only.
A program may use at most 256 MiB of HBM per device.

```python
import math
import jax
import jax.numpy as jnp
from jax import lax

D = 768
HEADS = 12
HEAD_DIM = 64
FF = 3072
LEN_A = 256
LEN_B = 512
TOKENS_A = 8192
TOKENS_B = 16384


def ragged_lengths(seed_key, longest, count_rows):
    draw_key, pick_key = jax.random.split(seed_key)
    drawn_values = jax.random.randint(draw_key, (count_rows,), longest // 2, longest + 1)
    chosen = jax.random.randint(pick_key, (), 0, count_rows)
    return jnp.where(jnp.arange(count_rows) == chosen, longest, drawn_values).astype(jnp.int32)


def draw_len_short(key, part):
    key = jax.random.fold_in(key, 11)
    return ragged_lengths(key, LEN_A, TOKENS_A // LEN_A)


def draw_len_long(key, part):
    key = jax.random.fold_in(key, 23)
    return ragged_lengths(key, LEN_B, TOKENS_B // LEN_B)


def with_spikes(values, rng, source, target, blocks, factor):
    def block_of(axis_at):
        return (jnp.arange(values.shape[axis_at]) // (values.shape[axis_at] // blocks)).reshape((-1,) + (1,) * (values.ndim - 1 - axis_at))

    near = jax.random.permutation(rng, blocks)[block_of(target)]
    far = (block_of(target) + blocks // 2) % blocks
    return jnp.where((block_of(source) == near) | (block_of(source) == far), factor * values, values)


def levels(rng, extent, cuts, low, top_value):
    def one(dim, blocks):
        heights = jax.random.uniform(jax.random.fold_in(jax.random.fold_in(rng, 6), dim), (blocks,), jnp.float32, low / len(cuts), top_value / len(cuts))
        return jnp.repeat(jnp.exp(heights), extent[dim] // blocks).reshape((-1,) + (1,) * (len(extent) - dim - 1))

    factor_of = one(*cuts[0])
    for cut in cuts[1:]:
        factor_of = factor_of * one(*cut)
    return factor_of


def centred(own_key, extent, scale, most, cuts=(), kind=jnp.bfloat16):
    drawn = scale * jax.random.normal(own_key, extent, jnp.float32)
    if cuts:
        drawn = drawn * levels(own_key, extent, cuts, -0.22, 0.18)
    return jnp.clip(drawn, -most, most).astype(kind)


def gaussian_with(own_key, shape, spread, most, cuts, heavy, dtype=jnp.bfloat16):
    array = spread * jax.random.normal(own_key, shape, jnp.float32)
    if cuts:
        array = array * levels(own_key, shape, cuts, -0.22, 0.18)
    return jnp.clip(with_spikes(array, jax.random.fold_in(own_key, 3), *heavy), -most, most).astype(dtype)


def setup_inputs(seed: int = 0) -> dict:
    streams_of = jax.random.split(jax.random.key(seed), 25)
    return {
        "act_short": centred(streams_of[0], (TOKENS_A, D), 1.0, 6.0, ((0, 32),)),
        "act_long": centred(streams_of[1], (TOKENS_B, D), 1.0, 6.0, ((0, 32),)),
        "cot_short": gaussian_with(streams_of[2], (TOKENS_A, D), 1.0, 6.0, ((0, 32),), (0, 1, 32, 2.75)),
        "cot_long": gaussian_with(streams_of[3], (TOKENS_B, D), 1.0, 6.0, ((0, 32),), (0, 1, 32, 2.75)),
        "len_short": draw_len_short(jax.random.fold_in(streams_of[24], 71), 0),
        "len_long": draw_len_long(jax.random.fold_in(streams_of[24], 71), 0),
        "attn_in": centred(streams_of[6], (3, D, D), D ** -0.5, 0.21875, ((1, 32),)),
        "conv_taps": centred(streams_of[7], (3, 3, D), 0.6, 3.0, ((2, 32),)),
        "w_out": centred(streams_of[8], (D, D), (D // 32) ** -0.5, 1.25, ((0, 32),)),
        "w_up": centred(streams_of[9], (D, FF), D ** -0.5, 0.21875, ((0, 32),)),
        "w_down": centred(streams_of[10], (FF, D), FF ** -0.5, 0.109375, ((0, 32),)),
        "gains": jnp.clip(1.0 + 0.1 * jax.random.normal(streams_of[11], (2, D), jnp.float32), 0.5, 1.5).astype(jnp.bfloat16),
        "mom_attn_in": centred(streams_of[12], (3, D, D), (0.55 * (TOKENS_A + TOKENS_B) ** 0.5), 512.0, ((1, 32),), jnp.float32),
        "mom_conv_taps": centred(streams_of[13], (3, 3, D), (0.55 * (TOKENS_A + TOKENS_B) ** 0.5), 512.0, ((2, 32),), jnp.float32),
        "mom_w_out": centred(streams_of[14], (D, D), (0.17 * (TOKENS_A + TOKENS_B) ** 0.5), 160.0, ((0, 32),), jnp.float32),
        "mom_w_up": centred(streams_of[15], (D, FF), (0.8 * (TOKENS_A + TOKENS_B) ** 0.5), 768.0, ((0, 32),), jnp.float32),
        "mom_w_down": centred(streams_of[16], (FF, D), (1.3 * (TOKENS_A + TOKENS_B) ** 0.5), 1280.0, ((0, 32),), jnp.float32),
        "mom_gains": centred(streams_of[17], (2, D), (1.1 * (TOKENS_A + TOKENS_B) ** 0.5), 1024.0, ((1, 32),), jnp.float32),
        "avg_attn_in": centred(streams_of[18], (3, D, D), D ** -0.5, 0.21875, ((1, 32),), jnp.float32),
        "avg_conv_taps": centred(streams_of[19], (3, 3, D), 0.6, 3.0, ((2, 32),), jnp.float32),
        "avg_w_out": centred(streams_of[20], (D, D), (D // 32) ** -0.5, 1.25, ((0, 32),), jnp.float32),
        "avg_w_up": centred(streams_of[21], (D, FF), D ** -0.5, 0.21875, ((0, 32),), jnp.float32),
        "avg_w_down": centred(streams_of[22], (FF, D), FF ** -0.5, 0.109375, ((0, 32),), jnp.float32),
        "avg_gains": jnp.clip(1.0 + 0.1 * jax.random.normal(streams_of[23], (2, D), jnp.float32), 0.5, 1.5),
    }


EPS = 1e-06
MOMENTUM = 0.9
AVERAGE = 0.5
RATES = (0.03, 0.5, 0.6, 0.025, 0.007, 0.05)
NEG = -1e+30
HEAD_SCALE = 0.125
HIGH = lax.Precision.HIGHEST

@jax.custom_vjp
def low(v):
    return lax.optimization_barrier(v.astype(jnp.bfloat16)).astype(jnp.float32)

@jax.custom_vjp
def low_back(v):
    return v

def low_keep(v):
    return (low(v), None)

def low_pass(kept, grad):
    return (grad,)

def back_keep(v):
    return (v, None)

def back_low(kept, grad):
    return (low(grad),)
low.defvjp(low_keep, low_pass)
low_back.defvjp(back_keep, back_low)

def rms_scale(values):
    return lax.rsqrt(lax.optimization_barrier(jnp.mean(values * values, axis=-1, keepdims=True)) + EPS)

def delayed(values, offset):
    return jnp.concatenate([jnp.zeros_like(values[:, :offset, :]), values[:, :-offset, :]], axis=1)

def conv_apply(taps, projected):
    return taps[:, 0, None, :] * projected + taps[:, 1, None, :] * delayed(projected, 1) + taps[:, 2, None, :] * delayed(projected, 2)

def attend_head(group):
    queries, key_rows, value_rows = group
    length = queries.shape[0]
    scores = jnp.dot(queries, key_rows.T, precision=HIGH) * HEAD_SCALE
    scores = low_back(scores)
    causal = jnp.arange(length)[:, None] >= jnp.arange(length)[None, :]
    scores = jnp.where(causal, scores, NEG)
    weights = jax.nn.softmax(scores, axis=-1)
    return jnp.dot(low(weights), value_rows, precision=HIGH)

def layer(params, stream):
    attn_in, conv_taps, w_out, w_up, w_down, gains = params
    length = stream.shape[0]
    normed = low(stream * rms_scale(stream) * gains[0])
    projected = low_back(jnp.einsum('td,kde->kte', normed, attn_in, precision=HIGH))
    mixed = low(conv_apply(conv_taps, projected))
    split = mixed.reshape(3, length, HEADS, HEAD_DIM).transpose(0, 2, 1, 3)
    per_head = lax.map(jax.checkpoint(attend_head), (split[0], split[1], split[2]))
    attended = per_head.transpose(1, 0, 2).reshape(length, D)
    attended = low_back(low(attended))
    branch = low_back(jnp.dot(attended, w_out, precision=HIGH))
    middle = stream + branch
    normed_two = low(middle * rms_scale(middle) * gains[1])
    hidden = low_back(jnp.dot(normed_two, w_up, precision=HIGH))
    squared = low(jnp.square(jax.nn.relu(hidden)))
    result = low_back(jnp.dot(squared, w_down, precision=HIGH))
    return middle + result

def run_group(params, acts, cots, lengths, length):
    count_rows = lengths.shape[0]
    acts = acts.reshape(count_rows, length, D).astype(jnp.float32)
    cots = cots.reshape(count_rows, length, D).astype(jnp.float32)
    positions = jnp.arange(length)

    def one_sequence(totals, item):
        stream, upstream, limit = item
        upstream = jnp.where((positions < limit)[:, None], upstream, jnp.zeros_like(upstream))
        output, pullback = jax.vjp(layer, params, stream)
        grad_params, grad_stream = pullback(upstream)
        totals = jax.tree.map(jnp.add, totals, grad_params)
        return (totals, (output.astype(jnp.bfloat16), grad_stream))
    zeros = jax.tree.map(jnp.zeros_like, params)
    totals, (outputs, backs) = lax.scan(one_sequence, zeros, (acts, cots, lengths))
    return (outputs.reshape(count_rows * length, D), backs.reshape(count_rows * length, D), totals)

def update(weight, grad, moment, average, rate):
    moment_new = MOMENTUM * moment + grad
    weight_new = weight.astype(jnp.float32) - rate * (grad + MOMENTUM * moment_new)
    average_new = AVERAGE * average + (1.0 - AVERAGE) * weight_new
    return (grad, moment_new, weight_new, average_new)

def reference(act_short, act_long, cot_short, cot_long, len_short, len_long, attn_in, conv_taps, w_out, w_up, w_down, gains, mom_attn_in, mom_conv_taps, mom_w_out, mom_w_up, mom_w_down, mom_gains, avg_attn_in, avg_conv_taps, avg_w_out, avg_w_up, avg_w_down, avg_gains):
    owned = (attn_in, conv_taps, w_out, w_up, w_down, gains)
    params = tuple((weight.astype(jnp.float32) for weight in owned))
    out_short, back_short, grads_short = run_group(params, act_short, cot_short, len_short, LEN_A)
    out_long, back_long, grads_long = run_group(params, act_long, cot_long, len_long, LEN_B)
    totals = jax.tree.map(jnp.add, grads_short, grads_long)
    moments = (mom_attn_in, mom_conv_taps, mom_w_out, mom_w_up, mom_w_down, mom_gains)
    averages = (avg_attn_in, avg_conv_taps, avg_w_out, avg_w_up, avg_w_down, avg_gains)
    scale_tokens = math.sqrt(TOKENS_A + TOKENS_B)
    results = [out_short, out_long, back_short, back_long]
    for position in range(6):
        results.extend(update(owned[position], totals[position], moments[position], averages[position], RATES[position] / scale_tokens))
    return tuple(results)
```

```python
import functools
import math

import jax
import jax.numpy as jnp
from jax import lax
from jax.experimental import pallas as pl
from jax.experimental.pallas import tpu as pltpu
from jax.sharding import PartitionSpec as P

D = 768
HEAD_DIM = 64
GROUP = 256
GROUPS = D // GROUP
BLOCK = 256
LANES = 128

EPS = 1e-06
MOMENTUM = 0.9
AVERAGE = 0.5
RATES = (0.03, 0.5, 0.6, 0.025, 0.007, 0.05)
NEG = -1e30
HEAD_SCALE = 0.125
AXES = ("dp", "fsdp")
BF = jnp.bfloat16
F32 = jnp.float32
MIB = 1024 * 1024
PEAK_PER_US = 1.15e9
WEIGHT = 3.0


class Grid:
    def __init__(self, mesh):
        self.a = mesh.shape["dp"]
        self.f = mesh.shape["fsdp"]
        self.x = 2
        self.z = self.f // 4

    def index(self, a, z, x, c):
        return a * self.f + (z * self.x + x) * 2 + c

    def perm(self, move):
        pairs = []
        for a in range(self.a):
            for z in range(self.z):
                for x in range(self.x):
                    for c in range(2):
                        pairs.append((self.index(a, z, x, c), self.index(*move(a, z, x, c))))
        return pairs

    def swap_core(self):
        return self.perm(lambda a, z, x, c: (a, z, x, 1 - c))

    def shift_plane(self, da, dx):
        return self.perm(lambda a, z, x, c: ((a + da) % self.a, z, (x + dx) % self.x, c))

    def shift_z(self, dz):
        return self.perm(lambda a, z, x, c: (a, (z + dz) % self.z, x, c))

    def here(self):
        f = lax.axis_index("fsdp")
        return lax.axis_index("dp"), f // 4, (f // 2) % 2, f % 2

    def plane_moves(self):
        return [(da, dx) for da in range(self.a) for dx in range(self.x) if da or dx]


def after(value, *others):
    return lax.optimization_barrier((value,) + others)[0]


def place_kernel(grid, dims, spots, *refs):
    count = len(spots)
    out, sems = refs[count], refs[count + 1]
    here = grid.here()
    copies = []
    for piece, spot in enumerate(spots):
        at = spot(*here)
        where = tuple(slice(None) if dim is None else at[dim] for dim in dims)
        copies.append(pltpu.make_async_copy(refs[piece], out.at[where], sems.at[piece]))
    for copy in copies:
        copy.start()
    for copy in copies:
        copy.wait()


def place(grid, pieces, spots, dims, out_shape):
    return pl.pallas_call(
        functools.partial(place_kernel, grid, dims, spots),
        out_shape=jax.ShapeDtypeStruct(tuple(out_shape), pieces[0].dtype),
        in_specs=[pl.BlockSpec(memory_space=pl.ANY)] * len(pieces),
        out_specs=pl.BlockSpec(memory_space=pl.ANY),
        scratch_shapes=[pltpu.SemaphoreType.DMA((len(pieces),))],
        cost_estimate=cost(1.0),
        compiler_params=pltpu.CompilerParams(vmem_limit_bytes=2 * MIB),
        name="place",
    )(*pieces)


def z_moves(grid):
    return [
        (
            grid.shift_z(dz),
            lambda a, z, x, c, dz=dz: ((z + dz) % grid.z,),
            lambda a, z, x, c, dz=dz: ((z - dz) % grid.z,),
        )
        for dz in range(1, grid.z)
    ]


def a_moves(grid):
    return [
        (
            grid.shift_plane(da, 0),
            lambda a, z, x, c, da=da: ((a + da) % grid.a,),
            lambda a, z, x, c, da=da: ((a - da) % grid.a,),
        )
        for da in range(1, grid.a)
    ]


def x_moves(grid):
    return [
        (
            grid.shift_plane(0, 1),
            lambda a, z, x, c: (1 - x,),
            lambda a, z, x, c: (1 - x,),
        )
    ]


def both_moves(grid):
    return [
        (
            grid.shift_plane(da, dx),
            lambda a, z, x, c, da=da, dx=dx: ((a + da) % grid.a, (x + dx) % grid.x),
            lambda a, z, x, c, da=da, dx=dx: ((a - da) % grid.a, (x - dx) % grid.x),
        )
        for da, dx in grid.plane_moves()
    ]


OWN_Z = lambda a, z, x, c: (z,)
OWN_A = lambda a, z, x, c: (a,)
OWN_X = lambda a, z, x, c: (x,)
OWN_AX = lambda a, z, x, c: (a, x)


def exchange(value, moves):
    return [lax.ppermute(value, AXES, pairs) for pairs, _, _ in moves]


def arrived(moves):
    return [brought for _, _, brought in moves]


def gather_z(grid, chunk):
    moves = z_moves(grid)
    pieces = [chunk] + exchange(chunk, moves)
    return place(grid, pieces, [OWN_Z] + arrived(moves), (0,), (grid.z,) + chunk.shape)


def swap(grid, value):
    return lax.ppermute(value, AXES, grid.swap_core())


def join(grid, plane, other):
    r, n = plane.shape[-2:]
    plane, other = plane.reshape(-1, r, n), other.reshape(-1, r, n)
    spots = [lambda a, z, x, c: (c,), lambda a, z, x, c: (1 - c,)]
    whole_shape = (plane.shape[0], 2, r, n)
    return place(grid, [plane, other], spots, (None, 0), whole_shape).reshape(-1, n)


def combine_kernel(axes, grid, spots, count, *refs):
    pieces, outs = refs[:count], refs[count:]
    here = grid.here()
    lead = pieces[0].ndim - 2
    free = [axis for axis in range(lead) if axis not in axes]
    for spot, out in zip(spots, outs):
        at = spot(*here)

        def add_up(rest):
            where = [0] * lead
            for axis, value in zip(axes, at):
                where[axis] = value
            for axis, value in zip(free, rest):
                where[axis] = value
            where = tuple(where)
            total = pieces[0][where].astype(F32)
            for piece in pieces[1:]:
                total = total + piece[where].astype(F32)
            return total

        rests = [()]
        for axis in free:
            rests = [rest + (i,) for rest in rests for i in range(pieces[0].shape[axis])]
        for rest in rests:
            out[rest if rest else ...] = add_up(rest).astype(out.dtype)


def combine(grid, pieces, axes, spots, steps=None, types=None):
    shape = pieces[0].shape
    lead = len(shape) - 2
    types = types or [BF] * len(spots)
    out_shape = tuple(shape[i] for i in range(lead) if i not in axes) + shape[-2:]
    if steps is None:
        spec = pl.BlockSpec(shape, lambda i: (0,) * len(shape))
        out_spec = pl.BlockSpec(out_shape, lambda i: (0,) * len(out_shape))
        count = 1
    else:
        count = shape[steps]
        block = tuple(1 if i == steps else shape[i] for i in range(len(shape)))
        spec = pl.BlockSpec(block, lambda i: tuple(i if j == steps else 0 for j in range(len(shape))))
        out_at = steps - sum(1 for axis in axes if axis < steps)
        out_block = tuple(1 if i == out_at else v for i, v in enumerate(out_shape))
        out_spec = pl.BlockSpec(
            out_block, lambda i: tuple(i if j == out_at else 0 for j in range(len(out_shape)))
        )
    return pl.pallas_call(
        functools.partial(combine_kernel, axes, grid, spots, len(pieces)),
        grid=(count,),
        in_specs=[spec] * len(pieces),
        out_specs=[out_spec] * len(spots),
        out_shape=[jax.ShapeDtypeStruct(out_shape, kind) for kind in types],
        cost_estimate=cost(2.0),
        compiler_params=params(8),
        name="combine",
    )(*pieces)


def send(parts, moves):
    return [parts[0]] + [
        lax.ppermute(part, AXES, pairs) for part, (pairs, _, _) in zip(parts[1:], moves)
    ]


def leaving(moves):
    return [sent for _, sent, _ in moves]


def core_step(grid, kept, sent):
    return [kept, swap(grid, sent)]


def x_step(grid, pieces, x_axis, z_axis):
    moves = x_moves(grid)
    return send(combine(grid, pieces, (x_axis,), [OWN_X] + leaving(moves), z_axis), moves)


def a_step(grid, pieces, z_axis):
    moves = a_moves(grid)
    return send(combine(grid, pieces, (0,), [OWN_A] + leaving(moves), z_axis), moves)


def both_step(grid, pieces):
    moves = both_moves(grid)
    return send(combine(grid, pieces, (0, 2), [OWN_AX] + leaving(moves), 1), moves)


def z_step(grid, pieces):
    moves = z_moves(grid)
    types = [F32] + [BF] * len(moves)
    return send(combine(grid, pieces, (0,), [OWN_Z] + leaving(moves), None, types), moves)


def dot(left, right):
    return lax.dot_general(left, right, (((1,), (0,)), ((), ())), preferred_element_type=F32)


def dot_bt(left, right):
    return lax.dot_general(left, right, (((1,), (1,)), ((), ())), preferred_element_type=F32)


def dot_at(left, right):
    return lax.dot_general(left, right, (((0,), (0,)), ((), ())), preferred_element_type=F32)


def rms_scale(values):
    return lax.rsqrt(jnp.mean(values * values, axis=-1, keepdims=True) + EPS)


def norm_back(values, gain, grad):
    scale = rms_scale(values)
    scaled = grad * gain
    inner = jnp.mean(scaled * values, axis=-1, keepdims=True)
    grad_gain = jnp.sum(grad * (values * scale), axis=0, keepdims=True)
    return scale * scaled - values * (scale * scale * scale * inner), grad_gain


def positions_of(rows, short, width):
    row = lax.broadcasted_iota(jnp.int32, (rows, width), 0)
    return jnp.where(row < short, row, row - short), row < short


def shift_down(values, offset, position):
    return jnp.where(position >= offset, pltpu.roll(values, offset, 0), 0.0)


def shift_up(values, offset, room):
    rows = values.shape[0]
    return jnp.where(room >= offset, pltpu.roll(values, rows - offset, 0), 0.0)


def head_mask(half):
    lane = lax.broadcasted_iota(jnp.int32, (1, LANES), 1)
    return (lane // HEAD_DIM) == half


def blocks_of(rows, short):
    found = []
    for start, length in ((0, short), (short, rows - short)):
        for block in range(length // BLOCK):
            found.append((start + block * BLOCK, start, (block + 1) * BLOCK))
    return found


def store_split(value, owner_rows, kept, sent, lanes=slice(None)):
    core = lax.axis_index("fsdp") % 2
    for mine, first, second in ((0, kept, sent), (1, sent, kept)):

        @pl.when(core == mine)
        def _():
            for pair in range(value.shape[0] // (2 * owner_rows)):
                at = 2 * pair * owner_rows
                first[pair, :, lanes] = value[at : at + owner_rows].astype(BF)
                second[pair, :, lanes] = value[at + owner_rows : at + 2 * owner_rows].astype(BF)


def front_kernel(
    short, xs, xl, wq, wk, wv, wsmall, normed, projected, mixed, attended, small, small_scr
):
    step = pl.program_id(0)
    rows = normed.shape[0]

    @pl.when(step == 0)
    def _():
        turned = jnp.transpose(wsmall[...].astype(F32))[:16]
        small[...] = turned
        for g in range(GROUPS):
            small_scr[g] = turned[:, g * GROUP : (g + 1) * GROUP]
        gain = turned[9:10]
        for ref, first, count in ((xs, 0, short), (xl, short, rows - short)):
            x = ref[...].astype(F32)
            normed[first : first + count] = (x * rms_scale(x) * gain).astype(BF)

    taps = small_scr[step]
    position, _ = positions_of(rows, short, GROUP)
    base = normed[...]
    for k, w in enumerate((wq, wk, wv)):
        p = dot(base, w[...])
        projected[k] = p
        mixed[k] = (
            taps[3 * k : 3 * k + 1] * p
            + taps[3 * k + 1 : 3 * k + 2] * shift_down(p, 1, position)
            + taps[3 * k + 2 : 3 * k + 3] * shift_down(p, 2, position)
        ).astype(BF)
    for pair in range(GROUP // LANES):
        lanes = slice(pair * LANES, (pair + 1) * LANES)
        for first, key_first, key_count in blocks_of(rows, short):
            queries = mixed[0, first : first + BLOCK, lanes]
            keys = mixed[1, key_first : key_first + key_count, lanes]
            values = mixed[2, key_first : key_first + key_count, lanes]
            row = lax.broadcasted_iota(jnp.int32, (BLOCK, key_count), 0) + (first - key_first)
            causal = lax.broadcasted_iota(jnp.int32, (BLOCK, key_count), 1) <= row
            total = None
            for half in range(2):
                scale = jnp.where(head_mask(half), HEAD_SCALE, 0.0).astype(BF)
                keep = jnp.where(head_mask(half), 1.0, 0.0).astype(BF)
                scores = jnp.where(causal, dot_bt(queries * scale, keys), NEG)
                peak = jnp.max(scores, axis=-1, keepdims=True)
                exponent = jnp.exp(scores - peak)
                weights = exponent * (1.0 / jnp.sum(exponent, axis=-1, keepdims=True))
                part = dot(weights.astype(BF), values * keep)
                total = part if total is None else total + part
            attended[first : first + BLOCK, lanes] = total.astype(BF)


def up_kernel(
    short, owner_rows, ls, ll, xs, xl, cs, cl, attended, wout, wup, small,
    middle, normed, upstream, active, kept, sent,
):
    step = pl.program_id(0)
    rows = normed.shape[0]

    @pl.when(step == 0)
    def _():
        gain = small[10:11]
        branch = dot(attended[...], wout[...])
        for ref, cot, limit, first, count in (
            (xs, cs, ls, 0, short),
            (xl, cl, ll, short, rows - short),
        ):
            part = slice(first, first + count)
            mid = ref[...].astype(F32) + branch[part]
            middle[part] = mid
            normed[part] = (mid * rms_scale(mid) * gain).astype(BF)
            position = lax.broadcasted_iota(jnp.int32, (count, D), 0)
            wide = jnp.where(position < limit[0], cot[...].astype(F32), 0.0)
            upstream[part] = wide.astype(BF)

    hidden = jnp.maximum(dot(normed[...], wup[...]), 0.0)
    active[...] = hidden
    squared = (hidden * hidden).astype(BF)
    store_split(dot_at(squared, upstream[...]), owner_rows, kept, sent)


def down_kernel(
    last, owner_rows, upstream, wdown, active, wup, normed, attended, middle, small,
    kept, sent, grad_middle, grad_branch, grad_gain, total,
):
    step = pl.program_id(0)

    @pl.when(step < last)
    def _():
        grad_squared = dot_bt(upstream[...], wdown[...])
        grad_hidden = (grad_squared * (2.0 * active[...])).astype(BF)
        store_split(dot_at(normed[...], grad_hidden), owner_rows, kept, sent)
        part = dot_bt(grad_hidden, wup[...])

        @pl.when(step == 0)
        def _():
            total[...] = part

        @pl.when(step > 0)
        def _():
            total[...] += part

    @pl.when(step == last)
    def _():
        pulled, gain = norm_back(middle[...], small[10:11], total[...])
        grad_gain[...] = jnp.broadcast_to(gain, grad_gain.shape)
        wide = upstream[...].astype(F32) + pulled
        grad_middle[...] = wide
        low = wide.astype(BF)
        grad_branch[...] = low
        store_split(dot_at(attended[...], low), owner_rows, kept, sent)


def mixer_kernel(
    short, mixed, projected, branch, wout, small, *refs
):
    grad_projected, grad_taps, scratch = refs[-3:]
    rows = branch.shape[0]
    grad_attended = dot_bt(branch[...], wout[...]).astype(BF)
    for pair in range(GROUP // LANES):
        lanes = slice(pair * LANES, (pair + 1) * LANES)
        started = set()
        for first, key_first, key_count in blocks_of(rows, short):
            block = slice(first, first + BLOCK)
            spread = slice(key_first, key_first + key_count)
            queries = mixed[0, block, lanes]
            keys = mixed[1, spread, lanes]
            values = mixed[2, spread, lanes]
            grads = grad_attended[block, lanes]
            row = lax.broadcasted_iota(jnp.int32, (key_count, BLOCK), 1) + (first - key_first)
            causal = lax.broadcasted_iota(jnp.int32, (key_count, BLOCK), 0) <= row
            for_queries = for_keys = for_values = None
            for half in range(2):
                scale = jnp.where(head_mask(half), HEAD_SCALE, 0.0).astype(BF)
                keep = jnp.where(head_mask(half), 1.0, 0.0).astype(BF)
                scaled = queries * scale
                kept = grads * keep
                scores = jnp.where(causal, dot_bt(keys, scaled), NEG)
                peak = jnp.max(scores, axis=0, keepdims=True)
                exponent = jnp.exp(scores - peak)
                probs = exponent * (1.0 / jnp.sum(exponent, axis=0, keepdims=True))
                grad_probs = dot_bt(values, kept)
                inner = jnp.sum(probs * grad_probs, axis=0, keepdims=True)
                grad_scores = (probs * (grad_probs - inner)).astype(BF)
                to_values = dot(probs.astype(BF), kept)
                to_keys = dot(grad_scores, scaled)
                to_queries = dot_at(grad_scores, keys * scale)
                if half == 0:
                    for_queries, for_keys, for_values = to_queries, to_keys, to_values
                else:
                    for_queries = for_queries + to_queries
                    for_keys = for_keys + to_keys
                    for_values = for_values + to_values
            scratch[0, block, lanes] = for_queries
            for block_key in range(key_count // BLOCK):
                at = key_first + block_key * BLOCK
                inside = slice(block_key * BLOCK, (block_key + 1) * BLOCK)
                if at in started:
                    scratch[1, at : at + BLOCK, lanes] += for_keys[inside]
                    scratch[2, at : at + BLOCK, lanes] += for_values[inside]
                else:
                    started.add(at)
                    scratch[1, at : at + BLOCK, lanes] = for_keys[inside]
                    scratch[2, at : at + BLOCK, lanes] = for_values[inside]
    position, in_short = positions_of(rows, short, GROUP)
    room = jnp.where(in_short, short, rows - short) - 1 - position
    taps = small[...]
    for k in range(3):
        g = scratch[k]
        p = projected[k]
        grad_projected[k] = (
            taps[3 * k : 3 * k + 1] * g
            + taps[3 * k + 1 : 3 * k + 2] * shift_up(g, 1, room)
            + taps[3 * k + 2 : 3 * k + 3] * shift_up(g, 2, room)
        ).astype(BF)
        grad_taps[3 * k : 3 * k + 1] = jnp.sum(g * p, axis=0, keepdims=True)
        for j in (1, 2):
            grad_taps[3 * k + j : 3 * k + j + 1] = jnp.sum(
                g * shift_down(p, j, position), axis=0, keepdims=True
            )
    grad_taps[9:16] = jnp.zeros((7, GROUP), F32)


def back_kernel(
    short, owner_rows, xs, xl, grad_projected, w, normed, grad_middle, small, grad_taps,
    grad_gain_two, kept, sent, back_short, back_long, total,
):
    step = pl.program_id(0)
    g = grad_projected[0]
    lanes = pl.ds(pl.multiple_of(step * D, D), D)
    store_split(dot_at(normed[...], g), owner_rows, kept, sent, lanes)
    part = dot_bt(g, w[...])

    @pl.when(step == 0)
    def _():
        total[...] = part

    @pl.when(step > 0)
    def _():
        total[...] += part

    @pl.when(step == 2)
    def _():
        rows = normed.shape[0]
        gain_sum = None
        for ref, out, first, count in (
            (xs, back_short, 0, short),
            (xl, back_long, short, rows - short),
        ):
            rows_of = slice(first, first + count)
            pulled, gain = norm_back(ref[...].astype(F32), small[9:10], total[rows_of])
            out[...] = grad_middle[rows_of] + pulled
            gain_sum = gain if gain_sum is None else gain_sum + gain
        row = lax.broadcasted_iota(jnp.int32, (16, D), 0)
        packed = jnp.where(row == 9, gain_sum, grad_taps[...])
        packed = jnp.where(row == 10, grad_gain_two[0:1], packed)
        packed = jnp.concatenate([packed, jnp.zeros((LANES - 16, D), F32)], axis=0)
        store_split(
            jnp.transpose(packed), owner_rows, kept, sent, slice(3 * D, 3 * D + LANES)
        )


def output_kernel(short, active, wdown, middle, out_short, out_long, total):
    step = pl.program_id(0)
    hidden = active[...]
    part = dot((hidden * hidden).astype(BF), wdown[...])

    @pl.when(step == 0)
    def _():
        total[...] = middle[...] + part

    @pl.when(step > 0)
    def _():
        total[...] += part

    @pl.when(step == pl.num_programs(0) - 1)
    def _():
        out_short[...] = total[:short].astype(BF)
        out_long[...] = total[short:].astype(BF)


def whole(shape):
    zeros = (0,) * len(shape)
    return pl.BlockSpec(shape, lambda i: zeros)


def smem():
    return pl.BlockSpec(memory_space=pltpu.SMEM)


def struct(shape, dtype):
    return jax.ShapeDtypeStruct(shape, dtype)


def params(mib):
    return pltpu.CompilerParams(
        vmem_limit_bytes=mib * MIB, dimension_semantics=("arbitrary",)
    )


def cost(us):
    return pl.CostEstimate(
        flops=int(us * PEAK_PER_US * WEIGHT), bytes_accessed=0, transcendentals=0
    )


def update(grad, rate, weight, moment, average, outs, at=Ellipsis):
    moment_new = MOMENTUM * moment[at] + grad
    weight_new = weight[at].astype(F32) - rate * (grad + MOMENTUM * moment_new)
    outs[0][at] = grad
    outs[1][at] = moment_new
    outs[2][at] = weight_new
    outs[3][at] = AVERAGE * average[at] + (1.0 - AVERAGE) * weight_new


def finish_kernel(kind, count, rates, *refs):
    pieces, rest = refs[:count], refs[count:]
    total = pieces[0][...]
    for piece in pieces[1:]:
        total = total + piece[...].astype(F32)
    sets = len(rates)
    held = [rest[3 * i : 3 * i + 3] for i in range(sets)]
    outs = [rest[3 * sets + 4 * i : 3 * sets + 4 * i + 4] for i in range(sets)]
    if kind == "down":
        update(total, rates[0], *held[0], outs[0])
    elif kind == "up":
        update(total[:, :D], rates[0], *held[0], outs[0])
        update(total[:, D:], rates[1], *held[1], outs[1])
    else:
        for k in range(3):
            update(total[:, k * D : (k + 1) * D], rates[0], *held[0], outs[0], k)
        r = total.shape[0]
        rest_rows = jnp.zeros((LANES - r, LANES), F32)
        turned = jnp.transpose(jnp.concatenate([total[:, 3 * D :], rest_rows], axis=0))
        for k in range(3):
            update(turned[3 * k : 3 * k + 3, :r], rates[1], *held[1], outs[1], k)
        update(turned[9:11, :r], rates[2], *held[2], outs[2])


def finish(kind, pieces, sets, rates):
    flat = [array for one in sets for array in one]
    shapes = [one[0].shape for one in sets for _ in range(4)]
    outs = pl.pallas_call(
        functools.partial(finish_kernel, kind, len(pieces), rates),
        grid=(1,),
        in_specs=[whole(array.shape) for array in list(pieces) + flat],
        out_specs=[whole(shape) for shape in shapes],
        out_shape=[struct(shape, F32) for shape in shapes],
        cost_estimate=cost(1.5),
        compiler_params=params(8),
        name="finish",
    )(*pieces, *flat)
    return [outs[4 * i : 4 * i + 4] for i in range(len(sets))]


def front(act_short, act_long, w_attn):
    short, rows = act_short.shape[0], act_short.shape[0] + act_long.shape[0]
    return pl.pallas_call(
        functools.partial(front_kernel, short),
        grid=(GROUPS,),
        in_specs=[
            whole(act_short.shape),
            whole(act_long.shape),
            pl.BlockSpec((D, GROUP), lambda i: (0, i)),
            pl.BlockSpec((D, GROUP), lambda i: (0, GROUPS + i)),
            pl.BlockSpec((D, GROUP), lambda i: (0, 2 * GROUPS + i)),
            pl.BlockSpec((D, LANES), lambda i: (0, 3 * D // LANES)),
        ],
        out_specs=[
            whole((rows, D)),
            pl.BlockSpec((3, rows, GROUP), lambda i: (0, 0, i)),
            pl.BlockSpec((3, rows, GROUP), lambda i: (0, 0, i)),
            pl.BlockSpec((rows, GROUP), lambda i: (0, i)),
            whole((16, D)),
        ],
        out_shape=[
            struct((rows, D), BF),
            struct((3, rows, D), F32),
            struct((3, rows, D), BF),
            struct((rows, D), BF),
            struct((16, D), F32),
        ],
        scratch_shapes=[pltpu.VMEM((GROUPS, 16, GROUP), F32)],
        cost_estimate=cost(16),
        compiler_params=params(20),
        name="front",
    )(act_short, act_long, w_attn, w_attn, w_attn, w_attn)


def up(act_short, act_long, cot_short, cot_long, len_short, len_long, attended, w_up, small, s):
    short, rows = act_short.shape[0], act_short.shape[0] + act_long.shape[0]
    ff = w_up.shape[1] - D
    tiles = ff // D
    half = D // (2 * s)
    halves = struct((tiles * half, s, D), BF)
    return pl.pallas_call(
        functools.partial(up_kernel, short, s),
        grid=(tiles,),
        in_specs=[
            smem(),
            smem(),
            whole(act_short.shape),
            whole(act_long.shape),
            whole(cot_short.shape),
            whole(cot_long.shape),
            whole((rows, D)),
            pl.BlockSpec((D, D), lambda i: (0, 0)),
            pl.BlockSpec((D, D), lambda i: (0, 1 + i)),
            whole((16, D)),
        ],
        out_specs=[
            whole((rows, D)),
            whole((rows, D)),
            whole((rows, D)),
            pl.BlockSpec((rows, D), lambda i: (0, i)),
            pl.BlockSpec((half, s, D), lambda i: (i, 0, 0)),
            pl.BlockSpec((half, s, D), lambda i: (i, 0, 0)),
        ],
        out_shape=[
            struct((rows, D), F32),
            struct((rows, D), BF),
            struct((rows, D), BF),
            struct((rows, ff), F32),
            halves,
            halves,
        ],
        cost_estimate=cost(16),
        compiler_params=params(28),
        name="up",
    )(
        len_short, len_long, act_short, act_long, cot_short, cot_long, attended, w_up, w_up, small
    )


def down(upstream, w_down, active, w_up, normed_two, attended, middle, small, r):
    rows = upstream.shape[0]
    ff = w_down.shape[0]
    tiles = ff // D
    half = D // (2 * r)

    def last_tile(i):
        return jnp.minimum(i, tiles - 1)

    def put(i):
        return (0, 0, jnp.where(i < tiles, i + 1, 0))

    return pl.pallas_call(
        functools.partial(down_kernel, tiles, r),
        grid=(tiles + 1,),
        in_specs=[
            whole((rows, D)),
            pl.BlockSpec((D, D), lambda i: (last_tile(i), 0)),
            pl.BlockSpec((rows, D), lambda i: (0, last_tile(i))),
            pl.BlockSpec((D, D), lambda i: (0, 1 + last_tile(i))),
            whole((rows, D)),
            whole((rows, D)),
            whole((rows, D)),
            whole((16, D)),
        ],
        out_specs=[
            pl.BlockSpec((half, r, D), put),
            pl.BlockSpec((half, r, D), put),
            whole((rows, D)),
            whole((rows, D)),
            whole((8, D)),
        ],
        out_shape=[
            struct((half, r, D + ff), BF),
            struct((half, r, D + ff), BF),
            struct((rows, D), F32),
            struct((rows, D), BF),
            struct((8, D), F32),
        ],
        scratch_shapes=[pltpu.VMEM((rows, D), F32)],
        cost_estimate=cost(24),
        compiler_params=params(32),
        name="down",
    )(upstream, w_down, active, w_up, normed_two, attended, middle, small)


def mixer(short, first, count, mixed, projected, grad_branch, w_up, small, before=()):
    rows = grad_branch.shape[0]
    return pl.pallas_call(
        functools.partial(mixer_kernel, short),
        grid=(count,),
        in_specs=[
            pl.BlockSpec((3, rows, GROUP), lambda i: (0, 0, first + i)),
            pl.BlockSpec((3, rows, GROUP), lambda i: (0, 0, first + i)),
            whole((rows, D)),
            pl.BlockSpec((GROUP, D), lambda i: (first + i, 0)),
            pl.BlockSpec((16, GROUP), lambda i: (0, first + i)),
        ]
        + [pl.BlockSpec(memory_space=pl.ANY)] * len(before),
        out_specs=[
            pl.BlockSpec((3, rows, GROUP), lambda i: (0, 0, first + i)),
            pl.BlockSpec((16, GROUP), lambda i: (0, first + i)),
        ],
        out_shape=[struct((3, rows, D), BF), struct((16, D), F32)],
        input_output_aliases={5 + i: i for i in range(len(before))},
        scratch_shapes=[pltpu.VMEM((3, rows, GROUP), F32)],
        cost_estimate=cost(8 * count),
        compiler_params=params(24),
        name="mixer",
    )(mixed, projected, grad_branch, w_up, small, *before)


def back(
    act_short, act_long, grad_projected, w_attn, normed, grad_middle, small, grad_taps,
    grad_gain_two, r,
):
    short, rows = act_short.shape[0], normed.shape[0]
    wide = w_attn.shape[1]
    half = D // (2 * r)
    return pl.pallas_call(
        functools.partial(back_kernel, short, r),
        grid=(3,),
        in_specs=[
            whole(act_short.shape),
            whole(act_long.shape),
            pl.BlockSpec((1, rows, D), lambda i: (i, 0, 0)),
            pl.BlockSpec((D, D), lambda i: (0, i)),
            whole((rows, D)),
            whole((rows, D)),
            whole((16, D)),
            whole((16, D)),
            whole((8, D)),
        ],
        out_specs=[
            whole((half, r, wide)),
            whole((half, r, wide)),
            whole(act_short.shape),
            whole(act_long.shape),
        ],
        out_shape=[
            struct((half, r, wide), BF),
            struct((half, r, wide), BF),
            struct(act_short.shape, F32),
            struct(act_long.shape, F32),
        ],
        scratch_shapes=[pltpu.VMEM((rows, D), F32)],
        cost_estimate=cost(14),
        compiler_params=params(28),
        name="back",
    )(
        act_short, act_long, grad_projected, w_attn, normed, grad_middle, small, grad_taps,
        grad_gain_two,
    )


def output(act_short, act_long, active, w_down, middle):
    short, rows = act_short.shape[0], middle.shape[0]
    ff = w_down.shape[0]
    return pl.pallas_call(
        functools.partial(output_kernel, short),
        grid=(ff // D,),
        in_specs=[
            pl.BlockSpec((rows, D), lambda i: (0, i)),
            pl.BlockSpec((D, D), lambda i: (i, 0)),
            whole((rows, D)),
        ],
        out_specs=[whole(act_short.shape), whole(act_long.shape)],
        out_shape=[struct(act_short.shape, BF), struct(act_long.shape, BF)],
        scratch_shapes=[pltpu.VMEM((rows, D), F32)],
        cost_estimate=cost(9),
        compiler_params=params(20),
        name="output",
    )(active, w_down, middle)


def shards(grid, *args):
    act_short, act_long, cot_short, cot_long, len_short, len_long = args[:6]
    owned = args[6:12]
    moments = args[12:18]
    averages = args[18:24]
    attn_rows, conv_cols, out_rows, up_rows, down_rows, gain_cols = owned
    r = out_rows.shape[0]
    s = down_rows.shape[0]
    short = act_short.shape[0]
    rows = short + act_long.shape[0]

    small_rows = jnp.concatenate([conv_cols.reshape(9, r), gain_cols], axis=0).T
    small_rows = jnp.pad(small_rows, ((0, 0), (0, LANES - 11)))
    chunk_attn = jnp.concatenate([attn_rows[0], attn_rows[1], attn_rows[2], small_rows], axis=1)
    chunk_up = jnp.concatenate([out_rows, up_rows], axis=1)

    both, over_a, over_x = both_moves(grid), a_moves(grid), x_moves(grid)
    wide, wide_up = chunk_attn.shape[1], chunk_up.shape[1]
    col_attn = gather_z(grid, chunk_attn)
    col_up = gather_z(grid, after(chunk_up, col_attn))
    got_attn = exchange(col_attn, both)
    got_attn = [after(got, col_up) for got in got_attn]
    plane_attn = place(
        grid,
        [col_attn] + got_attn,
        [OWN_AX] + arrived(both),
        (0, None, 1),
        (grid.a, grid.z, grid.x, r, wide),
    )
    col_down = gather_z(grid, after(down_rows, col_up))
    other_attn = swap(grid, plane_attn)
    got_up = exchange(after(col_up, plane_attn), over_a)
    got_down = exchange(after(col_down, plane_attn), over_x)
    up_a = place(
        grid,
        [col_up] + got_up,
        [OWN_A] + arrived(over_a),
        (0,),
        (grid.a,) + col_up.shape,
    )
    down_x = place(
        grid,
        [col_down] + got_down,
        [OWN_X] + arrived(over_x),
        (None, 0),
        (grid.z, grid.x) + col_down.shape[1:],
    )
    w_attn = join(grid, plane_attn, other_attn)
    got_up = exchange(up_a, over_x)
    got_down = exchange(down_x, over_a)
    normed, projected, mixed, attended, small = front(
        act_short, act_long, after(w_attn, up_a, down_x)
    )
    got_up = [after(got, normed) for got in got_up]
    got_down = [after(got, normed) for got in got_down]
    plane_down = place(
        grid,
        [down_x] + got_down,
        [OWN_A] + arrived(over_a),
        (0,),
        (grid.a,) + down_x.shape,
    )
    plane_up = place(
        grid,
        [up_a] + [after(got, plane_down) for got in got_up],
        [OWN_X] + arrived(over_x),
        (None, None, 0),
        (grid.a, grid.z, grid.x, r, wide_up),
    )
    other_up = swap(grid, plane_up)
    other_down = swap(grid, plane_down)
    w_up = join(grid, plane_up, other_up)
    middle, normed_two, upstream, active, kept_down, sent_down = up(
        act_short, act_long, cot_short, cot_long, len_short, len_long, attended, w_up, small, s
    )
    w_down = join(grid, plane_down, after(other_down, normed_two))

    def spread(parts):
        return [part.reshape((grid.a, grid.z, grid.x) + part.shape[1:]) for part in parts]

    pieces_down = core_step(grid, kept_down, sent_down)
    kept_up, sent_up, grad_middle, grad_branch, grad_gain_two = down(
        upstream, w_down, active, w_up, normed_two, attended, middle, small, r
    )
    pieces_up = core_step(grid, kept_up, sent_up)
    pieces_down[1] = after(pieces_down[1], grad_branch)
    pieces_down = x_step(grid, spread(pieces_down), 2, 1)
    first = mixer(
        short, 0, 1, mixed, projected, after(grad_branch, pieces_down[0]), w_up, small
    )
    pieces_up[1] = after(pieces_up[1], first[1])
    pieces_up = a_step(grid, spread(pieces_up), 1)
    first = (after(first[0], pieces_up[0]), first[1])
    grad_projected, grad_taps = mixer(
        short, 1, GROUPS - 1, mixed, projected, grad_branch, w_up, small, before=first
    )
    pieces_down[1] = after(pieces_down[1], grad_taps)
    pieces_down = a_step(grid, pieces_down, 1)
    kept_attn, sent_attn, back_short, back_long = back(
        act_short, act_long, grad_projected, w_attn, normed,
        after(grad_middle, pieces_down[0]), small, grad_taps, grad_gain_two, r,
    )
    pieces_attn = core_step(grid, kept_attn, sent_attn)
    pieces_up[1] = after(pieces_up[1], back_short)
    pieces_up = x_step(grid, pieces_up, 1, 0)
    pieces_down[1] = after(pieces_down[1], pieces_up[0])
    pieces_down = z_step(grid, pieces_down)
    pieces_attn[1] = after(pieces_attn[1], pieces_up[0])
    pieces_attn = both_step(grid, spread(pieces_attn))
    out_short, out_long = output(
        act_short, act_long, active, w_down, after(middle, pieces_attn[0])
    )
    pieces_down[1:] = [after(piece, out_short) for piece in pieces_down[1:]]
    pieces_up[1] = after(pieces_up[1], out_short)

    scale_tokens = math.sqrt(rows * grid.a * grid.f)
    rates = [rate / scale_tokens for rate in RATES]
    sets = list(zip(owned, moments, averages))
    pieces_up = z_step(grid, pieces_up)
    (done_down,) = finish("down", pieces_down, [sets[4]], [rates[4]])
    pieces_attn = z_step(grid, pieces_attn)
    done_out, done_up = finish("up", pieces_up, sets[2:4], rates[2:4])
    done_attn, done_taps, done_gains = finish(
        "attn", pieces_attn, [sets[0], sets[1], sets[5]], [rates[0], rates[1], rates[5]]
    )
    results = [out_short, out_long, back_short, back_long]
    for done in (done_attn, done_taps, done_out, done_up, done_down, done_gains):
        results.extend(done)
    return tuple(results)


def solution(mesh):
    rows = P(AXES, None)
    weights = [P(None, AXES, None), P(None, None, AXES), rows, rows, rows, P(None, AXES)]
    in_specs = tuple([rows] * 4 + [P(AXES)] * 2 + weights * 3)
    out_specs = tuple([rows] * 4 + [spec for spec in weights for _ in range(4)])
    grid = Grid(mesh)

    def program(*args):
        return shards(grid, *args)

    return jax.shard_map(
        program, mesh=mesh, in_specs=in_specs, out_specs=out_specs, check_vma=False
    )
```

```python
import functools
import math

import jax
import jax.numpy as jnp
from jax import lax
from jax.experimental import pallas as pl
from jax.experimental.pallas import tpu as pltpu
from jax.sharding import PartitionSpec as P

D = 768
HEAD_DIM = 64
GROUP = 256
GROUPS = D // GROUP
BLOCK = 256
LANES = 128

EPS = 1e-06
MOMENTUM = 0.9
AVERAGE = 0.5
RATES = (0.03, 0.5, 0.6, 0.025, 0.007, 0.05)
NEG = -1e30
HEAD_SCALE = 0.125
AXES = ("dp", "fsdp")
BF = jnp.bfloat16
F32 = jnp.float32
MIB = 1024 * 1024
PEAK_PER_US = 1.15e9
WEIGHT = 1.0
HEAVY = 100


class Grid:
    def __init__(self, mesh):
        self.a = mesh.shape["dp"]
        self.f = mesh.shape["fsdp"]
        self.x = 2
        self.z = self.f // 4

    def index(self, a, z, x, c):
        return a * self.f + (z * self.x + x) * 2 + c

    def perm(self, move):
        pairs = []
        for a in range(self.a):
            for z in range(self.z):
                for x in range(self.x):
                    for c in range(2):
                        pairs.append((self.index(a, z, x, c), self.index(*move(a, z, x, c))))
        return pairs

    def swap_core(self):
        return self.perm(lambda a, z, x, c: (a, z, x, 1 - c))

    def shift_plane(self, da, dx):
        return self.perm(lambda a, z, x, c: ((a + da) % self.a, z, (x + dx) % self.x, c))

    def shift_z(self, dz):
        return self.perm(lambda a, z, x, c: (a, (z + dz) % self.z, x, c))

    def here(self):
        f = lax.axis_index("fsdp")
        return lax.axis_index("dp"), f // 4, (f // 2) % 2, f % 2

    def plane_moves(self):
        return [(da, dx) for da in range(self.a) for dx in range(self.x) if da or dx]


def after(value, *others):
    return lax.optimization_barrier((value,) + others)[0]


def relay_kernel(grid, body, count, *refs):
    body(grid.here(), refs[:count], refs[count:])


def along(shape, axis):
    if axis is None:
        return pl.BlockSpec(shape, lambda i: (0,) * len(shape))
    block = tuple(1 if j == axis else size for j, size in enumerate(shape))
    return pl.BlockSpec(block, lambda i: tuple(i if j == axis else 0 for j in range(len(shape))))


def relay(grid, name, body, steps, ins, outs):
    return pl.pallas_call(
        functools.partial(relay_kernel, grid, body, len(ins)),
        grid=(steps,),
        in_specs=[along(array.shape, axis) for array, axis in ins],
        out_specs=[along(shape, axis) for shape, _, axis in outs],
        out_shape=[jax.ShapeDtypeStruct(shape, kind) for shape, kind, _ in outs],
        cost_estimate=cost(1),
        compiler_params=params(8),
        name=name,
    )(*[array for array, _ in ins])


def z_moves(grid):
    return [
        (
            grid.shift_z(dz),
            lambda a, z, x, c, dz=dz: ((z + dz) % grid.z,),
            lambda a, z, x, c, dz=dz: ((z - dz) % grid.z,),
        )
        for dz in range(1, grid.z)
    ]


def a_moves(grid):
    return [
        (
            grid.shift_plane(da, 0),
            lambda a, z, x, c, da=da: ((a + da) % grid.a,),
            lambda a, z, x, c, da=da: ((a - da) % grid.a,),
        )
        for da in range(1, grid.a)
    ]


def x_moves(grid):
    return [
        (
            grid.shift_plane(0, 1),
            lambda a, z, x, c: (1 - x,),
            lambda a, z, x, c: (1 - x,),
        )
    ]


def both_moves(grid):
    return [
        (
            grid.shift_plane(da, dx),
            lambda a, z, x, c, da=da, dx=dx: ((a + da) % grid.a, (x + dx) % grid.x),
            lambda a, z, x, c, da=da, dx=dx: ((a - da) % grid.a, (x - dx) % grid.x),
        )
        for da, dx in grid.plane_moves()
    ]


OWN_Z = lambda a, z, x, c: (z,)
OWN_A = lambda a, z, x, c: (a,)
OWN_X = lambda a, z, x, c: (x,)
OWN_AX = lambda a, z, x, c: (a, x)


def exchange(value, moves):
    return [value] + [lax.ppermute(value, AXES, pairs) for pairs, _, _ in moves]


def send(parts, moves):
    return [parts[0]] + [
        lax.ppermute(part, AXES, pairs) for part, (pairs, _, _) in zip(parts[1:], moves)
    ]


def swap(grid, value):
    return lax.ppermute(value, AXES, grid.swap_core())


def arrived(own, moves):
    return [own] + [brought for _, _, brought in moves]


def leaving(own, moves):
    return [own] + [sent for _, sent, _ in moves]


def held_back(pieces, *others):
    return [pieces[0]] + [after(piece, *others) for piece in pieces[1:]]


def place_z(grid, pieces, cuts):
    spots = arrived(OWN_Z, z_moves(grid))
    r = pieces[0].shape[0]

    def body(here, ins, outs):
        for piece, spot in zip(ins, spots):
            at = spot(*here)[0]
            for out, (low, high) in zip(outs, cuts):
                out[at] = piece[:, low:high]

    outs = [((grid.z, r, high - low), BF, None) for low, high in cuts]
    return relay(grid, "place_z", body, 1, [(piece, None) for piece in pieces], outs)


def halves(grid, pieces, width):
    return place_z(grid, pieces, [(0, width // 2), (width // 2, width)])


def place_both(grid, pieces):
    spots = arrived(OWN_AX, both_moves(grid))

    def body(here, ins, outs):
        for piece, spot in zip(ins, spots):
            ia, ix = spot(*here)
            outs[0][ia, 0, ix] = piece[0]

    z, r, n = pieces[0].shape
    outs = [((grid.a, z, grid.x, r, n), BF, 1)]
    return relay(grid, "place_both", body, z, [(piece, 0) for piece in pieces], outs)[0]


def place_first(grid, over_a, over_x):
    a_spots = arrived(OWN_A, a_moves(grid))
    x_spots = arrived(OWN_X, x_moves(grid))

    def body(here, ins, outs):
        for piece, spot in zip(ins, a_spots):
            outs[0][spot(*here)[0], 0] = piece[0]
        for piece, spot in zip(ins[len(a_spots) :], x_spots):
            outs[1][0, spot(*here)[0]] = piece[0]

    z, r, n = over_a[0].shape
    m = over_x[0].shape[-1]
    ins = [(piece, 0) for piece in over_a + over_x]
    outs = [((grid.a, z, r, n), BF, 1), ((z, grid.x, r, m), BF, 0)]
    return relay(grid, "place_first", body, z, ins, outs)


def place_second(grid, over_x, over_a):
    x_spots = arrived(OWN_X, x_moves(grid))
    a_spots = arrived(OWN_A, a_moves(grid))
    z, r, n = over_x[0].shape[1:]
    m = over_a[0].shape[-1]

    def body(here, ins, outs):
        for piece, spot in zip(ins, x_spots):
            for ia in range(grid.a):
                outs[0][ia, 0, spot(*here)[0], :, :n] = piece[ia, 0]
        for piece, spot in zip(ins[len(x_spots) :], a_spots):
            for ix in range(grid.x):
                outs[0][spot(*here)[0], 0, ix, :, n:] = piece[0, ix]

    ins = [(piece, 1) for piece in over_x] + [(piece, 0) for piece in over_a]
    outs = [((grid.a, z, grid.x, r, n + m), BF, 1)]
    return relay(grid, "place_second", body, z, ins, outs)[0]


def join(grid, plane, other, width):
    r, n = plane.shape[-2:]
    parts = n // width
    owners = grid.a * grid.x

    def body(here, ins, outs):
        core = here[3]
        for source, at in ((ins[0], core), (ins[1], 1 - core)):
            for i in range(owners):
                for part in range(parts):
                    outs[0][0, i, at, part] = source[0, i, :, part * width : (part + 1) * width]

    plane, other = (
        array.reshape(grid.z, owners, r, n) for array in (plane, other)
    )
    outs = [((grid.z, owners, 2, parts, r, width), BF, 0)]
    (whole_array,) = relay(grid, "join", body, grid.z, [(plane, 0), (other, 0)], outs)
    return whole_array.reshape(-1, width)


def add_at(pieces, where):
    total = pieces[0][where].astype(F32)
    for piece in pieces[1:]:
        total = total + piece[where].astype(F32)
    return total


def add_core(grid, kept, got, cut):
    a_spots = leaving(OWN_A, a_moves(grid))
    x_spots = leaving(OWN_X, x_moves(grid))
    shape = (grid.a, grid.z, grid.x) + kept.shape[-2:]
    kept, got = kept.reshape(shape), got.reshape(shape)
    r, n = shape[-2:]
    low, high = slice(0, cut), slice(cut, n)

    def body(here, ins, outs):
        for out, spot in zip(outs, a_spots):
            for ix in range(grid.x):
                out[0, ix] = add_at(ins, (spot(*here)[0], 0, ix, slice(None), low)).astype(BF)
        for out, spot in zip(outs[len(a_spots) :], x_spots):
            for ia in range(grid.a):
                out[ia, 0] = add_at(ins, (ia, 0, spot(*here)[0], slice(None), high)).astype(BF)

    outs = [((grid.z, grid.x, r, cut), BF, 0)] * len(a_spots)
    outs += [((grid.a, grid.z, r, n - cut), BF, 1)] * len(x_spots)
    parts = relay(grid, "add_core", body, grid.z, [(kept, 1), (got, 1)], outs)
    return (
        send(parts[: len(a_spots)], a_moves(grid)),
        send(parts[len(a_spots) :], x_moves(grid)),
    )


def add_plane(grid, low, high):
    x_spots = leaving(OWN_X, x_moves(grid))
    a_spots = leaving(OWN_A, a_moves(grid))
    z, _, r, n = low[0].shape
    m = high[0].shape[-1]

    def body(here, ins, outs):
        for out, spot in zip(outs, x_spots):
            out[0] = add_at(ins[: len(low)], (0, spot(*here)[0])).astype(BF)
        for out, spot in zip(outs[len(x_spots) :], a_spots):
            out[0] = add_at(ins[len(low) :], (spot(*here)[0], 0)).astype(BF)

    ins = [(piece, 0) for piece in low] + [(piece, 1) for piece in high]
    outs = [((z, r, n), BF, 0)] * len(x_spots) + [((z, r, m), BF, 0)] * len(a_spots)
    parts = relay(grid, "add_plane", body, z, ins, outs)
    return (
        send(parts[: len(x_spots)], x_moves(grid)),
        send(parts[len(x_spots) :], a_moves(grid)),
    )


def add_both(grid, kept, got):
    spots = leaving(OWN_AX, both_moves(grid))
    shape = (grid.a, grid.z, grid.x) + kept.shape[-2:]

    def body(here, ins, outs):
        for out, spot in zip(outs, spots):
            ia, ix = spot(*here)
            out[0] = add_at(ins, (ia, 0, ix)).astype(BF)

    ins = [(kept.reshape(shape), 1), (got.reshape(shape), 1)]
    outs = [((grid.z,) + shape[-2:], BF, 0)] * len(spots)
    return send(relay(grid, "add_both", body, grid.z, ins, outs), both_moves(grid))


def add_z(grid, *halves):
    spots = leaving(OWN_Z, z_moves(grid))
    r = halves[0][0].shape[1]
    n = sum(half[0].shape[-1] for half in halves)

    def body(here, ins, outs):
        for out, spot in zip(outs, spots):
            at, first, lane = spot(*here)[0], 0, 0
            for half in halves:
                width = half[0].shape[-1]
                total = add_at(ins[first : first + len(half)], at)
                out[:, lane : lane + width] = total.astype(out.dtype)
                first, lane = first + len(half), lane + width

    ins = [(piece, None) for half in halves for piece in half]
    outs = [((r, n), F32, None)] + [((r, n), BF, None)] * (len(spots) - 1)
    return send(relay(grid, "add_z", body, 1, ins, outs), z_moves(grid))


def dot(left, right):
    return lax.dot_general(left, right, (((1,), (0,)), ((), ())), preferred_element_type=F32)


def dot_bt(left, right):
    return lax.dot_general(left, right, (((1,), (1,)), ((), ())), preferred_element_type=F32)


def dot_at(left, right):
    return lax.dot_general(left, right, (((0,), (0,)), ((), ())), preferred_element_type=F32)


def rms_scale(values):
    return lax.rsqrt(jnp.mean(values * values, axis=-1, keepdims=True) + EPS)


def norm_back(values, gain, grad):
    scale = rms_scale(values)
    scaled = grad * gain
    inner = jnp.mean(scaled * values, axis=-1, keepdims=True)
    grad_gain = jnp.sum(grad * (values * scale), axis=0, keepdims=True)
    return scale * scaled - values * (scale * scale * scale * inner), grad_gain


def positions_of(rows, short, width):
    row = lax.broadcasted_iota(jnp.int32, (rows, width), 0)
    return jnp.where(row < short, row, row - short), row < short


def shift_down(values, offset, position):
    return jnp.where(position >= offset, pltpu.roll(values, offset, 0), 0.0)


def shift_up(values, offset, room):
    rows = values.shape[0]
    return jnp.where(room >= offset, pltpu.roll(values, rows - offset, 0), 0.0)


def head_mask(half):
    lane = lax.broadcasted_iota(jnp.int32, (1, LANES), 1)
    return (lane // HEAD_DIM) == half


def blocks_of(rows, short):
    found = []
    for start, length in ((0, short), (short, rows - short)):
        for block in range(length // BLOCK):
            found.append((start + block * BLOCK, start, (block + 1) * BLOCK))
    return found


def store_split(value, owner_rows, kept, sent, lanes=slice(None)):
    core = lax.axis_index("fsdp") % 2
    for mine, first, second in ((0, kept, sent), (1, sent, kept)):

        @pl.when(core == mine)
        def _():
            for pair in range(value.shape[0] // (2 * owner_rows)):
                at = 2 * pair * owner_rows
                first[pair, :, lanes] = value[at : at + owner_rows].astype(BF)
                second[pair, :, lanes] = value[at + owner_rows : at + 2 * owner_rows].astype(BF)


def front_kernel(short, xs, xl, wq, wk, wv, wsmall, normed, small, *refs):
    rows = normed.shape[0]
    turned = jnp.transpose(wsmall[...].astype(F32))[:16]
    small[...] = turned
    gain = turned[9:10]
    for ref, first, count in ((xs, 0, short), (xl, short, rows - short)):
        x = ref[...].astype(F32)
        normed[first : first + count] = (x * rms_scale(x) * gain).astype(BF)
    front_group(short, normed, small, wq, wk, wv, *refs)


def front_more_kernel(short, normed, small, wq, wk, wv, *refs):
    front_group(short, normed, small, wq, wk, wv, *refs[-3:])


def front_group(short, normed, small, wq, wk, wv, projected, mixed, attended):
    rows = normed.shape[0]
    taps = small[:, :GROUP]
    position, _ = positions_of(rows, short, GROUP)
    base = normed[...]
    for k, w in enumerate((wq, wk, wv)):
        p = dot(base, w[...])
        projected[k] = p.astype(BF)
        mixed[k] = (
            taps[3 * k : 3 * k + 1] * p
            + taps[3 * k + 1 : 3 * k + 2] * shift_down(p, 1, position)
            + taps[3 * k + 2 : 3 * k + 3] * shift_down(p, 2, position)
        ).astype(BF)
    for pair in range(GROUP // LANES):
        lanes = slice(pair * LANES, (pair + 1) * LANES)
        for first, key_first, key_count in blocks_of(rows, short):
            queries = mixed[0, first : first + BLOCK, lanes]
            keys = mixed[1, key_first : key_first + key_count, lanes]
            values = mixed[2, key_first : key_first + key_count, lanes]
            row = lax.broadcasted_iota(jnp.int32, (BLOCK, key_count), 0) + (first - key_first)
            causal = lax.broadcasted_iota(jnp.int32, (BLOCK, key_count), 1) <= row
            total = None
            for half in range(2):
                scale = jnp.where(head_mask(half), HEAD_SCALE, 0.0).astype(BF)
                keep = jnp.where(head_mask(half), 1.0, 0.0).astype(BF)
                scores = jnp.where(causal, dot_bt(queries * scale, keys), NEG)
                peak = jnp.max(scores, axis=-1, keepdims=True)
                exponent = jnp.exp(scores - peak)
                weights = exponent * (1.0 / jnp.sum(exponent, axis=-1, keepdims=True))
                part = dot(weights.astype(BF), values * keep)
                total = part if total is None else total + part
            attended[first : first + BLOCK, lanes] = total.astype(BF)


def up_tile(owner_rows, normed, upstream, wup, squared, kept, sent):
    hidden = jnp.maximum(dot(normed[...], wup[...]), 0.0)
    low = (hidden * hidden).astype(BF)
    squared[...] = low
    store_split(dot_at(low, upstream[...]), owner_rows, kept, sent)


def up_kernel(
    short, owner_rows, ls, ll, xs, xl, cs, cl, attended, wout, wup, small,
    middle, normed, upstream, squared, kept, sent,
):
    step = pl.program_id(0)
    rows = normed.shape[0]

    @pl.when(step == 0)
    def _():
        gain = small[10:11]
        branch = dot(attended[...], wout[...])
        for ref, cot, limit, first, count in (
            (xs, cs, ls, 0, short),
            (xl, cl, ll, short, rows - short),
        ):
            part = slice(first, first + count)
            mid = ref[...].astype(F32) + branch[part]
            middle[part] = mid
            normed[part] = (mid * rms_scale(mid) * gain).astype(BF)
            position = lax.broadcasted_iota(jnp.int32, (count, D), 0)
            wide = jnp.where(position < limit[0], cot[...].astype(F32), 0.0)
            upstream[part] = wide.astype(BF)

    up_tile(owner_rows, normed, upstream, wup, squared, kept, sent)


def up_more_kernel(owner_rows, normed, upstream, wup, *refs):
    squared, kept, sent = refs[-3:]
    up_tile(owner_rows, normed, upstream, wup, squared, kept, sent)


def down_tile(owner_rows, upstream, wdown, squared, wup, normed, kept, sent, total, first):
    grad_squared = dot_bt(upstream[...], wdown[...])
    active = jnp.sqrt(squared[...].astype(F32))
    grad_hidden = (grad_squared * (2.0 * active)).astype(BF)
    store_split(dot_at(normed[...], grad_hidden), owner_rows, kept, sent)
    part = dot_bt(grad_hidden, wup[...])

    @pl.when(first)
    def _():
        total[...] = part

    @pl.when(jnp.logical_not(first))
    def _():
        total[...] += part


def down_kernel(owner_rows, upstream, wdown, squared, wup, normed, kept, sent, total):
    first = pl.program_id(0) == 0
    down_tile(owner_rows, upstream, wdown, squared, wup, normed, kept, sent, total, first)


def down_more_kernel(
    last, owner_rows, upstream, wdown, squared, wup, normed, attended, middle, small, before,
    *refs
):
    kept, sent, grad_middle, grad_branch, grad_gain, total = refs[-6:]
    step = pl.program_id(0)

    @pl.when(step == 0)
    def _():
        total[...] = before[...]

    @pl.when(step < last)
    def _():
        down_tile(owner_rows, upstream, wdown, squared, wup, normed, kept, sent, total, step < 0)

    @pl.when(step == last)
    def _():
        pulled, gain = norm_back(middle[...], small[10:11], total[...])
        grad_gain[...] = jnp.broadcast_to(gain, grad_gain.shape)
        wide = upstream[...].astype(F32) + pulled
        grad_middle[...] = wide
        low = wide.astype(BF)
        grad_branch[...] = low
        store_split(dot_at(attended[...], low), owner_rows, kept, sent)


def mixer_kernel(
    short, mixed, projected, branch, wout, small, *refs
):
    grad_projected, grad_taps, scratch = refs[-3:]
    rows = branch.shape[0]
    grad_attended = dot_bt(branch[...], wout[...]).astype(BF)
    for pair in range(GROUP // LANES):
        lanes = slice(pair * LANES, (pair + 1) * LANES)
        started = set()
        for first, key_first, key_count in blocks_of(rows, short):
            block = slice(first, first + BLOCK)
            spread = slice(key_first, key_first + key_count)
            queries = mixed[0, block, lanes]
            keys = mixed[1, spread, lanes]
            values = mixed[2, spread, lanes]
            grads = grad_attended[block, lanes]
            row = lax.broadcasted_iota(jnp.int32, (key_count, BLOCK), 1) + (first - key_first)
            causal = lax.broadcasted_iota(jnp.int32, (key_count, BLOCK), 0) <= row
            for_queries = for_keys = for_values = None
            for half in range(2):
                scale = jnp.where(head_mask(half), HEAD_SCALE, 0.0).astype(BF)
                keep = jnp.where(head_mask(half), 1.0, 0.0).astype(BF)
                scaled = queries * scale
                kept = grads * keep
                scores = jnp.where(causal, dot_bt(keys, scaled), NEG)
                peak = jnp.max(scores, axis=0, keepdims=True)
                exponent = jnp.exp(scores - peak)
                probs = exponent * (1.0 / jnp.sum(exponent, axis=0, keepdims=True))
                grad_probs = dot_bt(values, kept)
                inner = jnp.sum(probs * grad_probs, axis=0, keepdims=True)
                grad_scores = (probs * (grad_probs - inner)).astype(BF)
                to_values = dot(probs.astype(BF), kept)
                to_keys = dot(grad_scores, scaled)
                to_queries = dot_at(grad_scores, keys * scale)
                if half == 0:
                    for_queries, for_keys, for_values = to_queries, to_keys, to_values
                else:
                    for_queries = for_queries + to_queries
                    for_keys = for_keys + to_keys
                    for_values = for_values + to_values
            scratch[0, block, lanes] = for_queries
            for block_key in range(key_count // BLOCK):
                at = key_first + block_key * BLOCK
                inside = slice(block_key * BLOCK, (block_key + 1) * BLOCK)
                if at in started:
                    scratch[1, at : at + BLOCK, lanes] += for_keys[inside]
                    scratch[2, at : at + BLOCK, lanes] += for_values[inside]
                else:
                    started.add(at)
                    scratch[1, at : at + BLOCK, lanes] = for_keys[inside]
                    scratch[2, at : at + BLOCK, lanes] = for_values[inside]
    position, in_short = positions_of(rows, short, GROUP)
    room = jnp.where(in_short, short, rows - short) - 1 - position
    taps = small[...]
    for k in range(3):
        g = scratch[k]
        p = projected[k].astype(F32)
        grad_projected[k] = (
            taps[3 * k : 3 * k + 1] * g
            + taps[3 * k + 1 : 3 * k + 2] * shift_up(g, 1, room)
            + taps[3 * k + 2 : 3 * k + 3] * shift_up(g, 2, room)
        ).astype(BF)
        grad_taps[3 * k : 3 * k + 1] = jnp.sum(g * p, axis=0, keepdims=True)
        for j in (1, 2):
            grad_taps[3 * k + j : 3 * k + j + 1] = jnp.sum(
                g * shift_down(p, j, position), axis=0, keepdims=True
            )
    grad_taps[9:16] = jnp.zeros((7, GROUP), F32)


def back_kernel(owner_rows, grad_projected, w, normed, kept, sent, total):
    step = pl.program_id(0)
    g = grad_projected[0]
    store_split(dot_at(normed[...], g), owner_rows, kept, sent)
    part = dot_bt(g, w[...])

    @pl.when(step == 0)
    def _():
        total[...] = part

    @pl.when(step > 0)
    def _():
        total[...] += part


def back_more_kernel(
    short, owner_rows, xs, xl, grad_projected, w, normed, grad_middle, small, grad_taps,
    grad_gain_two, total, kept, sent, back_short, back_long,
):
    rows = normed.shape[0]
    g = grad_projected[0]
    store_split(dot_at(normed[...], g), owner_rows, kept, sent, slice(0, D))
    grad_normed = total[...] + dot_bt(g, w[...])
    gain_sum = None
    for ref, out, first, count in (
        (xs, back_short, 0, short),
        (xl, back_long, short, rows - short),
    ):
        rows_of = slice(first, first + count)
        pulled, gain = norm_back(ref[...].astype(F32), small[9:10], grad_normed[rows_of])
        out[...] = grad_middle[rows_of] + pulled
        gain_sum = gain if gain_sum is None else gain_sum + gain
    row = lax.broadcasted_iota(jnp.int32, (16, D), 0)
    packed = jnp.where(row == 9, gain_sum, grad_taps[...])
    packed = jnp.where(row == 10, grad_gain_two[0:1], packed)
    packed = jnp.concatenate([packed, jnp.zeros((LANES - 16, D), F32)], axis=0)
    store_split(jnp.transpose(packed), owner_rows, kept, sent, slice(D, D + LANES))


def output_kernel(short, squared, wdown, middle, out_short, out_long, total):
    step = pl.program_id(0)
    part = dot(squared[...], wdown[...])

    @pl.when(step == 0)
    def _():
        total[...] = middle[...] + part

    @pl.when(step > 0)
    def _():
        total[...] += part

    @pl.when(step == pl.num_programs(0) - 1)
    def _():
        out_short[...] = total[:short].astype(BF)
        out_long[...] = total[short:].astype(BF)


def whole(shape):
    zeros = (0,) * len(shape)
    return pl.BlockSpec(shape, lambda i: zeros, pipeline_mode=pl.Buffered(1))


def smem():
    return pl.BlockSpec(memory_space=pltpu.SMEM)


def struct(shape, dtype):
    return jax.ShapeDtypeStruct(shape, dtype)


def params(mib):
    return pltpu.CompilerParams(
        vmem_limit_bytes=mib * MIB, dimension_semantics=("arbitrary",)
    )


def cost(us):
    return pl.CostEstimate(
        flops=int(us * PEAK_PER_US * WEIGHT), bytes_accessed=0, transcendentals=0
    )


def update(grad, rate, weight, moment, average, outs, at=Ellipsis):
    moment_new = MOMENTUM * moment[at] + grad
    weight_new = weight[at].astype(F32) - rate * (grad + MOMENTUM * moment_new)
    outs[0][at] = grad
    outs[1][at] = moment_new
    outs[2][at] = weight_new
    outs[3][at] = AVERAGE * average[at] + (1.0 - AVERAGE) * weight_new


def total_of(pieces):
    total = pieces[0][...]
    for piece in pieces[1:]:
        total = total + piece[...].astype(F32)
    return total


def finish_kernel(kind, count, rates, *refs):
    pieces, rest = refs[:count], refs[count:]
    sets = len(rates)
    held = [rest[3 * i : 3 * i + 3] for i in range(sets)]
    outs = [rest[3 * sets + 4 * i : 3 * sets + 4 * i + 4] for i in range(sets)]
    if kind == "down":
        update(total_of(pieces), rates[0], *held[0], outs[0])
    elif kind == "up":
        total = total_of(pieces)
        update(total[:, :D], rates[0], *held[0], outs[0])
        update(total[:, D:], rates[1], *held[1], outs[1])
    else:
        total, more = total_of(pieces[: count // 2]), total_of(pieces[count // 2 :])
        for k in range(2):
            update(total[:, k * D : (k + 1) * D], rates[0], *held[0], outs[0], k)
        update(more[:, :D], rates[0], *held[0], outs[0], 2)
        r = total.shape[0]
        rest_rows = jnp.zeros((LANES - r, LANES), F32)
        turned = jnp.transpose(jnp.concatenate([more[:, D:], rest_rows], axis=0))
        for k in range(3):
            update(turned[3 * k : 3 * k + 3, :r], rates[1], *held[1], outs[1], k)
        update(turned[9:11, :r], rates[2], *held[2], outs[2])


def finish(kind, pieces, sets, rates):
    flat = [array for one in sets for array in one]
    shapes = [one[0].shape for one in sets for _ in range(4)]
    outs = pl.pallas_call(
        functools.partial(finish_kernel, kind, len(pieces), rates),
        grid=(1,),
        in_specs=[whole(array.shape) for array in list(pieces) + flat],
        out_specs=[whole(shape) for shape in shapes],
        out_shape=[struct(shape, F32) for shape in shapes],
        cost_estimate=cost(1.5),
        compiler_params=params(8),
        name="finish",
    )(*pieces, *flat)
    return [outs[4 * i : 4 * i + 4] for i in range(len(sets))]


def front_specs(rows, group):
    specs = [
        pl.BlockSpec((3, rows, GROUP), lambda i: (0, 0, group)),
        pl.BlockSpec((3, rows, GROUP), lambda i: (0, 0, group)),
        pl.BlockSpec((rows, GROUP), lambda i: (0, group)),
    ]
    shapes = [struct((3, rows, D), BF), struct((3, rows, D), BF), struct((rows, D), BF)]
    weights = [
        pl.BlockSpec((D, GROUP), lambda i, k=k: (0, k * GROUPS + group)) for k in range(3)
    ]
    return specs, shapes, weights


def front(act_short, act_long, w_attn):
    short, rows = act_short.shape[0], act_short.shape[0] + act_long.shape[0]
    specs, shapes, weights = front_specs(rows, 0)
    return pl.pallas_call(
        functools.partial(front_kernel, short),
        grid=(1,),
        in_specs=[whole(act_short.shape), whole(act_long.shape)]
        + weights
        + [pl.BlockSpec((D, LANES), lambda i: (0, 3 * D // LANES))],
        out_specs=[whole((rows, D)), whole((16, D))] + specs,
        out_shape=[struct((rows, D), BF), struct((16, D), F32)] + shapes,
        cost_estimate=cost(HEAVY),
        compiler_params=params(14),
        name="front",
    )(act_short, act_long, w_attn, w_attn, w_attn, w_attn)


def front_more(short, group, normed, small, w_attn, before):
    rows = normed.shape[0]
    specs, shapes, weights = front_specs(rows, group)
    again, aliases = kept_again(before, 5)
    return pl.pallas_call(
        functools.partial(front_more_kernel, short),
        grid=(1,),
        in_specs=[whole((rows, D)), pl.BlockSpec((16, GROUP), lambda i: (0, group))]
        + weights
        + again,
        out_specs=specs,
        out_shape=shapes,
        input_output_aliases=aliases,
        cost_estimate=cost(HEAVY if group == 1 else 1),
        compiler_params=params(14),
        name="front_more",
    )(normed, small, w_attn, w_attn, w_attn, *before)


def kept_again(before, first):
    specs = [pl.BlockSpec(memory_space=pl.ANY)] * len(before)
    return specs, {first + i: i for i in range(len(before))}


def up(act_short, act_long, cot_short, cot_long, len_short, len_long, attended, w_up, small, s):
    short, rows = act_short.shape[0], act_short.shape[0] + act_long.shape[0]
    ff = w_up.shape[1] - D
    tiles = ff // D
    half = D // (2 * s)
    halves = struct((tiles * half, s, D), BF)
    return pl.pallas_call(
        functools.partial(up_kernel, short, s),
        grid=(tiles // 2,),
        in_specs=[
            smem(),
            smem(),
            whole(act_short.shape),
            whole(act_long.shape),
            whole(cot_short.shape),
            whole(cot_long.shape),
            whole((rows, D)),
            pl.BlockSpec((D, D), lambda i: (0, 0)),
            pl.BlockSpec((D, D), lambda i: (0, 1 + i)),
            whole((16, D)),
        ],
        out_specs=[
            whole((rows, D)),
            whole((rows, D)),
            whole((rows, D)),
            pl.BlockSpec((rows, D), lambda i: (0, i)),
            pl.BlockSpec((half, s, D), lambda i: (i, 0, 0)),
            pl.BlockSpec((half, s, D), lambda i: (i, 0, 0)),
        ],
        out_shape=[
            struct((rows, D), F32),
            struct((rows, D), BF),
            struct((rows, D), BF),
            struct((rows, ff), BF),
            halves,
            halves,
        ],
        cost_estimate=cost(HEAVY),
        compiler_params=params(12),
        name="up",
    )(
        len_short, len_long, act_short, act_long, cot_short, cot_long, attended, w_up, w_up, small
    )


def up_more(normed_two, upstream, w_up, s, before):
    rows = upstream.shape[0]
    tiles = (w_up.shape[1] - D) // D
    first = tiles // 2
    half = D // (2 * s)
    specs, aliases = kept_again(before, 3)
    return pl.pallas_call(
        functools.partial(up_more_kernel, s),
        grid=(tiles - first,),
        in_specs=[
            whole((rows, D)),
            whole((rows, D)),
            pl.BlockSpec((D, D), lambda i: (0, 1 + first + i)),
        ]
        + specs,
        out_specs=[
            pl.BlockSpec((rows, D), lambda i: (0, first + i)),
            pl.BlockSpec((half, s, D), lambda i: (first + i, 0, 0)),
            pl.BlockSpec((half, s, D), lambda i: (first + i, 0, 0)),
        ],
        out_shape=[struct(array.shape, array.dtype) for array in before],
        input_output_aliases=aliases,
        cost_estimate=cost(HEAVY),
        compiler_params=params(10),
        name="up_more",
    )(normed_two, upstream, w_up, *before)


def down(upstream, w_down, squared, w_up, normed_two, r):
    rows = upstream.shape[0]
    ff = w_down.shape[0]
    count = ff // D // 2
    half = D // (2 * r)
    return pl.pallas_call(
        functools.partial(down_kernel, r),
        grid=(count,),
        in_specs=[
            whole((rows, D)),
            pl.BlockSpec((D, D), lambda i: (i, 0)),
            pl.BlockSpec((rows, D), lambda i: (0, i)),
            pl.BlockSpec((D, D), lambda i: (0, 1 + i)),
            whole((rows, D)),
        ],
        out_specs=[
            pl.BlockSpec((half, r, D), lambda i: (0, 0, 1 + i)),
            pl.BlockSpec((half, r, D), lambda i: (0, 0, 1 + i)),
            whole((rows, D)),
        ],
        out_shape=[
            struct((half, r, D + ff), BF),
            struct((half, r, D + ff), BF),
            struct((rows, D), F32),
        ],
        cost_estimate=cost(HEAVY),
        compiler_params=params(14),
        name="down",
    )(upstream, w_down, squared, w_up, normed_two)


def down_more(
    upstream, w_down, squared, w_up, normed_two, attended, middle, small, r, total, before
):
    rows = upstream.shape[0]
    ff = w_down.shape[0]
    tiles = ff // D
    begun = tiles // 2
    last = tiles - begun
    half = D // (2 * r)

    def tile(i):
        return begun + jnp.minimum(i, last - 1)

    def put(i):
        return (0, 0, jnp.where(i < last, 1 + begun + i, 0))

    specs, aliases = kept_again(before, 9)
    return pl.pallas_call(
        functools.partial(down_more_kernel, last, r),
        grid=(last + 1,),
        in_specs=[
            whole((rows, D)),
            pl.BlockSpec((D, D), lambda i: (tile(i), 0)),
            pl.BlockSpec((rows, D), lambda i: (0, tile(i))),
            pl.BlockSpec((D, D), lambda i: (0, 1 + tile(i))),
            whole((rows, D)),
            whole((rows, D)),
            whole((rows, D)),
            whole((16, D)),
            whole((rows, D)),
        ]
        + specs,
        out_specs=[
            pl.BlockSpec((half, r, D), put),
            pl.BlockSpec((half, r, D), put),
            whole((rows, D)),
            whole((rows, D)),
            whole((8, D)),
        ],
        out_shape=[
            struct((half, r, D + ff), BF),
            struct((half, r, D + ff), BF),
            struct((rows, D), F32),
            struct((rows, D), BF),
            struct((8, D), F32),
        ],
        input_output_aliases=aliases,
        scratch_shapes=[pltpu.VMEM((rows, D), F32)],
        cost_estimate=cost(HEAVY),
        compiler_params=params(16),
        name="down_more",
    )(
        upstream, w_down, squared, w_up, normed_two, attended, middle, small, total, *before
    )


def mixer(short, first, count, mixed, projected, grad_branch, w_up, small, before=()):
    rows = grad_branch.shape[0]
    return pl.pallas_call(
        functools.partial(mixer_kernel, short),
        grid=(count,),
        in_specs=[
            pl.BlockSpec((3, rows, GROUP), lambda i: (0, 0, first + i)),
            pl.BlockSpec((3, rows, GROUP), lambda i: (0, 0, first + i)),
            whole((rows, D)),
            pl.BlockSpec((GROUP, D), lambda i: (first + i, 0)),
            pl.BlockSpec((16, GROUP), lambda i: (0, first + i)),
        ]
        + [pl.BlockSpec(memory_space=pl.ANY)] * len(before),
        out_specs=[
            pl.BlockSpec((3, rows, GROUP), lambda i: (0, 0, first + i)),
            pl.BlockSpec((16, GROUP), lambda i: (0, first + i)),
        ],
        out_shape=[struct((3, rows, D), BF), struct((16, D), F32)],
        input_output_aliases={5 + i: i for i in range(len(before))},
        scratch_shapes=[pltpu.VMEM((3, rows, GROUP), F32)],
        cost_estimate=cost(HEAVY),
        compiler_params=params(14),
        name="mixer",
    )(mixed, projected, grad_branch, w_up, small, *before)


def back(grad_projected, w_attn, normed, r):
    rows = normed.shape[0]
    half = D // (2 * r)
    return pl.pallas_call(
        functools.partial(back_kernel, r),
        grid=(2,),
        in_specs=[
            pl.BlockSpec((1, rows, D), lambda i: (i, 0, 0)),
            pl.BlockSpec((D, D), lambda i: (0, i)),
            whole((rows, D)),
        ],
        out_specs=[
            pl.BlockSpec((half, r, D), lambda i: (0, 0, i)),
            pl.BlockSpec((half, r, D), lambda i: (0, 0, i)),
            whole((rows, D)),
        ],
        out_shape=[
            struct((half, r, 2 * D), BF),
            struct((half, r, 2 * D), BF),
            struct((rows, D), F32),
        ],
        cost_estimate=cost(HEAVY),
        compiler_params=params(18),
        name="back",
    )(grad_projected, w_attn, normed)


def back_more(
    act_short, act_long, grad_projected, w_attn, normed, grad_middle, small, grad_taps,
    grad_gain_two, total, r,
):
    short, rows = act_short.shape[0], normed.shape[0]
    half = D // (2 * r)
    wide = D + LANES
    return pl.pallas_call(
        functools.partial(back_more_kernel, short, r),
        grid=(1,),
        in_specs=[
            whole(act_short.shape),
            whole(act_long.shape),
            pl.BlockSpec((1, rows, D), lambda i: (2, 0, 0)),
            pl.BlockSpec((D, D), lambda i: (0, 2)),
            whole((rows, D)),
            whole((rows, D)),
            whole((16, D)),
            whole((16, D)),
            whole((8, D)),
            whole((rows, D)),
        ],
        out_specs=[
            whole((half, r, wide)),
            whole((half, r, wide)),
            whole(act_short.shape),
            whole(act_long.shape),
        ],
        out_shape=[
            struct((half, r, wide), BF),
            struct((half, r, wide), BF),
            struct(act_short.shape, F32),
            struct(act_long.shape, F32),
        ],
        cost_estimate=cost(HEAVY),
        compiler_params=params(20),
        name="back_more",
    )(
        act_short, act_long, grad_projected, w_attn, normed, grad_middle, small, grad_taps,
        grad_gain_two, total,
    )


def output(act_short, act_long, squared, w_down, middle):
    short, rows = act_short.shape[0], middle.shape[0]
    ff = w_down.shape[0]
    return pl.pallas_call(
        functools.partial(output_kernel, short),
        grid=(ff // D,),
        in_specs=[
            pl.BlockSpec((rows, D), lambda i: (0, i)),
            pl.BlockSpec((D, D), lambda i: (i, 0)),
            whole((rows, D)),
        ],
        out_specs=[whole(act_short.shape), whole(act_long.shape)],
        out_shape=[struct(act_short.shape, BF), struct(act_long.shape, BF)],
        scratch_shapes=[pltpu.VMEM((rows, D), F32)],
        cost_estimate=cost(HEAVY),
        compiler_params=params(10),
        name="output",
    )(squared, w_down, middle)


def shards(grid, *args):
    act_short, act_long, cot_short, cot_long, len_short, len_long = args[:6]
    owned = args[6:12]
    moments = args[12:18]
    averages = args[18:24]
    attn_rows, conv_cols, out_rows, up_rows, down_rows, gain_cols = owned
    r = out_rows.shape[0]
    s = down_rows.shape[0]
    short = act_short.shape[0]
    rows = short + act_long.shape[0]

    small_rows = jnp.concatenate([conv_cols.reshape(9, r), gain_cols], axis=0).T
    small_rows = jnp.pad(small_rows, ((0, 0), (0, LANES - 11)))
    chunk_attn = jnp.concatenate([attn_rows[0], attn_rows[1], attn_rows[2], small_rows], axis=1)
    parts = s // r
    chunk_up = jnp.concatenate([out_rows, up_rows], axis=1)
    chunk_down = jnp.concatenate([down_rows[i * r : (i + 1) * r] for i in range(parts)], axis=1)
    wide, wide_up, wide_down = chunk_attn.shape[1], chunk_up.shape[1], chunk_down.shape[1]
    over_a, over_x, over_z = a_moves(grid), x_moves(grid), z_moves(grid)

    pieces = exchange(chunk_attn, over_z)
    (col_attn,) = place_z(grid, pieces, [(0, wide)])
    pieces_attn = exchange(col_attn, both_moves(grid))
    pieces_up = exchange(after(chunk_up, col_attn), over_z)
    plane_attn = place_both(grid, held_back(pieces_attn, *pieces_up[1:]))
    other_attn = swap(grid, plane_attn)
    up_low, up_high = halves(grid, held_back(pieces_up, plane_attn), wide_up)
    pieces_down = exchange(after(chunk_down, plane_attn), over_z)
    up_low, up_high = exchange(up_low, over_a), exchange(up_high, over_x)
    w_attn = join(grid, plane_attn, other_attn, wide)
    normed, small, *begun = front(act_short, act_long, w_attn)
    up_low, up_high = place_first(grid, held_back(up_low, normed), held_back(up_high, normed))
    up_low, up_high = exchange(up_low, over_x), exchange(up_high, over_a)
    begun = front_more(short, 1, after(normed, up_low[0]), small, w_attn, begun)
    down_low, down_high = halves(grid, held_back(pieces_down, begun[2]), wide_down)
    down_low, down_high = exchange(down_low, over_a), exchange(down_high, over_x)
    projected, mixed, attended = front_more(
        short, 2, after(normed, down_low[0]), small, w_attn, begun
    )
    down_low, down_high = place_first(
        grid, held_back(down_low, attended), held_back(down_high, attended)
    )
    plane_up = place_second(
        grid, held_back(up_low, attended, down_low), held_back(up_high, attended, down_low)
    )
    other_up = swap(grid, plane_up)
    down_low, down_high = exchange(after(down_low, plane_up), over_x), exchange(down_high, over_a)
    w_up = join(grid, plane_up, after(other_up, down_low[0]), wide_up)
    middle, normed_two, upstream, *begun = up(
        act_short, act_long, cot_short, cot_long, len_short, len_long, attended, w_up, small, s
    )
    plane_down = place_second(
        grid, held_back(down_low, normed_two), held_back(down_high, normed_two)
    )
    other_down = swap(grid, plane_down)
    squared, kept_down, sent_down = up_more(
        after(normed_two, plane_down), upstream, w_up, s, begun
    )
    w_down = join(grid, plane_down, after(other_down, squared), D)

    sent_down = swap(grid, sent_down)
    *begun, total = down(upstream, w_down, squared, w_up, normed_two, r)
    low_down, high_down = add_core(grid, kept_down, after(sent_down, total), D // 2)
    kept_up, sent_up, grad_middle, grad_branch, grad_gain_two = down_more(
        after(upstream, low_down[0]), w_down, squared, w_up, normed_two, attended, middle, small,
        r, total, begun,
    )
    sent_up = swap(grid, sent_up)
    low_down, high_down = add_plane(
        grid, held_back(low_down, grad_branch), held_back(high_down, grad_branch)
    )
    first = mixer(short, 0, 1, mixed, projected, after(grad_branch, low_down[0]), w_up, small)
    low_up, high_up = add_core(grid, kept_up, after(sent_up, first[1]), wide_up // 2)
    pieces_down = add_z(grid, held_back(low_down, first[1]), held_back(high_down, first[1]))
    first = (after(first[0], low_up[0], pieces_down[0]), first[1])
    grad_projected, grad_taps = mixer(
        short, 1, GROUPS - 1, mixed, projected, grad_branch, w_up, small, before=first
    )
    low_up, high_up = add_plane(
        grid, held_back(low_up, grad_taps), held_back(high_up, grad_taps)
    )
    pieces_down = held_back(pieces_down, grad_taps)
    kept_qk, sent_qk, total = back(
        grad_projected, w_attn, after(normed, low_up[0], *pieces_down[1:]), r
    )
    sent_qk = swap(grid, sent_qk)
    pieces_up = add_z(grid, held_back(low_up, total), held_back(high_up, total))
    kept_v, sent_v, back_short, back_long = back_more(
        act_short, act_long, grad_projected, w_attn, normed, grad_middle, small, grad_taps,
        grad_gain_two, total, r,
    )
    sent_v = swap(grid, sent_v)
    pieces_qk = add_both(grid, kept_qk, after(sent_qk, back_short))
    out_short, out_long = output(
        act_short, act_long, squared, w_down, after(middle, back_short, pieces_qk[0], pieces_up[0])
    )
    pieces_qk = held_back(pieces_qk, out_short)
    pieces_up = held_back(pieces_up, out_short)
    pieces_v = add_both(grid, kept_v, after(sent_v, out_short, *pieces_qk[1:]))
    pieces_down = held_back(pieces_down, pieces_v[0])
    pieces_qk = add_z(grid, held_back(pieces_qk, pieces_v[0]))
    pieces_v = add_z(grid, held_back(pieces_v, pieces_qk[0]))
    pieces_attn = list(pieces_qk) + list(pieces_v)

    scale_tokens = math.sqrt(rows * grid.a * grid.f)
    rates = [rate / scale_tokens for rate in RATES]
    sets = list(zip(owned, moments, averages))
    (done_down,) = finish("down", pieces_down, [sets[4]], [rates[4]])
    done_out, done_up = finish("up", pieces_up, sets[2:4], rates[2:4])
    done_attn, done_taps, done_gains = finish(
        "attn", pieces_attn, [sets[0], sets[1], sets[5]], [rates[0], rates[1], rates[5]]
    )
    results = [out_short, out_long, back_short, back_long]
    for done in (done_attn, done_taps, done_out, done_up, done_down, done_gains):
        results.extend(done)
    return tuple(results)


def solution(mesh):
    rows = P(AXES, None)
    weights = [P(None, AXES, None), P(None, None, AXES), rows, rows, rows, P(None, AXES)]
    in_specs = tuple([rows] * 4 + [P(AXES)] * 2 + weights * 3)
    out_specs = tuple([rows] * 4 + [spec for spec in weights for _ in range(4)])
    grid = Grid(mesh)

    def program(*args):
        return shards(grid, *args)

    return jax.shard_map(
        program, mesh=mesh, in_specs=in_specs, out_specs=out_specs, check_vma=False
    )
```

```python
import functools
import math

import jax
import jax.numpy as jnp
from jax import lax
from jax.experimental import pallas as pl
from jax.experimental.pallas import tpu as pltpu
from jax.sharding import PartitionSpec as P

D = 768
HEAD_DIM = 64
GROUP = 256
GROUPS = D // GROUP
BLOCK = 256
LANES = 128

EPS = 1e-06
MOMENTUM = 0.9
AVERAGE = 0.5
RATES = (0.03, 0.5, 0.6, 0.025, 0.007, 0.05)
NEG = -1e30
HEAD_SCALE = 0.125
AXES = ("dp", "fsdp")
BF = jnp.bfloat16
F32 = jnp.float32
MIB = 1024 * 1024
PEAK_PER_US = 1.15e9
WEIGHT = 1.0
HEAVY = 100


class Grid:
    def __init__(self, mesh):
        self.a = mesh.shape["dp"]
        self.f = mesh.shape["fsdp"]
        self.x = 2
        self.z = self.f // 4

    def index(self, a, z, x, c):
        return a * self.f + (z * self.x + x) * 2 + c

    def perm(self, move):
        pairs = []
        for a in range(self.a):
            for z in range(self.z):
                for x in range(self.x):
                    for c in range(2):
                        pairs.append((self.index(a, z, x, c), self.index(*move(a, z, x, c))))
        return pairs

    def swap_core(self):
        return self.perm(lambda a, z, x, c: (a, z, x, 1 - c))

    def shift_plane(self, da, dx):
        return self.perm(lambda a, z, x, c: ((a + da) % self.a, z, (x + dx) % self.x, c))

    def shift_z(self, dz):
        return self.perm(lambda a, z, x, c: (a, (z + dz) % self.z, x, c))

    def here(self):
        f = lax.axis_index("fsdp")
        return lax.axis_index("dp"), f // 4, (f // 2) % 2, f % 2

    def plane_moves(self):
        return [(da, dx) for da in range(self.a) for dx in range(self.x) if da or dx]


def after(value, *others):
    return lax.optimization_barrier((value,) + others)[0]


def relay_kernel(grid, body, count, *refs):
    body(grid.here(), refs[:count], refs[count:])


def along(shape, axis):
    if axis is None:
        return pl.BlockSpec(shape, lambda i: (0,) * len(shape))
    block = tuple(1 if j == axis else size for j, size in enumerate(shape))
    return pl.BlockSpec(block, lambda i: tuple(i if j == axis else 0 for j in range(len(shape))))


def relay(grid, name, body, steps, ins, outs, weight=1):
    return pl.pallas_call(
        functools.partial(relay_kernel, grid, body, len(ins)),
        grid=(steps,),
        in_specs=[along(array.shape, axis) for array, axis in ins],
        out_specs=[along(shape, axis) for shape, _, axis in outs],
        out_shape=[jax.ShapeDtypeStruct(shape, kind) for shape, kind, _ in outs],
        cost_estimate=cost(weight),
        compiler_params=params(8),
        name=name,
    )(*[array for array, _ in ins])


def z_moves(grid):
    return [
        (
            grid.shift_z(dz),
            lambda a, z, x, c, dz=dz: ((z + dz) % grid.z,),
            lambda a, z, x, c, dz=dz: ((z - dz) % grid.z,),
        )
        for dz in range(1, grid.z)
    ]


def a_moves(grid):
    return [
        (
            grid.shift_plane(da, 0),
            lambda a, z, x, c, da=da: ((a + da) % grid.a,),
            lambda a, z, x, c, da=da: ((a - da) % grid.a,),
        )
        for da in range(1, grid.a)
    ]


def x_moves(grid):
    return [
        (
            grid.shift_plane(0, 1),
            lambda a, z, x, c: (1 - x,),
            lambda a, z, x, c: (1 - x,),
        )
    ]


def both_moves(grid):
    return [
        (
            grid.shift_plane(da, dx),
            lambda a, z, x, c, da=da, dx=dx: ((a + da) % grid.a, (x + dx) % grid.x),
            lambda a, z, x, c, da=da, dx=dx: ((a - da) % grid.a, (x - dx) % grid.x),
        )
        for da, dx in grid.plane_moves()
    ]


OWN_Z = lambda a, z, x, c: (z,)
OWN_A = lambda a, z, x, c: (a,)
OWN_X = lambda a, z, x, c: (x,)
OWN_AX = lambda a, z, x, c: (a, x)


def exchange(value, moves):
    return [value] + [lax.ppermute(value, AXES, pairs) for pairs, _, _ in moves]


def send(parts, moves):
    return [parts[0]] + [
        lax.ppermute(part, AXES, pairs) for part, (pairs, _, _) in zip(parts[1:], moves)
    ]


def swap(grid, value):
    return lax.ppermute(value, AXES, grid.swap_core())


def arrived(own, moves):
    return [own] + [brought for _, _, brought in moves]


def leaving(own, moves):
    return [own] + [sent for _, sent, _ in moves]


def held_back(pieces, *others):
    return [pieces[0]] + [after(piece, *others) for piece in pieces[1:]]


def place_z(grid, pieces, cuts):
    spots = arrived(OWN_Z, z_moves(grid))
    r = pieces[0].shape[0]

    def body(here, ins, outs):
        for piece, spot in zip(ins, spots):
            at = spot(*here)[0]
            for out, (low, high) in zip(outs, cuts):
                out[at] = piece[:, low:high]

    outs = [((grid.z, r, high - low), BF, None) for low, high in cuts]
    return relay(grid, "place_z", body, 1, [(piece, None) for piece in pieces], outs)


def halves(grid, pieces, width):
    return place_z(grid, pieces, [(0, width // 2), (width // 2, width)])


def place_both(grid, pieces):
    spots = arrived(OWN_AX, both_moves(grid))

    def body(here, ins, outs):
        for piece, spot in zip(ins, spots):
            ia, ix = spot(*here)
            outs[0][ia, 0, ix] = piece[0]

    z, r, n = pieces[0].shape
    outs = [((grid.a, z, grid.x, r, n), BF, 1)]
    return relay(grid, "place_both", body, z, [(piece, 0) for piece in pieces], outs)[0]


def place_first(grid, over_a, over_x):
    a_spots = arrived(OWN_A, a_moves(grid))
    x_spots = arrived(OWN_X, x_moves(grid))

    def body(here, ins, outs):
        for piece, spot in zip(ins, a_spots):
            outs[0][spot(*here)[0], 0] = piece[0]
        for piece, spot in zip(ins[len(a_spots) :], x_spots):
            outs[1][0, spot(*here)[0]] = piece[0]

    z, r, n = over_a[0].shape
    m = over_x[0].shape[-1]
    ins = [(piece, 0) for piece in over_a + over_x]
    outs = [((grid.a, z, r, n), BF, 1), ((z, grid.x, r, m), BF, 0)]
    return relay(grid, "place_first", body, z, ins, outs)


def place_second(grid, over_x, over_a):
    x_spots = arrived(OWN_X, x_moves(grid))
    a_spots = arrived(OWN_A, a_moves(grid))
    z, r, n = over_x[0].shape[1:]
    m = over_a[0].shape[-1]

    def body(here, ins, outs):
        for piece, spot in zip(ins, x_spots):
            for ia in range(grid.a):
                outs[0][ia, 0, spot(*here)[0], :, :n] = piece[ia, 0]
        for piece, spot in zip(ins[len(x_spots) :], a_spots):
            for ix in range(grid.x):
                outs[0][spot(*here)[0], 0, ix, :, n:] = piece[0, ix]

    ins = [(piece, 1) for piece in over_x] + [(piece, 0) for piece in over_a]
    outs = [((grid.a, z, grid.x, r, n + m), BF, 1)]
    return relay(grid, "place_second", body, z, ins, outs)[0]


def join(grid, plane, other, width):
    r, n = plane.shape[-2:]
    parts = n // width
    owners = grid.a * grid.x

    def body(here, ins, outs):
        core = here[3]
        for source, at in ((ins[0], core), (ins[1], 1 - core)):
            for i in range(owners):
                for part in range(parts):
                    outs[0][0, i, at, part] = source[0, i, :, part * width : (part + 1) * width]

    plane, other = (
        array.reshape(grid.z, owners, r, n) for array in (plane, other)
    )
    outs = [((grid.z, owners, 2, parts, r, width), BF, 0)]
    (whole_array,) = relay(grid, "join", body, grid.z, [(plane, 0), (other, 0)], outs)
    return whole_array.reshape(-1, width)


def add_at(pieces, where):
    total = pieces[0][where].astype(F32)
    for piece in pieces[1:]:
        total = total + piece[where].astype(F32)
    return total


def add_core(grid, kept, got, cut):
    a_spots = leaving(OWN_A, a_moves(grid))
    x_spots = leaving(OWN_X, x_moves(grid))
    shape = (grid.a, grid.z, grid.x) + kept.shape[-2:]
    kept, got = kept.reshape(shape), got.reshape(shape)
    r, n = shape[-2:]
    low, high = slice(0, cut), slice(cut, n)

    def body(here, ins, outs):
        for out, spot in zip(outs, a_spots):
            for ix in range(grid.x):
                out[0, ix] = add_at(ins, (spot(*here)[0], 0, ix, slice(None), low)).astype(BF)
        for out, spot in zip(outs[len(a_spots) :], x_spots):
            for ia in range(grid.a):
                out[ia, 0] = add_at(ins, (ia, 0, spot(*here)[0], slice(None), high)).astype(BF)

    outs = [((grid.z, grid.x, r, cut), BF, 0)] * len(a_spots)
    outs += [((grid.a, grid.z, r, n - cut), BF, 1)] * len(x_spots)
    parts = relay(grid, "add_core", body, grid.z, [(kept, 1), (got, 1)], outs)
    return (
        send(parts[: len(a_spots)], a_moves(grid)),
        send(parts[len(a_spots) :], x_moves(grid)),
    )


def add_plane(grid, low, high):
    x_spots = leaving(OWN_X, x_moves(grid))
    a_spots = leaving(OWN_A, a_moves(grid))
    z, _, r, n = low[0].shape
    m = high[0].shape[-1]

    def body(here, ins, outs):
        for out, spot in zip(outs, x_spots):
            out[0] = add_at(ins[: len(low)], (0, spot(*here)[0])).astype(BF)
        for out, spot in zip(outs[len(x_spots) :], a_spots):
            out[0] = add_at(ins[len(low) :], (spot(*here)[0], 0)).astype(BF)

    ins = [(piece, 0) for piece in low] + [(piece, 1) for piece in high]
    outs = [((z, r, n), BF, 0)] * len(x_spots) + [((z, r, m), BF, 0)] * len(a_spots)
    parts = relay(grid, "add_plane", body, z, ins, outs, HEAVY)
    return (
        send(parts[: len(x_spots)], x_moves(grid)),
        send(parts[len(x_spots) :], a_moves(grid)),
    )


def add_both(grid, kept, got, weight=1):
    spots = leaving(OWN_AX, both_moves(grid))
    shape = (grid.a, grid.z, grid.x) + kept.shape[-2:]

    def body(here, ins, outs):
        for out, spot in zip(outs, spots):
            ia, ix = spot(*here)
            out[0] = add_at(ins, (ia, 0, ix)).astype(BF)

    ins = [(kept.reshape(shape), 1), (got.reshape(shape), 1)]
    outs = [((grid.z,) + shape[-2:], BF, 0)] * len(spots)
    return send(relay(grid, "add_both", body, grid.z, ins, outs, weight), both_moves(grid))


def add_z(grid, r, parts):
    spots = leaving(OWN_Z, z_moves(grid))
    lanes, end = [], 0
    for part in parts:
        widths = [half[0].shape[-1] for half in part]
        lanes.append((end, widths))
        end += sum(widths) * (part[0][0].shape[1] // r)

    def body(here, ins, outs):
        for out, spot in zip(outs, spots):
            at, first = spot(*here)[0], 0
            for part, (start, widths) in zip(parts, lanes):
                for i, half in enumerate(part):
                    total = add_at(ins[first : first + len(half)], at)
                    for slab in range(total.shape[0] // r):
                        low = start + slab * sum(widths) + sum(widths[:i])
                        piece = total[slab * r : (slab + 1) * r]
                        out[:, low : low + widths[i]] = piece.astype(out.dtype)
                    first += len(half)

    ins = [(piece, None) for part in parts for half in part for piece in half]
    outs = [((r, end), F32, None)] + [((r, end), BF, None)] * (len(spots) - 1)
    return send(relay(grid, "add_z", body, 1, ins, outs), z_moves(grid))


def dot(left, right):
    return lax.dot_general(left, right, (((1,), (0,)), ((), ())), preferred_element_type=F32)


def dot_bt(left, right):
    return lax.dot_general(left, right, (((1,), (1,)), ((), ())), preferred_element_type=F32)


def dot_at(left, right):
    return lax.dot_general(left, right, (((0,), (0,)), ((), ())), preferred_element_type=F32)


def rms_scale(values):
    return lax.rsqrt(jnp.mean(values * values, axis=-1, keepdims=True) + EPS)


def norm_back(values, gain, grad):
    scale = rms_scale(values)
    scaled = grad * gain
    inner = jnp.mean(scaled * values, axis=-1, keepdims=True)
    grad_gain = jnp.sum(grad * (values * scale), axis=0, keepdims=True)
    return scale * scaled - values * (scale * scale * scale * inner), grad_gain


def positions_of(rows, short, width):
    row = lax.broadcasted_iota(jnp.int32, (rows, width), 0)
    return jnp.where(row < short, row, row - short), row < short


def shift_down(values, offset, position):
    return jnp.where(position >= offset, pltpu.roll(values, offset, 0), 0.0)


def shift_up(values, offset, room):
    rows = values.shape[0]
    return jnp.where(room >= offset, pltpu.roll(values, rows - offset, 0), 0.0)


def head_mask(half):
    lane = lax.broadcasted_iota(jnp.int32, (1, LANES), 1)
    return (lane // HEAD_DIM) == half


def blocks_of(rows, short):
    found = []
    for start, length in ((0, short), (short, rows - short)):
        for block in range(length // BLOCK):
            found.append((start + block * BLOCK, start, (block + 1) * BLOCK))
    return found


def store_split(value, owner_rows, kept, sent, lanes=slice(None)):
    first = lax.axis_index("fsdp") % 2 == 0
    for pair in range(value.shape[0] // (2 * owner_rows)):
        at = 2 * pair * owner_rows
        even, odd = value[at : at + owner_rows], value[at + owner_rows : at + 2 * owner_rows]
        kept[pair, :, lanes] = jnp.where(first, even, odd).astype(BF)
        sent[pair, :, lanes] = jnp.where(first, odd, even).astype(BF)


def _():
            for pair in range(value.shape[0] // (2 * owner_rows)):
                at = 2 * pair * owner_rows
                first[pair, :, lanes] = value[at : at + owner_rows].astype(BF)
                second[pair, :, lanes] = value[at + owner_rows : at + 2 * owner_rows].astype(BF)


def front_kernel(short, xs, xl, w, normed, small, *refs):
    rows = normed.shape[0]
    turned = jnp.transpose(w[:, 3 * D : 3 * D + LANES].astype(F32))[:16]
    small[...] = turned
    gain = turned[9:10]
    for ref, first, count in ((xs, 0, short), (xl, short, rows - short)):
        x = ref[...].astype(F32)
        normed[first : first + count] = (x * rms_scale(x) * gain).astype(BF)
    front_group(short, 0, normed, small, w, *refs)


def front_more_kernel(short, group, normed, small, w, *refs):
    front_group(short, group, normed, small, w, *refs[-3:])


def front_group(short, group, normed, small, w, projected, mixed, attended):
    rows = normed.shape[0]
    columns = slice(group * GROUP, (group + 1) * GROUP)
    taps = small[:, columns]
    position, _ = positions_of(rows, short, GROUP)
    base = normed[...]
    for k in range(3):
        p = dot(base, w[:, k * D + group * GROUP : k * D + (group + 1) * GROUP])
        projected[k, :, columns] = p.astype(BF)
        mixed[k, :, columns] = (
            taps[3 * k : 3 * k + 1] * p
            + taps[3 * k + 1 : 3 * k + 2] * shift_down(p, 1, position)
            + taps[3 * k + 2 : 3 * k + 3] * shift_down(p, 2, position)
        ).astype(BF)
    for pair in range(GROUP // LANES):
        lane = group * GROUP + pair * LANES
        lanes = slice(lane, lane + LANES)
        for first, key_first, key_count in blocks_of(rows, short):
            queries = mixed[0, first : first + BLOCK, lanes]
            keys = mixed[1, key_first : key_first + key_count, lanes]
            values = mixed[2, key_first : key_first + key_count, lanes]
            row = lax.broadcasted_iota(jnp.int32, (BLOCK, key_count), 0) + (first - key_first)
            causal = lax.broadcasted_iota(jnp.int32, (BLOCK, key_count), 1) <= row
            total = None
            for half in range(2):
                scale = jnp.where(head_mask(half), HEAD_SCALE, 0.0).astype(BF)
                keep = jnp.where(head_mask(half), 1.0, 0.0).astype(BF)
                scores = jnp.where(causal, dot_bt(queries * scale, keys), NEG)
                peak = jnp.max(scores, axis=-1, keepdims=True)
                exponent = jnp.exp(scores - peak)
                weights = exponent * (1.0 / jnp.sum(exponent, axis=-1, keepdims=True))
                part = dot(weights.astype(BF), values * keep)
                total = part if total is None else total + part
            attended[first : first + BLOCK, lanes] = total.astype(BF)


def pack_kernel(attn, taps, gains, out, scratch):
    r = attn.shape[1]
    scratch[...] = jnp.zeros_like(scratch)
    for k in range(3):
        out[:, k * D : (k + 1) * D] = attn[k]
        scratch[3 * k : 3 * k + 3, :r] = taps[k].astype(F32)
    scratch[9:11, :r] = gains[...].astype(F32)
    out[:, 3 * D :] = jnp.transpose(scratch[...])[:r].astype(BF)


def up_tile(owner_rows, normed, upstream, wup, squared, kept, sent):
    hidden = jnp.maximum(dot(normed[...], wup[...]), 0.0)
    low = (hidden * hidden).astype(BF)
    squared[...] = low
    store_split(dot_at(low, upstream[...]), owner_rows, kept, sent)


def up_kernel(
    short, owner_rows, ls, ll, xs, xl, cs, cl, attended, wout, wup, small,
    middle, normed, upstream, squared, kept, sent,
):
    step = pl.program_id(0)
    rows = normed.shape[0]

    @pl.when(step == 0)
    def _():
        gain = small[10:11]
        branch = dot(attended[...], wout[...])
        for ref, cot, limit, first, count in (
            (xs, cs, ls, 0, short),
            (xl, cl, ll, short, rows - short),
        ):
            part = slice(first, first + count)
            mid = ref[...].astype(F32) + branch[part]
            middle[part] = mid
            normed[part] = (mid * rms_scale(mid) * gain).astype(BF)
            position = lax.broadcasted_iota(jnp.int32, (count, D), 0)
            wide = jnp.where(position < limit[0], cot[...].astype(F32), 0.0)
            upstream[part] = wide.astype(BF)

    up_tile(owner_rows, normed, upstream, wup, squared, kept, sent)


def up_more_kernel(owner_rows, normed, upstream, wup, *refs):
    kept, sent, squared = refs[-3:]
    up_tile(owner_rows, normed, upstream, wup, squared, kept, sent)


def down_tile(owner_rows, upstream, wdown, squared, wup, normed, kept, sent, total, first):
    grad_squared = dot_bt(upstream[...], wdown[...])
    active = jnp.sqrt(squared[...].astype(F32))
    grad_hidden = (grad_squared * (2.0 * active)).astype(BF)
    store_split(dot_at(normed[...], grad_hidden), owner_rows, kept, sent)
    part = dot_bt(grad_hidden, wup[...])

    @pl.when(first)
    def _():
        total[...] = part

    @pl.when(jnp.logical_not(first))
    def _():
        total[...] += part


def down_kernel(owner_rows, upstream, wdown, squared, wup, normed, kept, sent, total):
    first = pl.program_id(0) == 0
    down_tile(owner_rows, upstream, wdown, squared, wup, normed, kept, sent, total, first)


def down_more_kernel(
    last, owner_rows, upstream, wdown, squared, wup, normed, attended, middle, small, before,
    *refs
):
    kept, sent, grad_middle, grad_branch, grad_gain, total = refs[-6:]
    step = pl.program_id(0)

    @pl.when(step == 0)
    def _():
        total[...] = before[...]

    @pl.when(step < last)
    def _():
        down_tile(owner_rows, upstream, wdown, squared, wup, normed, kept, sent, total, step < 0)

    @pl.when(step == last)
    def _():
        pulled, gain = norm_back(middle[...], small[10:11], total[...])
        grad_gain[...] = jnp.broadcast_to(gain, grad_gain.shape)
        wide = upstream[...].astype(F32) + pulled
        grad_middle[...] = wide
        low = wide.astype(BF)
        grad_branch[...] = low
        store_split(dot_at(attended[...], low), owner_rows, kept, sent)


def mixer_kernel(
    short, owner_rows, group, mixed, projected, branch, w_up, small, normed, w, *refs
):
    scratch, w_out, ready = refs[-3:]
    refs = refs[:-2]
    columns = slice(group * GROUP, (group + 1) * GROUP)
    fetch = pltpu.make_async_copy(w_up.at[columns, :D], w_out, ready)
    fetch.start()
    if group == 0:
        before = None
    else:
        before, refs = refs[0], refs[1:]
    if group < GROUPS - 1:
        kept, sent, taps_out, total = refs[-5:-1]
    else:
        xs, xl, grad_middle, taps_before, grad_gain_two = refs[:5]
        kept, sent, back_short, back_long = refs[-5:-1]
    rows = branch.shape[0]
    fetch.wait()
    grad_attended = dot_bt(branch[...], w_out[...]).astype(BF)
    for pair in range(GROUP // LANES):
        lanes = slice(pair * LANES, (pair + 1) * LANES)
        lane = group * GROUP + pair * LANES
        far = slice(lane, lane + LANES)
        started = set()
        for first, key_first, key_count in blocks_of(rows, short):
            block = slice(first, first + BLOCK)
            spread = slice(key_first, key_first + key_count)
            queries = mixed[0, block, far]
            keys = mixed[1, spread, far]
            values = mixed[2, spread, far]
            grads = grad_attended[block, lanes]
            row = lax.broadcasted_iota(jnp.int32, (key_count, BLOCK), 1) + (first - key_first)
            causal = lax.broadcasted_iota(jnp.int32, (key_count, BLOCK), 0) <= row
            for_queries = for_keys = for_values = None
            for half in range(2):
                scale = jnp.where(head_mask(half), HEAD_SCALE, 0.0).astype(BF)
                keep = jnp.where(head_mask(half), 1.0, 0.0).astype(BF)
                scaled = queries * scale
                own = grads * keep
                scores = jnp.where(causal, dot_bt(keys, scaled), NEG)
                peak = jnp.max(scores, axis=0, keepdims=True)
                exponent = jnp.exp(scores - peak)
                probs = exponent * (1.0 / jnp.sum(exponent, axis=0, keepdims=True))
                grad_probs = dot_bt(values, own)
                inner = jnp.sum(probs * grad_probs, axis=0, keepdims=True)
                grad_scores = (probs * (grad_probs - inner)).astype(BF)
                to_values = dot(probs.astype(BF), own)
                to_keys = dot(grad_scores, scaled)
                to_queries = dot_at(grad_scores, keys * scale)
                if half == 0:
                    for_queries, for_keys, for_values = to_queries, to_keys, to_values
                else:
                    for_queries = for_queries + to_queries
                    for_keys = for_keys + to_keys
                    for_values = for_values + to_values
            scratch[0, block, lanes] = for_queries
            for block_key in range(key_count // BLOCK):
                at = key_first + block_key * BLOCK
                inside = slice(block_key * BLOCK, (block_key + 1) * BLOCK)
                if at in started:
                    scratch[1, at : at + BLOCK, lanes] += for_keys[inside]
                    scratch[2, at : at + BLOCK, lanes] += for_values[inside]
                else:
                    started.add(at)
                    scratch[1, at : at + BLOCK, lanes] = for_keys[inside]
                    scratch[2, at : at + BLOCK, lanes] = for_values[inside]
    position, in_short = positions_of(rows, short, GROUP)
    room = jnp.where(in_short, short, rows - short) - 1 - position
    taps = small[:, columns]
    tap_rows = []
    grad_normed = None if before is None else before[...]
    for k in range(3):
        g = scratch[k]
        p = projected[k, :, columns].astype(F32)
        low = (
            taps[3 * k : 3 * k + 1] * g
            + taps[3 * k + 1 : 3 * k + 2] * shift_up(g, 1, room)
            + taps[3 * k + 2 : 3 * k + 3] * shift_up(g, 2, room)
        ).astype(BF)
        lane = (0 if group == GROUPS - 1 else group * D) + k * GROUP
        lanes = slice(lane, lane + GROUP)
        store_split(dot_at(normed[...], low), owner_rows, kept, sent, lanes)
        part = dot_bt(low, w[:, k * D + group * GROUP : k * D + (group + 1) * GROUP])
        grad_normed = part if grad_normed is None else grad_normed + part
        tap_rows.append(jnp.sum(g * p, axis=0, keepdims=True))
        for j in (1, 2):
            tap_rows.append(jnp.sum(g * shift_down(p, j, position), axis=0, keepdims=True))
    if group < GROUPS - 1:
        for i, row in enumerate(tap_rows):
            taps_out[i : i + 1, columns] = row
        total[...] = grad_normed
        return
    gain_sum = None
    for ref, out, first, count in (
        (xs, back_short, 0, short),
        (xl, back_long, short, rows - short),
    ):
        rows_of = slice(first, first + count)
        pulled, gain = norm_back(ref[...].astype(F32), small[9:10], grad_normed[rows_of])
        out[...] = grad_middle[rows_of] + pulled
        gain_sum = gain if gain_sum is None else gain_sum + gain
    row = lax.broadcasted_iota(jnp.int32, (LANES, GROUP), 0)
    for g in range(GROUPS):
        lanes = slice(g * GROUP, (g + 1) * GROUP)
        packed = jnp.where(row == 9, gain_sum[:, lanes], jnp.zeros((LANES, GROUP), F32))
        packed = jnp.where(row == 10, grad_gain_two[0:1, lanes], packed)
        for i, tap_row in enumerate(tap_rows):
            tap = tap_row if g == group else taps_before[i : i + 1, lanes]
            packed = jnp.where(row == i, tap, packed)
        packed_all = packed if g == 0 else jnp.concatenate([packed_all, packed], axis=1)
    store_split(jnp.transpose(packed_all), owner_rows, kept, sent, slice(D, D + LANES))


def output_kernel(short, first, squared, more, wdown, middle, out_short, out_long, total):
    step = pl.program_id(0)

    @pl.when(step == 0)
    def _():
        total[...] = middle[...] + dot(squared[...], wdown[...])

    @pl.when(jnp.logical_and(step > 0, step < first))
    def _():
        total[...] += dot(squared[...], wdown[...])

    @pl.when(step >= first)
    def _():
        total[...] += dot(more[...], wdown[...])

    @pl.when(step == pl.num_programs(0) - 1)
    def _():
        out_short[...] = total[:short].astype(BF)
        out_long[...] = total[short:].astype(BF)


def whole(shape):
    zeros = (0,) * len(shape)
    return pl.BlockSpec(shape, lambda i: zeros, pipeline_mode=pl.Buffered(1))


def smem():
    return pl.BlockSpec(memory_space=pltpu.SMEM)


def vmem():
    return pl.BlockSpec(memory_space=pltpu.VMEM)


def vmem_call(kernel, name, ins, out_shape, mib, weight, scratch=(), aliases=None, far=()):
    specs = [
        pl.BlockSpec(memory_space=pl.ANY) if i in far else vmem() for i in range(len(ins))
    ]
    return pl.pallas_call(
        kernel,
        in_specs=specs,
        out_specs=[vmem()] * len(out_shape),
        out_shape=out_shape,
        input_output_aliases=aliases or {},
        scratch_shapes=list(scratch),
        cost_estimate=cost(weight),
        compiler_params=pltpu.CompilerParams(vmem_limit_bytes=mib * MIB),
        name=name,
    )(*ins)


def struct(shape, dtype):
    return jax.ShapeDtypeStruct(shape, dtype)


def params(mib):
    return pltpu.CompilerParams(
        vmem_limit_bytes=mib * MIB, dimension_semantics=("arbitrary",)
    )


def cost(us):
    return pl.CostEstimate(
        flops=int(us * PEAK_PER_US * WEIGHT), bytes_accessed=0, transcendentals=0
    )


def update(grad, rate, weight, moment, average, outs, at=Ellipsis):
    moment_new = MOMENTUM * moment[at] + grad
    weight_new = weight.astype(F32) - rate * (grad + MOMENTUM * moment_new)
    outs[0][at] = grad
    outs[1][at] = moment_new
    outs[2][at] = weight_new
    outs[3][at] = AVERAGE * average[at] + (1.0 - AVERAGE) * weight_new


def total_of(pieces):
    total = pieces[0][...]
    for piece in pieces[1:]:
        total = total + piece[...].astype(F32)
    return total


def finish_kernel(kind, count, rates, *refs):
    pieces, rest = refs[:count], refs[count:]
    sets = len(rates)
    held = [rest[3 * i : 3 * i + 3] for i in range(sets)]
    outs = [rest[3 * sets + 4 * i : 3 * sets + 4 * i + 4] for i in range(sets)]
    if kind == "up":
        total = total_of(pieces)
        update(total[:, :D], rates[0], held[0][0][...], *held[0][1:], outs[0])
        update(total[:, D:], rates[1], held[1][0][...], *held[1][1:], outs[1])
    elif kind == "down":
        total = total_of(pieces)
        r = total.shape[0]
        weight = held[0][0][...].astype(F32)
        for slab in range(weight.shape[0] // r):
            at = slice(slab * r, (slab + 1) * r)
            grad = total[:, slab * D : (slab + 1) * D]
            update(grad, rates[0], weight[at], *held[0][1:], outs[0], at)
    else:
        total = total_of(pieces)
        r = total.shape[0]
        for k in range(3):
            for g in range(GROUPS):
                at = (k, slice(None), slice(g * GROUP, (g + 1) * GROUP))
                low = g * D + k * GROUP
                update(
                    total[:, low : low + GROUP], rates[0], held[0][0][at], *held[0][1:], outs[0], at
                )
        rest_rows = jnp.zeros((LANES - r, LANES), F32)
        turned = jnp.transpose(jnp.concatenate([total[:, GROUPS * D :], rest_rows], axis=0))
        for k in range(3):
            grad = turned[3 * k : 3 * k + 3, :r]
            update(grad, rates[1], held[1][0][k], *held[1][1:], outs[1], k)
        update(turned[9:11, :r], rates[2], held[2][0][...], *held[2][1:], outs[2])


def finish(kind, pieces, sets, rates, weight=1.5):
    flat = [array for one in sets for array in one]
    shapes = [one[0].shape for one in sets for _ in range(4)]
    outs = pl.pallas_call(
        functools.partial(finish_kernel, kind, len(pieces), rates),
        grid=(1,),
        in_specs=[whole(array.shape) for array in list(pieces) + flat],
        out_specs=[whole(shape) for shape in shapes],
        out_shape=[struct(shape, F32) for shape in shapes],
        cost_estimate=cost(weight),
        compiler_params=params(8),
        name="finish",
    )(*pieces, *flat)
    return [outs[4 * i : 4 * i + 4] for i in range(len(sets))]


def pack(attn_rows, conv_cols, gain_cols):
    shape = (attn_rows.shape[1], 3 * D + LANES)
    return pl.pallas_call(
        pack_kernel,
        grid=(1,),
        in_specs=[whole(array.shape) for array in (attn_rows, conv_cols, gain_cols)],
        out_specs=whole(shape),
        out_shape=struct(shape, BF),
        scratch_shapes=[pltpu.VMEM((LANES, LANES), F32)],
        cost_estimate=cost(1),
        compiler_params=params(4),
        name="pack",
    )(attn_rows, conv_cols, gain_cols)


def front(act_short, act_long, w_attn):
    short, rows = act_short.shape[0], act_short.shape[0] + act_long.shape[0]
    shapes = [
        struct((rows, D), BF),
        struct((16, D), F32),
        struct((3, rows, D), BF),
        struct((3, rows, D), BF),
        struct((rows, D), BF),
    ]
    kernel = functools.partial(front_kernel, short)
    return vmem_call(kernel, "front", [act_short, act_long, w_attn], shapes, 16, HEAVY)


def front_more(short, group, normed, small, w_attn, before):
    shapes = [struct(array.shape, array.dtype) for array in before]
    return vmem_call(
        functools.partial(front_more_kernel, short, group),
        "front_more",
        [normed, small, w_attn, *before],
        shapes,
        16,
        HEAVY if group == 1 else 1,
        aliases={3 + i: i for i in range(len(before))},
    )


def kept_again(before, first):
    specs = [pl.BlockSpec(memory_space=pl.ANY)] * len(before)
    return specs, {first + i: i for i in range(len(before))}


def up(act_short, act_long, cot_short, cot_long, len_short, len_long, attended, w_up, small, s):
    short, rows = act_short.shape[0], act_short.shape[0] + act_long.shape[0]
    ff = w_up.shape[1] - D
    tiles = ff // D
    half = D // (2 * s)
    halves = struct((tiles * half, s, D), BF)
    return pl.pallas_call(
        functools.partial(up_kernel, short, s),
        grid=(tiles // 2,),
        in_specs=[
            smem(),
            smem(),
            whole(act_short.shape),
            whole(act_long.shape),
            whole(cot_short.shape),
            whole(cot_long.shape),
            whole((rows, D)),
            pl.BlockSpec((D, D), lambda i: (0, 0)),
            pl.BlockSpec((D, D), lambda i: (0, 1 + i)),
            whole((16, D)),
        ],
        out_specs=[
            whole((rows, D)),
            whole((rows, D)),
            whole((rows, D)),
            pl.BlockSpec((rows, D), lambda i: (0, i)),
            pl.BlockSpec((half, s, D), lambda i: (i, 0, 0)),
            pl.BlockSpec((half, s, D), lambda i: (i, 0, 0)),
        ],
        out_shape=[
            struct((rows, D), F32),
            struct((rows, D), BF),
            struct((rows, D), BF),
            struct((rows, ff // 2), BF),
            halves,
            halves,
        ],
        cost_estimate=cost(HEAVY),
        compiler_params=params(12),
        name="up",
    )(
        len_short, len_long, act_short, act_long, cot_short, cot_long, attended, w_up, w_up, small
    )


def up_more(normed_two, upstream, w_up, s, before):
    rows = upstream.shape[0]
    tiles = (w_up.shape[1] - D) // D
    first = tiles // 2
    half = D // (2 * s)
    specs, aliases = kept_again(before, 3)
    return pl.pallas_call(
        functools.partial(up_more_kernel, s),
        grid=(tiles - first,),
        in_specs=[
            whole((rows, D)),
            whole((rows, D)),
            pl.BlockSpec((D, D), lambda i: (0, 1 + first + i)),
        ]
        + specs,
        out_specs=[
            pl.BlockSpec((half, s, D), lambda i: (first + i, 0, 0)),
            pl.BlockSpec((half, s, D), lambda i: (first + i, 0, 0)),
            pl.BlockSpec((rows, D), lambda i: (0, i)),
        ],
        out_shape=[struct(array.shape, array.dtype) for array in before]
        + [struct((rows, (tiles - first) * D), BF)],
        input_output_aliases=aliases,
        cost_estimate=cost(HEAVY),
        compiler_params=params(10),
        name="up_more",
    )(normed_two, upstream, w_up, *before)


def down(upstream, w_down, squared, w_up, normed_two, r):
    rows = upstream.shape[0]
    ff = w_down.shape[0]
    count = ff // D // 2
    half = D // (2 * r)
    return pl.pallas_call(
        functools.partial(down_kernel, r),
        grid=(count,),
        in_specs=[
            whole((rows, D)),
            pl.BlockSpec((D, D), lambda i: (i, 0)),
            pl.BlockSpec((rows, D), lambda i: (0, i)),
            pl.BlockSpec((D, D), lambda i: (0, 1 + i)),
            whole((rows, D)),
        ],
        out_specs=[
            pl.BlockSpec((half, r, D), lambda i: (0, 0, 1 + i)),
            pl.BlockSpec((half, r, D), lambda i: (0, 0, 1 + i)),
            whole((rows, D)),
        ],
        out_shape=[
            struct((half, r, D + ff), BF),
            struct((half, r, D + ff), BF),
            struct((rows, D), F32),
        ],
        cost_estimate=cost(HEAVY),
        compiler_params=params(15),
        name="down",
    )(upstream, w_down, squared, w_up, normed_two)


def down_more(
    upstream, w_down, squared, w_up, normed_two, attended, middle, small, r, total, before
):
    rows = upstream.shape[0]
    ff = w_down.shape[0]
    tiles = ff // D
    begun = tiles // 2
    last = tiles - begun
    half = D // (2 * r)

    def tile(i):
        return begun + jnp.minimum(i, last - 1)

    def put(i):
        return (0, 0, jnp.where(i < last, 1 + begun + i, 0))

    specs, aliases = kept_again(before, 9)
    return pl.pallas_call(
        functools.partial(down_more_kernel, last, r),
        grid=(last + 1,),
        in_specs=[
            whole((rows, D)),
            pl.BlockSpec((D, D), lambda i: (tile(i), 0)),
            pl.BlockSpec((rows, D), lambda i: (0, tile(i) - begun)),
            pl.BlockSpec((D, D), lambda i: (0, 1 + tile(i))),
            whole((rows, D)),
            whole((rows, D)),
            whole((rows, D)),
            whole((16, D)),
            whole((rows, D)),
        ]
        + specs,
        out_specs=[
            pl.BlockSpec((half, r, D), put),
            pl.BlockSpec((half, r, D), put),
            whole((rows, D)),
            whole((rows, D)),
            whole((8, D)),
        ],
        out_shape=[
            struct((half, r, D + ff), BF),
            struct((half, r, D + ff), BF),
            struct((rows, D), F32),
            struct((rows, D), BF),
            struct((8, D), F32),
        ],
        input_output_aliases=aliases,
        scratch_shapes=[pltpu.VMEM((rows, D), F32)],
        cost_estimate=cost(HEAVY),
        compiler_params=params(16),
        name="down_more",
    )(
        upstream, w_down, squared, w_up, normed_two, attended, middle, small, total, *before
    )


def mixer(
    short, r, group, mixed, projected, grad_branch, w_up, small, normed, w_attn, total=None,
    before=(), last=(),
):
    rows = grad_branch.shape[0]
    half = D // (2 * r)
    ins = [mixed, projected, grad_branch, w_up, small, normed, w_attn]
    if group > 0:
        ins = ins + [total]
    aliases = {}
    if group < GROUPS - 1:
        aliases = {len(ins) + i: i for i in range(len(before))}
        ins = ins + list(before)
        part = struct((half, r, (GROUPS - 1) * D), BF)
        out_shape = [part, part, struct((16, D), F32), struct((rows, D), F32)]
    else:
        act_short, act_long = last[:2]
        ins = ins + list(last)
        part = struct((half, r, D + LANES), BF)
        out_shape = [part, part, struct(act_short.shape, F32), struct(act_long.shape, F32)]
    return vmem_call(
        functools.partial(mixer_kernel, short, r, group),
        "mixer",
        ins,
        out_shape,
        16,
        2 if group == 1 else HEAVY,
        scratch=[
            pltpu.VMEM((3, rows, GROUP), F32),
            pltpu.VMEM((GROUP, D), BF),
            pltpu.SemaphoreType.DMA,
        ],
        aliases=aliases,
        far=(3,),
    )


def output(act_short, act_long, squared, more, w_down, middle):
    short, rows = act_short.shape[0], middle.shape[0]
    ff = w_down.shape[0]
    first = squared.shape[1] // D
    return pl.pallas_call(
        functools.partial(output_kernel, short, first),
        grid=(ff // D,),
        in_specs=[
            pl.BlockSpec((rows, D), lambda i: (0, jnp.minimum(i, first - 1))),
            pl.BlockSpec((rows, D), lambda i: (0, jnp.maximum(i - first, 0))),
            pl.BlockSpec((D, D), lambda i: (i, 0)),
            whole((rows, D)),
        ],
        out_specs=[whole(act_short.shape), whole(act_long.shape)],
        out_shape=[struct(act_short.shape, BF), struct(act_long.shape, BF)],
        scratch_shapes=[pltpu.VMEM((rows, D), F32)],
        cost_estimate=cost(HEAVY),
        compiler_params=params(12),
        name="output",
    )(squared, more, w_down, middle)


def shards(grid, *args):
    act_short, act_long, cot_short, cot_long, len_short, len_long = args[:6]
    owned = args[6:12]
    moments = args[12:18]
    averages = args[18:24]
    attn_rows, conv_cols, out_rows, up_rows, down_rows, gain_cols = owned
    r = out_rows.shape[0]
    s = down_rows.shape[0]
    short = act_short.shape[0]
    rows = short + act_long.shape[0]

    chunk_attn = pack(attn_rows, conv_cols, gain_cols)
    parts = s // r
    chunk_up = jnp.concatenate([out_rows, up_rows], axis=1)
    chunk_down = jnp.concatenate([down_rows[i * r : (i + 1) * r] for i in range(parts)], axis=1)
    wide, wide_up, wide_down = chunk_attn.shape[1], chunk_up.shape[1], chunk_down.shape[1]
    over_a, over_x, over_z = a_moves(grid), x_moves(grid), z_moves(grid)

    pieces = exchange(chunk_attn, over_z)
    (col_attn,) = place_z(grid, pieces, [(0, wide)])
    pieces_attn = exchange(col_attn, both_moves(grid))
    pieces_up = exchange(after(chunk_up, col_attn), over_z)
    plane_attn = place_both(grid, held_back(pieces_attn, *pieces_up[1:]))
    other_attn = swap(grid, plane_attn)
    up_low, up_high = halves(grid, held_back(pieces_up, plane_attn), wide_up)
    up_low, up_high = exchange(up_low, over_a), exchange(up_high, over_x)
    w_attn = join(grid, plane_attn, other_attn, wide)
    normed, small, *begun = front(act_short, act_long, w_attn)
    pieces_down = exchange(after(chunk_down, normed), over_z)
    up_low, up_high = place_first(grid, held_back(up_low, normed), held_back(up_high, normed))
    up_low, up_high = exchange(up_low, over_x), exchange(up_high, over_a)
    begun = front_more(short, 1, after(normed, up_low[0]), small, w_attn, begun)
    down_low, down_high = halves(grid, held_back(pieces_down, begun[2]), wide_down)
    down_low, down_high = exchange(down_low, over_a), exchange(down_high, over_x)
    projected, mixed, attended = front_more(
        short, 2, after(normed, down_low[0]), small, w_attn, begun
    )
    down_low, down_high = place_first(
        grid, held_back(down_low, attended), held_back(down_high, attended)
    )
    plane_up = place_second(
        grid, held_back(up_low, attended, down_low), held_back(up_high, attended, down_low)
    )
    other_up = swap(grid, plane_up)
    down_low, down_high = exchange(after(down_low, plane_up), over_x), exchange(down_high, over_a)
    w_up = join(grid, plane_up, after(other_up, down_low[0]), wide_up)
    middle, normed_two, upstream, squared, *begun = up(
        act_short, act_long, cot_short, cot_long, len_short, len_long, attended, w_up, small, s
    )
    plane_down = place_second(
        grid, held_back(down_low, normed_two), held_back(down_high, normed_two)
    )
    other_down = swap(grid, plane_down)
    kept_down, sent_down, more = up_more(
        after(normed_two, plane_down), upstream, w_up, s, begun
    )
    w_down = join(grid, plane_down, after(other_down, more), D)

    sent_down = swap(grid, sent_down)
    *begun, total = down(upstream, w_down, squared, w_up, normed_two, r)
    low_down, high_down = add_core(grid, kept_down, after(sent_down, total), D // 2)
    kept_up, sent_up, grad_middle, grad_branch, grad_gain_two = down_more(
        after(upstream, low_down[0]), w_down, more, w_up, normed_two, attended, middle, small,
        r, total, begun,
    )
    sent_up = swap(grid, sent_up)
    low_down, high_down = add_plane(
        grid, held_back(low_down, grad_branch), held_back(high_down, grad_branch)
    )
    low_up, high_up = add_core(grid, kept_up, after(sent_up, low_down[0]), wide_up // 2)
    shared = (mixed, projected, grad_branch, w_up, small, normed, w_attn)
    *begun, total = mixer(
        short, r, 0, mixed, projected, after(grad_branch, low_up[0]), *shared[3:]
    )
    pieces_down = add_z(
        grid, r, [(held_back(low_down, total), held_back(high_down, total))]
    )
    kept_a, sent_a, grad_taps, total = mixer(
        short, r, 1, *shared, total=after(total, pieces_down[0]), before=begun
    )
    sent_a = swap(grid, sent_a)
    pieces_down = held_back(pieces_down, total)
    low_up, high_up = add_plane(
        grid, held_back(low_up, *pieces_down[1:]), held_back(high_up, *pieces_down[1:])
    )
    pieces_a = add_both(grid, kept_a, after(sent_a, low_up[0]))
    kept_b, sent_b, back_short, back_long = mixer(
        short, r, 2, *shared, total=after(total, pieces_a[0]),
        last=(act_short, act_long, grad_middle, grad_taps, grad_gain_two),
    )
    low_up, high_up = held_back(low_up, back_short), held_back(high_up, back_short)
    sent_b = swap(grid, after(sent_b, *low_up[1:], *high_up[1:]))
    pieces_a = held_back(pieces_a, back_short)
    scale_tokens = math.sqrt(rows * grid.a * grid.f)
    rates = [rate / scale_tokens for rate in RATES]
    sets = list(zip(owned, moments, averages))
    pieces_down[0] = after(pieces_down[0], back_short, *pieces_a[1:], *low_up[1:], *high_up[1:])
    (done_down,) = finish("down", pieces_down, sets[4:5], rates[4:5], HEAVY)
    pieces_b = add_both(grid, kept_b, after(sent_b, done_down[0]))
    pieces_up = add_z(grid, r, [(held_back(low_up, pieces_b[0]), high_up)])
    out_short, out_long = output(
        act_short, act_long, squared, more, w_down, after(middle, pieces_b[0], pieces_up[0])
    )
    pieces_attn = add_z(grid, r, [(pieces_a,), (held_back(pieces_b, out_short),)])
    pieces_up = held_back(pieces_up, pieces_attn[0])
    done_out, done_up = finish("up", pieces_up, sets[2:4], rates[2:4])
    done_attn, done_taps, done_gains = finish(
        "attn", pieces_attn, [sets[0], sets[1], sets[5]], [rates[0], rates[1], rates[5]]
    )
    results = [out_short, out_long, back_short, back_long]
    for done in (done_attn, done_taps, done_out, done_up, done_down, done_gains):
        results.extend(done)
    return tuple(results)


def solution(mesh):
    rows = P(AXES, None)
    weights = [P(None, AXES, None), P(None, None, AXES), rows, rows, rows, P(None, AXES)]
    in_specs = tuple([rows] * 4 + [P(AXES)] * 2 + weights * 3)
    out_specs = tuple([rows] * 4 + [spec for spec in weights for _ in range(4)])
    grid = Grid(mesh)

    def program(*args):
        return shards(grid, *args)

    return jax.shard_map(
        program, mesh=mesh, in_specs=in_specs, out_specs=out_specs, check_vma=False
    )
```

```python
import functools
import math

import jax
import jax.numpy as jnp
from jax import lax
from jax.experimental import pallas as pl
from jax.experimental.pallas import tpu as pltpu
from jax.sharding import PartitionSpec as P

D = 768
HEAD_DIM = 64
GROUP = 256
GROUPS = D // GROUP
BLOCK = 256
LANES = 128

EPS = 1e-06
MOMENTUM = 0.9
AVERAGE = 0.5
RATES = (0.03, 0.5, 0.6, 0.025, 0.007, 0.05)
NEG = -1e30
HEAD_SCALE = 0.125
AXES = ("dp", "fsdp")
BF = jnp.bfloat16
F32 = jnp.float32
MIB = 1024 * 1024
PEAK_PER_US = 1.15e9
WEIGHT = 1.0
HEAVY = 100


class Grid:
    def __init__(self, mesh):
        self.a = mesh.shape["dp"]
        self.f = mesh.shape["fsdp"]
        self.x = 2
        self.z = self.f // 4

    def index(self, a, z, x, c):
        return a * self.f + (z * self.x + x) * 2 + c

    def perm(self, move):
        pairs = []
        for a in range(self.a):
            for z in range(self.z):
                for x in range(self.x):
                    for c in range(2):
                        pairs.append((self.index(a, z, x, c), self.index(*move(a, z, x, c))))
        return pairs

    def swap_core(self):
        return self.perm(lambda a, z, x, c: (a, z, x, 1 - c))

    def shift_plane(self, da, dx):
        return self.perm(lambda a, z, x, c: ((a + da) % self.a, z, (x + dx) % self.x, c))

    def shift_z(self, dz):
        return self.perm(lambda a, z, x, c: (a, (z + dz) % self.z, x, c))

    def flip_z(self, bit):
        return self.perm(lambda a, z, x, c: (a, z ^ bit, x, c))

    def z_bits(self):
        bits, bit = [], 1
        while bit < self.z:
            bits.append(bit)
            bit *= 2
        return bits

    def here(self):
        f = lax.axis_index("fsdp")
        return lax.axis_index("dp"), f // 4, (f // 2) % 2, f % 2

    def plane_moves(self):
        return [(da, dx) for da in range(self.a) for dx in range(self.x) if da or dx]


def after(value, *others):
    return lax.optimization_barrier((value,) + others)[0]


def relay_kernel(grid, body, count, *refs):
    body(grid.here(), refs[:count], refs[count:])


def along(shape, axis):
    if axis is None:
        return pl.BlockSpec(shape, lambda i: (0,) * len(shape))
    block = tuple(1 if j == axis else size for j, size in enumerate(shape))
    return pl.BlockSpec(block, lambda i: tuple(i if j == axis else 0 for j in range(len(shape))))


def relay(grid, name, body, steps, ins, outs, weight=1):
    return pl.pallas_call(
        functools.partial(relay_kernel, grid, body, len(ins)),
        grid=(steps,),
        in_specs=[along(array.shape, axis) for array, axis in ins],
        out_specs=[along(shape, axis) for shape, _, axis in outs],
        out_shape=[jax.ShapeDtypeStruct(shape, kind) for shape, kind, _ in outs],
        cost_estimate=cost(weight),
        compiler_params=params(8),
        name=name,
    )(*[array for array, _ in ins])


def z_moves(grid):
    return [
        (
            grid.shift_z(dz),
            lambda a, z, x, c, dz=dz: ((z + dz) % grid.z,),
            lambda a, z, x, c, dz=dz: ((z - dz) % grid.z,),
        )
        for dz in range(1, grid.z)
    ]


def a_moves(grid):
    return [
        (
            grid.shift_plane(da, 0),
            lambda a, z, x, c, da=da: ((a + da) % grid.a,),
            lambda a, z, x, c, da=da: ((a - da) % grid.a,),
        )
        for da in range(1, grid.a)
    ]


def x_moves(grid):
    return [
        (
            grid.shift_plane(0, 1),
            lambda a, z, x, c: (1 - x,),
            lambda a, z, x, c: (1 - x,),
        )
    ]


def both_moves(grid):
    return [
        (
            grid.shift_plane(da, dx),
            lambda a, z, x, c, da=da, dx=dx: ((a + da) % grid.a, (x + dx) % grid.x),
            lambda a, z, x, c, da=da, dx=dx: ((a - da) % grid.a, (x - dx) % grid.x),
        )
        for da, dx in grid.plane_moves()
    ]


OWN_Z = lambda a, z, x, c: (z,)
OWN_A = lambda a, z, x, c: (a,)
OWN_X = lambda a, z, x, c: (x,)
OWN_AX = lambda a, z, x, c: (a, x)


def exchange(value, moves):
    return [value] + [lax.ppermute(value, AXES, pairs) for pairs, _, _ in moves]


def send(parts, moves):
    return [parts[0]] + [
        lax.ppermute(part, AXES, pairs) for part, (pairs, _, _) in zip(parts[1:], moves)
    ]


def swap(grid, value):
    return lax.ppermute(value, AXES, grid.swap_core())


def arrived(own, moves):
    return [own] + [brought for _, _, brought in moves]


def leaving(own, moves):
    return [own] + [sent for _, sent, _ in moves]


def held_back(pieces, *others):
    return [pieces[0]] + [after(piece, *others) for piece in pieces[1:]]


def place_z(grid, pieces, cuts):
    spots = arrived(OWN_Z, z_moves(grid))
    r = pieces[0].shape[0]

    def body(here, ins, outs):
        for piece, spot in zip(ins, spots):
            at = spot(*here)[0]
            for out, (low, high) in zip(outs, cuts):
                out[at] = piece[:, low:high]

    outs = [((grid.z, r, high - low), BF, None) for low, high in cuts]
    return relay(grid, "place_z", body, 1, [(piece, None) for piece in pieces], outs)


def flip(grid, value, bit):
    return lax.ppermute(value, AXES, grid.flip_z(bit))


def halves(grid, pieces, width):
    return place_z(grid, pieces, [(0, width // 2), (width // 2, width)])


def place_both(grid, pieces):
    spots = arrived(OWN_AX, both_moves(grid))

    def body(here, ins, outs):
        for piece, spot in zip(ins, spots):
            ia, ix = spot(*here)
            outs[0][ia, 0, ix] = piece[0]

    z, r, n = pieces[0].shape
    outs = [((grid.a, z, grid.x, r, n), BF, 1)]
    return relay(grid, "place_both", body, z, [(piece, 0) for piece in pieces], outs)[0]


def place_first(grid, over_a, over_x, weight=1):
    a_spots = arrived(OWN_A, a_moves(grid))
    x_spots = arrived(OWN_X, x_moves(grid))

    def body(here, ins, outs):
        for piece, spot in zip(ins, a_spots):
            outs[0][spot(*here)[0], 0] = piece[0]
        for piece, spot in zip(ins[len(a_spots) :], x_spots):
            outs[1][0, spot(*here)[0]] = piece[0]

    z, r, n = over_a[0].shape
    m = over_x[0].shape[-1]
    ins = [(piece, 0) for piece in over_a + over_x]
    outs = [((grid.a, z, r, n), BF, 1), ((z, grid.x, r, m), BF, 0)]
    return relay(grid, "place_first", body, z, ins, outs, weight)


def place_second(grid, over_x, over_a):
    x_spots = arrived(OWN_X, x_moves(grid))
    a_spots = arrived(OWN_A, a_moves(grid))
    z, r, n = over_x[0].shape[1:]
    m = over_a[0].shape[-1]

    def body(here, ins, outs):
        for piece, spot in zip(ins, x_spots):
            for ia in range(grid.a):
                outs[0][ia, 0, spot(*here)[0], :, :n] = piece[ia, 0]
        for piece, spot in zip(ins[len(x_spots) :], a_spots):
            for ix in range(grid.x):
                outs[0][spot(*here)[0], 0, ix, :, n:] = piece[0, ix]

    ins = [(piece, 1) for piece in over_x] + [(piece, 0) for piece in over_a]
    outs = [((grid.a, z, grid.x, r, n + m), BF, 1)]
    return relay(grid, "place_second", body, z, ins, outs)[0]


def join(grid, plane, other, width):
    r, n = plane.shape[-2:]
    parts = n // width
    owners = grid.a * grid.x

    def body(here, ins, outs):
        core = here[3]
        for source, at in ((ins[0], core), (ins[1], 1 - core)):
            for i in range(owners):
                for part in range(parts):
                    outs[0][0, i, at, part] = source[0, i, :, part * width : (part + 1) * width]

    plane, other = (
        array.reshape(grid.z, owners, r, n) for array in (plane, other)
    )
    outs = [((grid.z, owners, 2, parts, r, width), BF, 0)]
    (whole_array,) = relay(grid, "join", body, grid.z, [(plane, 0), (other, 0)], outs)
    return whole_array.reshape(-1, width)


def add_at(pieces, where):
    total = pieces[0][where].astype(F32)
    for piece in pieces[1:]:
        total = total + piece[where].astype(F32)
    return total


def add_core(grid, kept, got, cut):
    a_spots = leaving(OWN_A, a_moves(grid))
    x_spots = leaving(OWN_X, x_moves(grid))
    shape = (grid.a, grid.z, grid.x) + kept.shape[-2:]
    kept, got = kept.reshape(shape), got.reshape(shape)
    r, n = shape[-2:]
    low, high = slice(0, cut), slice(cut, n)

    def body(here, ins, outs):
        for out, spot in zip(outs, a_spots):
            for ix in range(grid.x):
                out[0, ix] = add_at(ins, (spot(*here)[0], 0, ix, slice(None), low)).astype(BF)
        for out, spot in zip(outs[len(a_spots) :], x_spots):
            for ia in range(grid.a):
                out[ia, 0] = add_at(ins, (ia, 0, spot(*here)[0], slice(None), high)).astype(BF)

    outs = [((grid.z, grid.x, r, cut), BF, 0)] * len(a_spots)
    outs += [((grid.a, grid.z, r, n - cut), BF, 1)] * len(x_spots)
    parts = relay(grid, "add_core", body, grid.z, [(kept, 1), (got, 1)], outs)
    return (
        send(parts[: len(a_spots)], a_moves(grid)),
        send(parts[len(a_spots) :], x_moves(grid)),
    )


def add_plane(grid, low, high):
    x_spots = leaving(OWN_X, x_moves(grid))
    a_spots = leaving(OWN_A, a_moves(grid))
    z, _, r, n = low[0].shape
    m = high[0].shape[-1]

    def body(here, ins, outs):
        for out, spot in zip(outs, x_spots):
            out[0] = add_at(ins[: len(low)], (0, spot(*here)[0])).astype(BF)
        for out, spot in zip(outs[len(x_spots) :], a_spots):
            out[0] = add_at(ins[len(low) :], (spot(*here)[0], 0)).astype(BF)

    ins = [(piece, 0) for piece in low] + [(piece, 1) for piece in high]
    outs = [((z, r, n), BF, 0)] * len(x_spots) + [((z, r, m), BF, 0)] * len(a_spots)
    parts = relay(grid, "add_plane", body, z, ins, outs, HEAVY)
    return (
        send(parts[: len(x_spots)], x_moves(grid)),
        send(parts[len(x_spots) :], a_moves(grid)),
    )


def add_both(grid, kept, got, weight=1):
    spots = leaving(OWN_AX, both_moves(grid))
    shape = (grid.a, grid.z, grid.x) + kept.shape[-2:]

    def body(here, ins, outs):
        for out, spot in zip(outs, spots):
            ia, ix = spot(*here)
            out[0] = add_at(ins, (ia, 0, ix)).astype(BF)

    ins = [(kept.reshape(shape), 1), (got.reshape(shape), 1)]
    outs = [((grid.z,) + shape[-2:], BF, 0)] * len(spots)
    return send(relay(grid, "add_both", body, grid.z, ins, outs, weight), both_moves(grid))


def add_z(grid, r, parts):
    lanes, end = [], 0
    for part in parts:
        widths = [half[0].shape[-1] for half in part]
        lanes.append((end, widths))
        end += sum(widths) * (part[0][0].shape[1] // r)
    count = grid.z // 2

    def body(here, ins, outs):
        mine = here[1] % 2
        for out, bit in ((outs[0], mine), (outs[1], 1 - mine)):
            for place in range(count):
                at, first = 2 * place + bit, 0
                for part, (start, widths) in zip(parts, lanes):
                    for i, half in enumerate(part):
                        total = add_at(ins[first : first + len(half)], at)
                        for slab in range(total.shape[0] // r):
                            low = start + slab * sum(widths) + sum(widths[:i])
                            piece = total[slab * r : (slab + 1) * r]
                            out[place, :, low : low + widths[i]] = piece.astype(BF)
                        first += len(half)

    ins = [(piece, None) for part in parts for half in part for piece in half]
    outs = [((count, r, end), BF, None)] * 2
    kept, sent = relay(grid, "add_z", body, 1, ins, outs)
    return [kept, flip(grid, sent, 1)]


def add_rest(grid, pieces):
    for bit in grid.z_bits()[1:]:
        count, r, n = pieces[0].shape
        last = count == 2

        def body(here, ins, outs):
            mine = (here[1] // bit) % 2
            for out, at in ((outs[0], mine), (outs[1], 1 - mine)):
                for place in range(count // 2):
                    where = Ellipsis if last else place
                    out[where] = add_at(ins, 2 * place + at).astype(out.dtype)

        shape = (r, n) if last else (count // 2, r, n)
        outs = [(shape, F32 if last else BF, None), (shape, BF, None)]
        kept, sent = relay(grid, "add_rest", body, 1, [(piece, None) for piece in pieces], outs)
        pieces = [kept, flip(grid, sent, bit)]
    return pieces


def dot(left, right):
    return lax.dot_general(left, right, (((1,), (0,)), ((), ())), preferred_element_type=F32)


def dot_bt(left, right):
    return lax.dot_general(left, right, (((1,), (1,)), ((), ())), preferred_element_type=F32)


def dot_at(left, right):
    return lax.dot_general(left, right, (((0,), (0,)), ((), ())), preferred_element_type=F32)


def rms_scale(values):
    return lax.rsqrt(jnp.mean(values * values, axis=-1, keepdims=True) + EPS)


def norm_back(values, gain, grad):
    scale = rms_scale(values)
    scaled = grad * gain
    inner = jnp.mean(scaled * values, axis=-1, keepdims=True)
    grad_gain = jnp.sum(grad * (values * scale), axis=0, keepdims=True)
    return scale * scaled - values * (scale * scale * scale * inner), grad_gain


def positions_of(rows, short, width):
    row = lax.broadcasted_iota(jnp.int32, (rows, width), 0)
    return jnp.where(row < short, row, row - short), row < short


def shift_down(values, offset, position):
    return jnp.where(position >= offset, pltpu.roll(values, offset, 0), 0.0)


def shift_up(values, offset, room):
    rows = values.shape[0]
    return jnp.where(room >= offset, pltpu.roll(values, rows - offset, 0), 0.0)


def head_mask(half):
    lane = lax.broadcasted_iota(jnp.int32, (1, LANES), 1)
    return (lane // HEAD_DIM) == half


def blocks_of(rows, short):
    found = []
    for start, length in ((0, short), (short, rows - short)):
        for block in range(length // BLOCK):
            found.append((start + block * BLOCK, start, (block + 1) * BLOCK))
    return found


def store_split(value, owner_rows, kept, sent, lanes=slice(None)):
    first = lax.axis_index("fsdp") % 2 == 0
    for pair in range(value.shape[0] // (2 * owner_rows)):
        at = 2 * pair * owner_rows
        even, odd = value[at : at + owner_rows], value[at + owner_rows : at + 2 * owner_rows]
        kept[pair, :, lanes] = jnp.where(first, even, odd).astype(BF)
        sent[pair, :, lanes] = jnp.where(first, odd, even).astype(BF)


def _():
            for pair in range(value.shape[0] // (2 * owner_rows)):
                at = 2 * pair * owner_rows
                first[pair, :, lanes] = value[at : at + owner_rows].astype(BF)
                second[pair, :, lanes] = value[at + owner_rows : at + 2 * owner_rows].astype(BF)


def front_kernel(short, xs, xl, w, normed, small, *refs):
    rows = normed.shape[0]
    turned = jnp.transpose(w[:, 3 * D : 3 * D + LANES].astype(F32))[:16]
    small[...] = turned
    gain = turned[9:10]
    for ref, first, count in ((xs, 0, short), (xl, short, rows - short)):
        x = ref[...].astype(F32)
        normed[first : first + count] = (x * rms_scale(x) * gain).astype(BF)
    front_group(short, 0, normed, small, w, *refs)


def front_more_kernel(short, group, normed, small, w, *refs):
    front_group(short, group, normed, small, w, *refs[-3:])


def front_group(short, group, normed, small, w, projected, mixed, attended):
    rows = normed.shape[0]
    columns = slice(group * GROUP, (group + 1) * GROUP)
    taps = small[:, columns]
    position, _ = positions_of(rows, short, GROUP)
    base = normed[...]
    for k in range(3):
        p = dot(base, w[:, k * D + group * GROUP : k * D + (group + 1) * GROUP])
        projected[k, :, columns] = p.astype(BF)
        mixed[k, :, columns] = (
            taps[3 * k : 3 * k + 1] * p
            + taps[3 * k + 1 : 3 * k + 2] * shift_down(p, 1, position)
            + taps[3 * k + 2 : 3 * k + 3] * shift_down(p, 2, position)
        ).astype(BF)
    for pair in range(GROUP // LANES):
        lane = group * GROUP + pair * LANES
        lanes = slice(lane, lane + LANES)
        for first, key_first, key_count in blocks_of(rows, short):
            queries = mixed[0, first : first + BLOCK, lanes]
            keys = mixed[1, key_first : key_first + key_count, lanes]
            values = mixed[2, key_first : key_first + key_count, lanes]
            row = lax.broadcasted_iota(jnp.int32, (BLOCK, key_count), 0) + (first - key_first)
            causal = lax.broadcasted_iota(jnp.int32, (BLOCK, key_count), 1) <= row
            total = None
            for half in range(2):
                scale = jnp.where(head_mask(half), HEAD_SCALE, 0.0).astype(BF)
                keep = jnp.where(head_mask(half), 1.0, 0.0).astype(BF)
                scores = jnp.where(causal, dot_bt(queries * scale, keys), NEG)
                peak = jnp.max(scores, axis=-1, keepdims=True)
                exponent = jnp.exp(scores - peak)
                weights = exponent * (1.0 / jnp.sum(exponent, axis=-1, keepdims=True))
                part = dot(weights.astype(BF), values * keep)
                total = part if total is None else total + part
            attended[first : first + BLOCK, lanes] = total.astype(BF)


def pack_kernel(attn, taps, gains, out, scratch):
    r = attn.shape[1]
    scratch[...] = jnp.zeros_like(scratch)
    for k in range(3):
        out[:, k * D : (k + 1) * D] = attn[k]
        scratch[3 * k : 3 * k + 3, :r] = taps[k].astype(F32)
    scratch[9:11, :r] = gains[...].astype(F32)
    out[:, 3 * D :] = jnp.transpose(scratch[...])[:r].astype(BF)


def up_tile(owner_rows, normed, upstream, wup, squared, kept, sent):
    hidden = jnp.maximum(dot(normed[...], wup[...]), 0.0)
    low = (hidden * hidden).astype(BF)
    squared[...] = low
    store_split(dot_at(low, upstream[...]), owner_rows, kept, sent)


def up_kernel(
    short, owner_rows, ls, ll, xs, xl, cs, cl, attended, wout, wup, small,
    middle, normed, upstream, squared, kept, sent,
):
    step = pl.program_id(0)
    rows = normed.shape[0]

    @pl.when(step == 0)
    def _():
        gain = small[10:11]
        branch = dot(attended[...], wout[...])
        for ref, cot, limit, first, count in (
            (xs, cs, ls, 0, short),
            (xl, cl, ll, short, rows - short),
        ):
            part = slice(first, first + count)
            mid = ref[...].astype(F32) + branch[part]
            middle[part] = mid
            normed[part] = (mid * rms_scale(mid) * gain).astype(BF)
            position = lax.broadcasted_iota(jnp.int32, (count, D), 0)
            wide = jnp.where(position < limit[0], cot[...].astype(F32), 0.0)
            upstream[part] = wide.astype(BF)

    up_tile(owner_rows, normed, upstream, wup, squared, kept, sent)


def up_more_kernel(owner_rows, normed, upstream, wup, *refs):
    kept, sent, squared = refs[-3:]
    up_tile(owner_rows, normed, upstream, wup, squared, kept, sent)


def down_tile(owner_rows, upstream, wdown, squared, wup, normed, kept, sent, total, first):
    grad_squared = dot_bt(upstream[...], wdown[...])
    active = jnp.sqrt(squared[...].astype(F32))
    grad_hidden = (grad_squared * (2.0 * active)).astype(BF)
    store_split(dot_at(normed[...], grad_hidden), owner_rows, kept, sent)
    part = dot_bt(grad_hidden, wup[...])

    @pl.when(first)
    def _():
        total[...] = part

    @pl.when(jnp.logical_not(first))
    def _():
        total[...] += part


def down_kernel(owner_rows, upstream, wdown, squared, wup, normed, kept, sent, total):
    first = pl.program_id(0) == 0
    down_tile(owner_rows, upstream, wdown, squared, wup, normed, kept, sent, total, first)


def down_more_kernel(
    last, owner_rows, upstream, wdown, squared, wup, normed, attended, middle, small, before,
    *refs
):
    kept, sent, grad_middle, grad_branch, grad_gain, total = refs[-6:]
    step = pl.program_id(0)

    @pl.when(step == 0)
    def _():
        total[...] = before[...]

    @pl.when(step < last)
    def _():
        down_tile(owner_rows, upstream, wdown, squared, wup, normed, kept, sent, total, step < 0)

    @pl.when(step == last)
    def _():
        pulled, gain = norm_back(middle[...], small[10:11], total[...])
        grad_gain[...] = jnp.broadcast_to(gain, grad_gain.shape)
        wide = upstream[...].astype(F32) + pulled
        grad_middle[...] = wide
        low = wide.astype(BF)
        grad_branch[...] = low
        store_split(dot_at(attended[...], low), owner_rows, kept, sent)


def mixer_kernel(
    short, owner_rows, group, mixed, projected, branch, w_up, small, normed, w, *refs
):
    scratch, w_out, ready = refs[-3:]
    refs = refs[:-2]
    columns = slice(group * GROUP, (group + 1) * GROUP)
    fetch = pltpu.make_async_copy(w_up.at[columns, :D], w_out, ready)
    fetch.start()
    if group == 0:
        before = None
    else:
        before, refs = refs[0], refs[1:]
    if group < GROUPS - 1:
        kept, sent, taps_out, total = refs[-5:-1]
    else:
        xs, xl, grad_middle, taps_before, grad_gain_two = refs[:5]
        kept, sent, back_short, back_long = refs[-5:-1]
    rows = branch.shape[0]
    fetch.wait()
    grad_attended = dot_bt(branch[...], w_out[...]).astype(BF)
    for pair in range(GROUP // LANES):
        lanes = slice(pair * LANES, (pair + 1) * LANES)
        lane = group * GROUP + pair * LANES
        far = slice(lane, lane + LANES)
        started = set()
        for first, key_first, key_count in blocks_of(rows, short):
            block = slice(first, first + BLOCK)
            spread = slice(key_first, key_first + key_count)
            queries = mixed[0, block, far]
            keys = mixed[1, spread, far]
            values = mixed[2, spread, far]
            grads = grad_attended[block, lanes]
            row = lax.broadcasted_iota(jnp.int32, (key_count, BLOCK), 1) + (first - key_first)
            causal = lax.broadcasted_iota(jnp.int32, (key_count, BLOCK), 0) <= row
            for_queries = for_keys = for_values = None
            for half in range(2):
                scale = jnp.where(head_mask(half), HEAD_SCALE, 0.0).astype(BF)
                keep = jnp.where(head_mask(half), 1.0, 0.0).astype(BF)
                scaled = queries * scale
                own = grads * keep
                scores = jnp.where(causal, dot_bt(keys, scaled), NEG)
                peak = jnp.max(scores, axis=0, keepdims=True)
                exponent = jnp.exp(scores - peak)
                probs = exponent * (1.0 / jnp.sum(exponent, axis=0, keepdims=True))
                grad_probs = dot_bt(values, own)
                inner = jnp.sum(probs * grad_probs, axis=0, keepdims=True)
                grad_scores = (probs * (grad_probs - inner)).astype(BF)
                to_values = dot(probs.astype(BF), own)
                to_keys = dot(grad_scores, scaled)
                to_queries = dot_at(grad_scores, keys * scale)
                if half == 0:
                    for_queries, for_keys, for_values = to_queries, to_keys, to_values
                else:
                    for_queries = for_queries + to_queries
                    for_keys = for_keys + to_keys
                    for_values = for_values + to_values
            scratch[0, block, lanes] = for_queries
            for block_key in range(key_count // BLOCK):
                at = key_first + block_key * BLOCK
                inside = slice(block_key * BLOCK, (block_key + 1) * BLOCK)
                if at in started:
                    scratch[1, at : at + BLOCK, lanes] += for_keys[inside]
                    scratch[2, at : at + BLOCK, lanes] += for_values[inside]
                else:
                    started.add(at)
                    scratch[1, at : at + BLOCK, lanes] = for_keys[inside]
                    scratch[2, at : at + BLOCK, lanes] = for_values[inside]
    position, in_short = positions_of(rows, short, GROUP)
    room = jnp.where(in_short, short, rows - short) - 1 - position
    taps = small[:, columns]
    tap_rows = []
    grad_normed = None if before is None else before[...]
    for k in range(3):
        g = scratch[k]
        p = projected[k, :, columns].astype(F32)
        low = (
            taps[3 * k : 3 * k + 1] * g
            + taps[3 * k + 1 : 3 * k + 2] * shift_up(g, 1, room)
            + taps[3 * k + 2 : 3 * k + 3] * shift_up(g, 2, room)
        ).astype(BF)
        lane = (0 if group == GROUPS - 1 else group * D) + k * GROUP
        lanes = slice(lane, lane + GROUP)
        store_split(dot_at(normed[...], low), owner_rows, kept, sent, lanes)
        part = dot_bt(low, w[:, k * D + group * GROUP : k * D + (group + 1) * GROUP])
        grad_normed = part if grad_normed is None else grad_normed + part
        tap_rows.append(jnp.sum(g * p, axis=0, keepdims=True))
        for j in (1, 2):
            tap_rows.append(jnp.sum(g * shift_down(p, j, position), axis=0, keepdims=True))
    if group < GROUPS - 1:
        for i, row in enumerate(tap_rows):
            taps_out[i : i + 1, columns] = row
        total[...] = grad_normed
        return
    gain_sum = None
    for ref, out, first, count in (
        (xs, back_short, 0, short),
        (xl, back_long, short, rows - short),
    ):
        rows_of = slice(first, first + count)
        pulled, gain = norm_back(ref[...].astype(F32), small[9:10], grad_normed[rows_of])
        out[...] = grad_middle[rows_of] + pulled
        gain_sum = gain if gain_sum is None else gain_sum + gain
    row = lax.broadcasted_iota(jnp.int32, (LANES, GROUP), 0)
    for g in range(GROUPS):
        lanes = slice(g * GROUP, (g + 1) * GROUP)
        packed = jnp.where(row == 9, gain_sum[:, lanes], jnp.zeros((LANES, GROUP), F32))
        packed = jnp.where(row == 10, grad_gain_two[0:1, lanes], packed)
        for i, tap_row in enumerate(tap_rows):
            tap = tap_row if g == group else taps_before[i : i + 1, lanes]
            packed = jnp.where(row == i, tap, packed)
        packed_all = packed if g == 0 else jnp.concatenate([packed_all, packed], axis=1)
    store_split(jnp.transpose(packed_all), owner_rows, kept, sent, slice(D, D + LANES))


def output_kernel(short, first, squared, more, wdown, middle, out_short, out_long, total):
    step = pl.program_id(0)

    @pl.when(step == 0)
    def _():
        total[...] = middle[...] + dot(squared[...], wdown[...])

    @pl.when(jnp.logical_and(step > 0, step < first))
    def _():
        total[...] += dot(squared[...], wdown[...])

    @pl.when(step >= first)
    def _():
        total[...] += dot(more[...], wdown[...])

    @pl.when(step == pl.num_programs(0) - 1)
    def _():
        out_short[...] = total[:short].astype(BF)
        out_long[...] = total[short:].astype(BF)


def whole(shape):
    zeros = (0,) * len(shape)
    return pl.BlockSpec(shape, lambda i: zeros, pipeline_mode=pl.Buffered(1))


def smem():
    return pl.BlockSpec(memory_space=pltpu.SMEM)


def vmem():
    return pl.BlockSpec(memory_space=pltpu.VMEM)


def vmem_call(kernel, name, ins, out_shape, mib, weight, scratch=(), aliases=None, far=()):
    specs = [
        pl.BlockSpec(memory_space=pl.ANY) if i in far else vmem() for i in range(len(ins))
    ]
    return pl.pallas_call(
        kernel,
        in_specs=specs,
        out_specs=[vmem()] * len(out_shape),
        out_shape=out_shape,
        input_output_aliases=aliases or {},
        scratch_shapes=list(scratch),
        cost_estimate=cost(weight),
        compiler_params=pltpu.CompilerParams(vmem_limit_bytes=mib * MIB),
        name=name,
    )(*ins)


def struct(shape, dtype):
    return jax.ShapeDtypeStruct(shape, dtype)


def params(mib):
    return pltpu.CompilerParams(
        vmem_limit_bytes=mib * MIB, dimension_semantics=("arbitrary",)
    )


def cost(us):
    return pl.CostEstimate(
        flops=int(us * PEAK_PER_US * WEIGHT), bytes_accessed=0, transcendentals=0
    )


def update(grad, rate, weight, moment, average, outs, at=Ellipsis):
    moment_new = MOMENTUM * moment[at] + grad
    weight_new = weight.astype(F32) - rate * (grad + MOMENTUM * moment_new)
    outs[0][at] = grad
    outs[1][at] = moment_new
    outs[2][at] = weight_new
    outs[3][at] = AVERAGE * average[at] + (1.0 - AVERAGE) * weight_new


def total_of(pieces):
    total = pieces[0][...]
    for piece in pieces[1:]:
        total = total + piece[...].astype(F32)
    return total


def finish_kernel(kind, count, rates, *refs):
    pieces, rest = refs[:count], refs[count:]
    sets = len(rates)
    held = [rest[3 * i : 3 * i + 3] for i in range(sets)]
    outs = [rest[3 * sets + 4 * i : 3 * sets + 4 * i + 4] for i in range(sets)]
    if kind == "up":
        total = total_of(pieces)
        update(total[:, :D], rates[0], held[0][0][...], *held[0][1:], outs[0])
        update(total[:, D:], rates[1], held[1][0][...], *held[1][1:], outs[1])
    elif kind == "down":
        total = total_of(pieces)
        r = total.shape[0]
        weight = held[0][0][...].astype(F32)
        for slab in range(weight.shape[0] // r):
            at = slice(slab * r, (slab + 1) * r)
            grad = total[:, slab * D : (slab + 1) * D]
            update(grad, rates[0], weight[at], *held[0][1:], outs[0], at)
    else:
        total = total_of(pieces)
        r = total.shape[0]
        for k in range(3):
            for g in range(GROUPS):
                at = (k, slice(None), slice(g * GROUP, (g + 1) * GROUP))
                low = g * D + k * GROUP
                update(
                    total[:, low : low + GROUP], rates[0], held[0][0][at], *held[0][1:], outs[0], at
                )
        rest_rows = jnp.zeros((LANES - r, LANES), F32)
        turned = jnp.transpose(jnp.concatenate([total[:, GROUPS * D :], rest_rows], axis=0))
        for k in range(3):
            grad = turned[3 * k : 3 * k + 3, :r]
            update(grad, rates[1], held[1][0][k], *held[1][1:], outs[1], k)
        update(turned[9:11, :r], rates[2], held[2][0][...], *held[2][1:], outs[2])


def finish(kind, pieces, sets, rates, weight=1.5):
    flat = [array for one in sets for array in one]
    shapes = [one[0].shape for one in sets for _ in range(4)]
    outs = pl.pallas_call(
        functools.partial(finish_kernel, kind, len(pieces), rates),
        grid=(1,),
        in_specs=[whole(array.shape) for array in list(pieces) + flat],
        out_specs=[whole(shape) for shape in shapes],
        out_shape=[struct(shape, F32) for shape in shapes],
        cost_estimate=cost(weight),
        compiler_params=params(8),
        name="finish",
    )(*pieces, *flat)
    return [outs[4 * i : 4 * i + 4] for i in range(len(sets))]


def pack(attn_rows, conv_cols, gain_cols):
    shape = (attn_rows.shape[1], 3 * D + LANES)
    return pl.pallas_call(
        pack_kernel,
        grid=(1,),
        in_specs=[whole(array.shape) for array in (attn_rows, conv_cols, gain_cols)],
        out_specs=whole(shape),
        out_shape=struct(shape, BF),
        scratch_shapes=[pltpu.VMEM((LANES, LANES), F32)],
        cost_estimate=cost(1),
        compiler_params=params(56),
        name="pack",
    )(attn_rows, conv_cols, gain_cols)


def front(act_short, act_long, w_attn):
    short, rows = act_short.shape[0], act_short.shape[0] + act_long.shape[0]
    shapes = [
        struct((rows, D), BF),
        struct((16, D), F32),
        struct((3, rows, D), BF),
        struct((3, rows, D), BF),
        struct((rows, D), BF),
    ]
    kernel = functools.partial(front_kernel, short)
    return vmem_call(kernel, "front", [act_short, act_long, w_attn], shapes, 16, HEAVY)


def front_more(short, group, normed, small, w_attn, before):
    shapes = [struct(array.shape, array.dtype) for array in before]
    return vmem_call(
        functools.partial(front_more_kernel, short, group),
        "front_more",
        [normed, small, w_attn, *before],
        shapes,
        16,
        1,
        aliases={3 + i: i for i in range(len(before))},
    )


def kept_again(before, first):
    specs = [pl.BlockSpec(memory_space=pl.ANY)] * len(before)
    return specs, {first + i: i for i in range(len(before))}


def up(act_short, act_long, cot_short, cot_long, len_short, len_long, attended, w_up, small, s):
    short, rows = act_short.shape[0], act_short.shape[0] + act_long.shape[0]
    ff = w_up.shape[1] - D
    tiles = ff // D
    half = D // (2 * s)
    halves = struct((tiles * half, s, D), BF)
    return pl.pallas_call(
        functools.partial(up_kernel, short, s),
        grid=(tiles // 2,),
        in_specs=[
            smem(),
            smem(),
            whole(act_short.shape),
            whole(act_long.shape),
            whole(cot_short.shape),
            whole(cot_long.shape),
            whole((rows, D)),
            pl.BlockSpec((D, D), lambda i: (0, 0)),
            pl.BlockSpec((D, D), lambda i: (0, 1 + i)),
            whole((16, D)),
        ],
        out_specs=[
            whole((rows, D)),
            whole((rows, D)),
            whole((rows, D)),
            pl.BlockSpec((rows, D), lambda i: (0, i)),
            pl.BlockSpec((half, s, D), lambda i: (i, 0, 0)),
            pl.BlockSpec((half, s, D), lambda i: (i, 0, 0)),
        ],
        out_shape=[
            struct((rows, D), F32),
            struct((rows, D), BF),
            struct((rows, D), BF),
            struct((rows, ff // 2), BF),
            halves,
            halves,
        ],
        cost_estimate=cost(HEAVY),
        compiler_params=params(12),
        name="up",
    )(
        len_short, len_long, act_short, act_long, cot_short, cot_long, attended, w_up, w_up, small
    )


def up_more(normed_two, upstream, w_up, s, before):
    rows = upstream.shape[0]
    tiles = (w_up.shape[1] - D) // D
    first = tiles // 2
    half = D // (2 * s)
    specs, aliases = kept_again(before, 3)
    return pl.pallas_call(
        functools.partial(up_more_kernel, s),
        grid=(tiles - first,),
        in_specs=[
            whole((rows, D)),
            whole((rows, D)),
            pl.BlockSpec((D, D), lambda i: (0, 1 + first + i)),
        ]
        + specs,
        out_specs=[
            pl.BlockSpec((half, s, D), lambda i: (first + i, 0, 0)),
            pl.BlockSpec((half, s, D), lambda i: (first + i, 0, 0)),
            pl.BlockSpec((rows, D), lambda i: (0, i)),
        ],
        out_shape=[struct(array.shape, array.dtype) for array in before]
        + [struct((rows, (tiles - first) * D), BF)],
        input_output_aliases=aliases,
        cost_estimate=cost(HEAVY),
        compiler_params=params(10),
        name="up_more",
    )(normed_two, upstream, w_up, *before)


def down(upstream, w_down, squared, w_up, normed_two, r):
    rows = upstream.shape[0]
    ff = w_down.shape[0]
    count = ff // D // 2
    half = D // (2 * r)
    return pl.pallas_call(
        functools.partial(down_kernel, r),
        grid=(count,),
        in_specs=[
            whole((rows, D)),
            pl.BlockSpec((D, D), lambda i: (i, 0)),
            pl.BlockSpec((rows, D), lambda i: (0, i)),
            pl.BlockSpec((D, D), lambda i: (0, 1 + i)),
            whole((rows, D)),
        ],
        out_specs=[
            pl.BlockSpec((half, r, D), lambda i: (0, 0, 1 + i)),
            pl.BlockSpec((half, r, D), lambda i: (0, 0, 1 + i)),
            whole((rows, D)),
        ],
        out_shape=[
            struct((half, r, D + ff), BF),
            struct((half, r, D + ff), BF),
            struct((rows, D), F32),
        ],
        cost_estimate=cost(HEAVY),
        compiler_params=params(15),
        name="down",
    )(upstream, w_down, squared, w_up, normed_two)


def down_more(
    upstream, w_down, squared, w_up, normed_two, attended, middle, small, r, total, before
):
    rows = upstream.shape[0]
    ff = w_down.shape[0]
    tiles = ff // D
    begun = tiles // 2
    last = tiles - begun
    half = D // (2 * r)

    def tile(i):
        return begun + jnp.minimum(i, last - 1)

    def put(i):
        return (0, 0, jnp.where(i < last, 1 + begun + i, 0))

    specs, aliases = kept_again(before, 9)
    return pl.pallas_call(
        functools.partial(down_more_kernel, last, r),
        grid=(last + 1,),
        in_specs=[
            whole((rows, D)),
            pl.BlockSpec((D, D), lambda i: (tile(i), 0)),
            pl.BlockSpec((rows, D), lambda i: (0, tile(i) - begun)),
            pl.BlockSpec((D, D), lambda i: (0, 1 + tile(i))),
            whole((rows, D)),
            whole((rows, D)),
            whole((rows, D)),
            whole((16, D)),
            whole((rows, D)),
        ]
        + specs,
        out_specs=[
            pl.BlockSpec((half, r, D), put),
            pl.BlockSpec((half, r, D), put),
            whole((rows, D)),
            whole((rows, D)),
            whole((8, D)),
        ],
        out_shape=[
            struct((half, r, D + ff), BF),
            struct((half, r, D + ff), BF),
            struct((rows, D), F32),
            struct((rows, D), BF),
            struct((8, D), F32),
        ],
        input_output_aliases=aliases,
        scratch_shapes=[pltpu.VMEM((rows, D), F32)],
        cost_estimate=cost(HEAVY),
        compiler_params=params(16),
        name="down_more",
    )(
        upstream, w_down, squared, w_up, normed_two, attended, middle, small, total, *before
    )


def mixer(
    short, r, group, mixed, projected, grad_branch, w_up, small, normed, w_attn, total=None,
    before=(), last=(),
):
    rows = grad_branch.shape[0]
    half = D // (2 * r)
    ins = [mixed, projected, grad_branch, w_up, small, normed, w_attn]
    if group > 0:
        ins = ins + [total]
    aliases = {}
    if group < GROUPS - 1:
        aliases = {len(ins) + i: i for i in range(len(before))}
        ins = ins + list(before)
        part = struct((half, r, (GROUPS - 1) * D), BF)
        out_shape = [part, part, struct((16, D), F32), struct((rows, D), F32)]
    else:
        act_short, act_long = last[:2]
        ins = ins + list(last)
        part = struct((half, r, D + LANES), BF)
        out_shape = [part, part, struct(act_short.shape, F32), struct(act_long.shape, F32)]
    return vmem_call(
        functools.partial(mixer_kernel, short, r, group),
        "mixer",
        ins,
        out_shape,
        16,
        2 if group == 1 else HEAVY,
        scratch=[
            pltpu.VMEM((3, rows, GROUP), F32),
            pltpu.VMEM((GROUP, D), BF),
            pltpu.SemaphoreType.DMA,
        ],
        aliases=aliases,
        far=(3,),
    )


def output(act_short, act_long, squared, more, w_down, middle):
    short, rows = act_short.shape[0], middle.shape[0]
    ff = w_down.shape[0]
    first = squared.shape[1] // D
    return pl.pallas_call(
        functools.partial(output_kernel, short, first),
        grid=(ff // D,),
        in_specs=[
            pl.BlockSpec((rows, D), lambda i: (0, jnp.minimum(i, first - 1))),
            pl.BlockSpec((rows, D), lambda i: (0, jnp.maximum(i - first, 0))),
            pl.BlockSpec((D, D), lambda i: (i, 0)),
            whole((rows, D)),
        ],
        out_specs=[whole(act_short.shape), whole(act_long.shape)],
        out_shape=[struct(act_short.shape, BF), struct(act_long.shape, BF)],
        scratch_shapes=[pltpu.VMEM((rows, D), F32)],
        cost_estimate=cost(HEAVY),
        compiler_params=params(12),
        name="output",
    )(squared, more, w_down, middle)


def shards(grid, *args):
    act_short, act_long, cot_short, cot_long, len_short, len_long = args[:6]
    owned = args[6:12]
    moments = args[12:18]
    averages = args[18:24]
    attn_rows, conv_cols, out_rows, up_rows, down_rows, gain_cols = owned
    r = out_rows.shape[0]
    s = down_rows.shape[0]
    short = act_short.shape[0]
    rows = short + act_long.shape[0]

    chunk_attn = pack(attn_rows, conv_cols, gain_cols)
    parts = s // r
    chunk_up = jnp.concatenate([out_rows, up_rows], axis=1)
    chunk_down = jnp.concatenate([down_rows[i * r : (i + 1) * r] for i in range(parts)], axis=1)
    wide, wide_up, wide_down = chunk_attn.shape[1], chunk_up.shape[1], chunk_down.shape[1]
    over_a, over_x, over_z = a_moves(grid), x_moves(grid), z_moves(grid)

    pieces = exchange(chunk_attn, over_z)
    (col_attn,) = place_z(grid, pieces, [(0, wide)])
    pieces_attn = exchange(col_attn, both_moves(grid))
    pieces_up = exchange(after(chunk_up, col_attn), over_z)
    plane_attn = place_both(grid, held_back(pieces_attn, *pieces_up[1:]))
    other_attn = swap(grid, plane_attn)
    up_low, up_high = halves(grid, held_back(pieces_up, plane_attn), wide_up)
    up_low, up_high = exchange(up_low, over_a), exchange(up_high, over_x)
    w_attn = join(grid, plane_attn, other_attn, wide)
    normed, small, *begun = front(act_short, act_long, w_attn)
    up_low, up_high = place_first(grid, held_back(up_low, normed), held_back(up_high, normed))
    pieces_down = exchange(after(chunk_down, up_low), over_z)
    up_low, up_high = exchange(up_low, over_x), exchange(up_high, over_a)
    begun = front_more(short, 1, after(normed, up_low[0]), small, w_attn, begun)
    down_low, down_high = halves(grid, held_back(pieces_down, begun[2]), wide_down)
    down_low, down_high = exchange(down_low, over_a), exchange(down_high, over_x)
    projected, mixed, attended = front_more(
        short, 2, after(normed, down_low[0]), small, w_attn, begun
    )
    plane_up = place_second(grid, held_back(up_low, attended), held_back(up_high, attended))
    other_up = swap(grid, plane_up)
    down_low, down_high = place_first(
        grid, held_back(down_low, plane_up), held_back(down_high, plane_up), HEAVY
    )
    down_low, down_high = exchange(down_low, over_x), exchange(down_high, over_a)
    w_up = join(grid, plane_up, after(other_up, down_low[0]), wide_up)
    middle, normed_two, upstream, squared, *begun = up(
        act_short, act_long, cot_short, cot_long, len_short, len_long, attended, w_up, small, s
    )
    plane_down = place_second(
        grid, held_back(down_low, normed_two), held_back(down_high, normed_two)
    )
    other_down = swap(grid, plane_down)
    kept_down, sent_down, more = up_more(
        after(normed_two, plane_down), upstream, w_up, s, begun
    )
    w_down = join(grid, plane_down, after(other_down, more), D)

    sent_down = swap(grid, sent_down)
    *begun, total = down(upstream, w_down, squared, w_up, normed_two, r)
    low_down, high_down = add_core(grid, kept_down, after(sent_down, total), D // 2)
    kept_up, sent_up, grad_middle, grad_branch, grad_gain_two = down_more(
        after(upstream, low_down[0]), w_down, more, w_up, normed_two, attended, middle, small,
        r, total, begun,
    )
    sent_up = swap(grid, sent_up)
    low_down, high_down = add_plane(
        grid, held_back(low_down, grad_branch), held_back(high_down, grad_branch)
    )
    low_up, high_up = add_core(grid, kept_up, after(sent_up, low_down[0]), wide_up // 2)
    shared = (mixed, projected, grad_branch, w_up, small, normed, w_attn)
    *begun, total = mixer(
        short, r, 0, mixed, projected, after(grad_branch, low_up[0]), *shared[3:]
    )
    pieces_down = add_z(
        grid, r, [(held_back(low_down, total), held_back(high_down, total))]
    )
    kept_a, sent_a, grad_taps, total = mixer(
        short, r, 1, *shared, total=after(total, pieces_down[0]), before=begun
    )
    sent_a = swap(grid, sent_a)
    pieces_down = add_rest(grid, held_back(pieces_down, total))
    low_up, high_up = add_plane(
        grid, held_back(low_up, pieces_down[0]), held_back(high_up, pieces_down[0])
    )
    low_a, high_a = add_core(grid, kept_a, after(sent_a, low_up[0]), D)
    kept_b, sent_b, back_short, back_long = mixer(
        short, r, 2, *shared, total=after(total, low_a[0]),
        last=(act_short, act_long, grad_middle, grad_taps, grad_gain_two),
    )
    low_up, high_up = held_back(low_up, back_short), held_back(high_up, back_short)
    sent_b = swap(grid, sent_b)
    pieces_up = add_z(grid, r, [(held_back(low_up, back_short), held_back(high_up, back_short))])
    pieces_down = held_back(pieces_down, back_short)
    low_a, high_a = add_plane(
        grid,
        held_back(low_a, pieces_up[0], pieces_down[1]),
        held_back(high_a, pieces_up[0], pieces_down[1]),
    )
    pieces_b = add_both(grid, kept_b, after(sent_b, low_a[0]))
    out_short, out_long = output(
        act_short, act_long, squared, more, w_down, after(middle, pieces_b[0])
    )
    low_a, high_a = held_back(low_a, out_short), held_back(high_a, out_short)
    pieces_up = add_rest(grid, held_back(pieces_up, out_short))
    pieces_b = held_back(pieces_b, pieces_up[0])
    pieces_attn = add_z(grid, r, [(low_a, high_a), (pieces_b,)])
    pieces_up = held_back(pieces_up, pieces_attn[0])
    pieces_attn = add_rest(grid, held_back(pieces_attn, pieces_up[1]))
    scale_tokens = math.sqrt(rows * grid.a * grid.f)
    rates = [rate / scale_tokens for rate in RATES]
    sets = list(zip(owned, moments, averages))
    (done_down,) = finish("down", pieces_down, sets[4:5], rates[4:5])
    done_out, done_up = finish("up", pieces_up, sets[2:4], rates[2:4])
    done_attn, done_taps, done_gains = finish(
        "attn", pieces_attn, [sets[0], sets[1], sets[5]], [rates[0], rates[1], rates[5]]
    )
    results = [out_short, out_long, back_short, back_long]
    for done in (done_attn, done_taps, done_out, done_up, done_down, done_gains):
        results.extend(done)
    return tuple(results)


def solution(mesh):
    rows = P(AXES, None)
    weights = [P(None, AXES, None), P(None, None, AXES), rows, rows, rows, P(None, AXES)]
    in_specs = tuple([rows] * 4 + [P(AXES)] * 2 + weights * 3)
    out_specs = tuple([rows] * 4 + [spec for spec in weights for _ in range(4)])
    grid = Grid(mesh)

    def program(*args):
        return shards(grid, *args)

    return jax.shard_map(
        program, mesh=mesh, in_specs=in_specs, out_specs=out_specs, check_vma=False
    )
```

```python
import functools
import math

import jax
import jax.numpy as jnp
from jax import lax
from jax.experimental import pallas as pl
from jax.experimental.pallas import tpu as pltpu
from jax.sharding import PartitionSpec as P

D = 768
HEAD_DIM = 64
GROUP = 256
GROUPS = D // GROUP
BLOCK = 256
LANES = 128

EPS = 1e-06
MOMENTUM = 0.9
AVERAGE = 0.5
RATES = (0.03, 0.5, 0.6, 0.025, 0.007, 0.05)
NEG = -1e30
HEAD_SCALE = 0.125
AXES = ("dp", "fsdp")
BF = jnp.bfloat16
F32 = jnp.float32
MIB = 1024 * 1024
PEAK_PER_US = 1.15e9
WEIGHT = 1.0
HEAVY = 100


class Grid:
    def __init__(self, mesh):
        self.a = mesh.shape["dp"]
        self.f = mesh.shape["fsdp"]
        self.x = 2
        self.z = self.f // 4

    def index(self, a, z, x, c):
        return a * self.f + (z * self.x + x) * 2 + c

    def perm(self, move):
        pairs = []
        for a in range(self.a):
            for z in range(self.z):
                for x in range(self.x):
                    for c in range(2):
                        pairs.append((self.index(a, z, x, c), self.index(*move(a, z, x, c))))
        return pairs

    def swap_core(self):
        return self.perm(lambda a, z, x, c: (a, z, x, 1 - c))

    def shift_plane(self, da, dx):
        return self.perm(lambda a, z, x, c: ((a + da) % self.a, z, (x + dx) % self.x, c))

    def shift_z(self, dz):
        return self.perm(lambda a, z, x, c: (a, (z + dz) % self.z, x, c))

    def flip_z(self, bit):
        return self.perm(lambda a, z, x, c: (a, z ^ bit, x, c))

    def z_bits(self):
        bits, bit = [], 1
        while bit < self.z:
            bits.append(bit)
            bit *= 2
        return bits

    def here(self):
        f = lax.axis_index("fsdp")
        return lax.axis_index("dp"), f // 4, (f // 2) % 2, f % 2

    def plane_moves(self):
        return [(da, dx) for da in range(self.a) for dx in range(self.x) if da or dx]


def after(value, *others):
    return lax.optimization_barrier((value,) + others)[0]


def relay_kernel(grid, body, count, *refs):
    body(grid.here(), refs[:count], refs[count:])


def along(shape, axis):
    if axis is None:
        return pl.BlockSpec(shape, lambda i: (0,) * len(shape))
    block = tuple(1 if j == axis else size for j, size in enumerate(shape))
    return pl.BlockSpec(block, lambda i: tuple(i if j == axis else 0 for j in range(len(shape))))


def relay(grid, name, body, steps, ins, outs, weight=1):
    return pl.pallas_call(
        functools.partial(relay_kernel, grid, body, len(ins)),
        grid=(steps,),
        in_specs=[along(array.shape, axis) for array, axis in ins],
        out_specs=[along(shape, axis) for shape, _, axis in outs],
        out_shape=[jax.ShapeDtypeStruct(shape, kind) for shape, kind, _ in outs],
        cost_estimate=cost(weight),
        compiler_params=params(8),
        name=name,
    )(*[array for array, _ in ins])


def z_moves(grid):
    return [
        (
            grid.shift_z(dz),
            lambda a, z, x, c, dz=dz: ((z + dz) % grid.z,),
            lambda a, z, x, c, dz=dz: ((z - dz) % grid.z,),
        )
        for dz in range(1, grid.z)
    ]


def a_moves(grid):
    return [
        (
            grid.shift_plane(da, 0),
            lambda a, z, x, c, da=da: ((a + da) % grid.a,),
            lambda a, z, x, c, da=da: ((a - da) % grid.a,),
        )
        for da in range(1, grid.a)
    ]


def x_moves(grid):
    return [
        (
            grid.shift_plane(0, 1),
            lambda a, z, x, c: (1 - x,),
            lambda a, z, x, c: (1 - x,),
        )
    ]


def both_moves(grid):
    return [
        (
            grid.shift_plane(da, dx),
            lambda a, z, x, c, da=da, dx=dx: ((a + da) % grid.a, (x + dx) % grid.x),
            lambda a, z, x, c, da=da, dx=dx: ((a - da) % grid.a, (x - dx) % grid.x),
        )
        for da, dx in grid.plane_moves()
    ]


OWN_Z = lambda a, z, x, c: (z,)
OWN_A = lambda a, z, x, c: (a,)
OWN_X = lambda a, z, x, c: (x,)
OWN_AX = lambda a, z, x, c: (a, x)


def exchange(value, moves):
    return [value] + [lax.ppermute(value, AXES, pairs) for pairs, _, _ in moves]


def send(parts, moves):
    return [parts[0]] + [
        lax.ppermute(part, AXES, pairs) for part, (pairs, _, _) in zip(parts[1:], moves)
    ]


def swap(grid, value):
    return lax.ppermute(value, AXES, grid.swap_core())


def arrived(own, moves):
    return [own] + [brought for _, _, brought in moves]


def leaving(own, moves):
    return [own] + [sent for _, sent, _ in moves]


def held_back(pieces, *others):
    return [pieces[0]] + [after(piece, *others) for piece in pieces[1:]]


def place_z(grid, pieces, cuts):
    spots = arrived(OWN_Z, z_moves(grid))
    r = pieces[0].shape[0]

    def body(here, ins, outs):
        for piece, spot in zip(ins, spots):
            at = spot(*here)[0]
            for out, (low, high) in zip(outs, cuts):
                out[at] = piece[:, low:high]

    outs = [((grid.z, r, high - low), BF, None) for low, high in cuts]
    return relay(grid, "place_z", body, 1, [(piece, None) for piece in pieces], outs)


def flip(grid, value, bit):
    return lax.ppermute(value, AXES, grid.flip_z(bit))


def halves(grid, pieces, width):
    return place_z(grid, pieces, [(0, width // 2), (width // 2, width)])


def place_both(grid, pieces):
    spots = arrived(OWN_AX, both_moves(grid))

    def body(here, ins, outs):
        for piece, spot in zip(ins, spots):
            ia, ix = spot(*here)
            outs[0][ia, 0, ix] = piece[0]

    z, r, n = pieces[0].shape
    outs = [((grid.a, z, grid.x, r, n), BF, 1)]
    return relay(grid, "place_both", body, z, [(piece, 0) for piece in pieces], outs)[0]


def place_first(grid, over_a, over_x, weight=1):
    a_spots = arrived(OWN_A, a_moves(grid))
    x_spots = arrived(OWN_X, x_moves(grid))

    def body(here, ins, outs):
        for piece, spot in zip(ins, a_spots):
            outs[0][spot(*here)[0], 0] = piece[0]
        for piece, spot in zip(ins[len(a_spots) :], x_spots):
            outs[1][0, spot(*here)[0]] = piece[0]

    z, r, n = over_a[0].shape
    m = over_x[0].shape[-1]
    ins = [(piece, 0) for piece in over_a + over_x]
    outs = [((grid.a, z, r, n), BF, 1), ((z, grid.x, r, m), BF, 0)]
    return relay(grid, "place_first", body, z, ins, outs, weight)


def place_second(grid, over_x, over_a):
    x_spots = arrived(OWN_X, x_moves(grid))
    a_spots = arrived(OWN_A, a_moves(grid))
    z, r, n = over_x[0].shape[1:]
    m = over_a[0].shape[-1]

    def body(here, ins, outs):
        for piece, spot in zip(ins, x_spots):
            for ia in range(grid.a):
                outs[0][ia, 0, spot(*here)[0], :, :n] = piece[ia, 0]
        for piece, spot in zip(ins[len(x_spots) :], a_spots):
            for ix in range(grid.x):
                outs[0][spot(*here)[0], 0, ix, :, n:] = piece[0, ix]

    ins = [(piece, 1) for piece in over_x] + [(piece, 0) for piece in over_a]
    outs = [((grid.a, z, grid.x, r, n + m), BF, 1)]
    return relay(grid, "place_second", body, z, ins, outs)[0]


def join(grid, plane, other, width):
    r, n = plane.shape[-2:]
    parts = n // width
    owners = grid.a * grid.x

    def body(here, ins, outs):
        core = here[3]
        for source, at in ((ins[0], core), (ins[1], 1 - core)):
            for i in range(owners):
                for part in range(parts):
                    outs[0][0, i, at, part] = source[0, i, :, part * width : (part + 1) * width]

    plane, other = (
        array.reshape(grid.z, owners, r, n) for array in (plane, other)
    )
    outs = [((grid.z, owners, 2, parts, r, width), BF, 0)]
    (whole_array,) = relay(grid, "join", body, grid.z, [(plane, 0), (other, 0)], outs)
    return whole_array.reshape(-1, width)


def add_at(pieces, where):
    total = pieces[0][where].astype(F32)
    for piece in pieces[1:]:
        total = total + piece[where].astype(F32)
    return total


def add_core(grid, kept, got, cut):
    a_spots = leaving(OWN_A, a_moves(grid))
    x_spots = leaving(OWN_X, x_moves(grid))
    shape = (grid.a, grid.z, grid.x) + kept.shape[-2:]
    kept, got = kept.reshape(shape), got.reshape(shape)
    r, n = shape[-2:]
    low, high = slice(0, cut), slice(cut, n)

    def body(here, ins, outs):
        for out, spot in zip(outs, a_spots):
            for ix in range(grid.x):
                out[0, ix] = add_at(ins, (spot(*here)[0], 0, ix, slice(None), low)).astype(BF)
        for out, spot in zip(outs[len(a_spots) :], x_spots):
            for ia in range(grid.a):
                out[ia, 0] = add_at(ins, (ia, 0, spot(*here)[0], slice(None), high)).astype(BF)

    outs = [((grid.z, grid.x, r, cut), BF, 0)] * len(a_spots)
    outs += [((grid.a, grid.z, r, n - cut), BF, 1)] * len(x_spots)
    parts = relay(grid, "add_core", body, grid.z, [(kept, 1), (got, 1)], outs)
    return (
        send(parts[: len(a_spots)], a_moves(grid)),
        send(parts[len(a_spots) :], x_moves(grid)),
    )


def add_plane(grid, low, high):
    x_spots = leaving(OWN_X, x_moves(grid))
    a_spots = leaving(OWN_A, a_moves(grid))
    z, _, r, n = low[0].shape
    m = high[0].shape[-1]

    def body(here, ins, outs):
        for out, spot in zip(outs, x_spots):
            out[0] = add_at(ins[: len(low)], (0, spot(*here)[0])).astype(BF)
        for out, spot in zip(outs[len(x_spots) :], a_spots):
            out[0] = add_at(ins[len(low) :], (spot(*here)[0], 0)).astype(BF)

    ins = [(piece, 0) for piece in low] + [(piece, 1) for piece in high]
    outs = [((z, r, n), BF, 0)] * len(x_spots) + [((z, r, m), BF, 0)] * len(a_spots)
    parts = relay(grid, "add_plane", body, z, ins, outs, HEAVY)
    return (
        send(parts[: len(x_spots)], x_moves(grid)),
        send(parts[len(x_spots) :], a_moves(grid)),
    )


def add_both(grid, kept, got, weight=1):
    spots = leaving(OWN_AX, both_moves(grid))
    shape = (grid.a, grid.z, grid.x) + kept.shape[-2:]

    def body(here, ins, outs):
        for out, spot in zip(outs, spots):
            ia, ix = spot(*here)
            out[0] = add_at(ins, (ia, 0, ix)).astype(BF)

    ins = [(kept.reshape(shape), 1), (got.reshape(shape), 1)]
    outs = [((grid.z,) + shape[-2:], BF, 0)] * len(spots)
    return send(relay(grid, "add_both", body, grid.z, ins, outs, weight), both_moves(grid))


def add_z(grid, r, parts):
    lanes, end = [], 0
    for part in parts:
        widths = [half[0].shape[-1] for half in part]
        lanes.append((end, widths))
        end += sum(widths) * (part[0][0].shape[1] // r)
    count = grid.z // 2

    def body(here, ins, outs):
        mine = here[1] % 2
        for out, bit in ((outs[0], mine), (outs[1], 1 - mine)):
            for place in range(count):
                at, first = 2 * place + bit, 0
                for part, (start, widths) in zip(parts, lanes):
                    for i, half in enumerate(part):
                        total = add_at(ins[first : first + len(half)], at)
                        for slab in range(total.shape[0] // r):
                            low = start + slab * sum(widths) + sum(widths[:i])
                            piece = total[slab * r : (slab + 1) * r]
                            out[place, :, low : low + widths[i]] = piece.astype(BF)
                        first += len(half)

    ins = [(piece, None) for part in parts for half in part for piece in half]
    outs = [((count, r, end), BF, None)] * 2
    kept, sent = relay(grid, "add_z", body, 1, ins, outs)
    return [kept, flip(grid, sent, 1)]


def add_rest(grid, pieces):
    for bit in grid.z_bits()[1:]:
        count, r, n = pieces[0].shape
        last = count == 2

        def body(here, ins, outs):
            mine = (here[1] // bit) % 2
            for out, at in ((outs[0], mine), (outs[1], 1 - mine)):
                for place in range(count // 2):
                    where = Ellipsis if last else place
                    out[where] = add_at(ins, 2 * place + at).astype(out.dtype)

        shape = (r, n) if last else (count // 2, r, n)
        outs = [(shape, F32 if last else BF, None), (shape, BF, None)]
        kept, sent = relay(grid, "add_rest", body, 1, [(piece, None) for piece in pieces], outs)
        pieces = [kept, flip(grid, sent, bit)]
    return pieces


def dot(left, right):
    return lax.dot_general(left, right, (((1,), (0,)), ((), ())), preferred_element_type=F32)


def dot_bt(left, right):
    return lax.dot_general(left, right, (((1,), (1,)), ((), ())), preferred_element_type=F32)


def dot_at(left, right):
    return lax.dot_general(left, right, (((0,), (0,)), ((), ())), preferred_element_type=F32)


def rms_scale(values):
    return lax.rsqrt(jnp.mean(values * values, axis=-1, keepdims=True) + EPS)


def norm_back(values, gain, grad):
    scale = rms_scale(values)
    scaled = grad * gain
    inner = jnp.mean(scaled * values, axis=-1, keepdims=True)
    grad_gain = jnp.sum(grad * (values * scale), axis=0, keepdims=True)
    return scale * scaled - values * (scale * scale * scale * inner), grad_gain


def positions_of(rows, short, width):
    row = lax.broadcasted_iota(jnp.int32, (rows, width), 0)
    return jnp.where(row < short, row, row - short), row < short


def shift_down(values, offset, position):
    return jnp.where(position >= offset, pltpu.roll(values, offset, 0), 0.0)


def shift_up(values, offset, room):
    rows = values.shape[0]
    return jnp.where(room >= offset, pltpu.roll(values, rows - offset, 0), 0.0)


def head_mask(half):
    lane = lax.broadcasted_iota(jnp.int32, (1, LANES), 1)
    return (lane // HEAD_DIM) == half


def blocks_of(rows, short):
    found = []
    for start, length in ((0, short), (short, rows - short)):
        for block in range(length // BLOCK):
            found.append((start + block * BLOCK, start, (block + 1) * BLOCK))
    return found


def store_split(value, owner_rows, kept, sent, lanes=slice(None)):
    first = lax.axis_index("fsdp") % 2 == 0
    for pair in range(value.shape[0] // (2 * owner_rows)):
        at = 2 * pair * owner_rows
        even, odd = value[at : at + owner_rows], value[at + owner_rows : at + 2 * owner_rows]
        kept[pair, :, lanes] = jnp.where(first, even, odd).astype(BF)
        sent[pair, :, lanes] = jnp.where(first, odd, even).astype(BF)


def _():
            for pair in range(value.shape[0] // (2 * owner_rows)):
                at = 2 * pair * owner_rows
                first[pair, :, lanes] = value[at : at + owner_rows].astype(BF)
                second[pair, :, lanes] = value[at + owner_rows : at + 2 * owner_rows].astype(BF)


def front_kernel(short, xs, xl, w, normed, small, *refs):
    rows = normed.shape[0]
    turned = jnp.transpose(w[:, 3 * D : 3 * D + LANES].astype(F32))[:16]
    small[...] = turned
    gain = turned[9:10]
    for ref, first, count in ((xs, 0, short), (xl, short, rows - short)):
        x = ref[...].astype(F32)
        normed[first : first + count] = (x * rms_scale(x) * gain).astype(BF)
    front_group(short, 0, normed, small, w, *refs)


def front_more_kernel(short, group, normed, small, w, *refs):
    front_group(short, group, normed, small, w, *refs[-3:])


def front_group(short, group, normed, small, w, projected, mixed, attended):
    rows = normed.shape[0]
    columns = slice(group * GROUP, (group + 1) * GROUP)
    taps = small[:, columns]
    position, _ = positions_of(rows, short, GROUP)
    base = normed[...]
    for k in range(3):
        p = dot(base, w[:, k * D + group * GROUP : k * D + (group + 1) * GROUP])
        projected[k, :, columns] = p.astype(BF)
        mixed[k, :, columns] = (
            taps[3 * k : 3 * k + 1] * p
            + taps[3 * k + 1 : 3 * k + 2] * shift_down(p, 1, position)
            + taps[3 * k + 2 : 3 * k + 3] * shift_down(p, 2, position)
        ).astype(BF)
    for pair in range(GROUP // LANES):
        lane = group * GROUP + pair * LANES
        lanes = slice(lane, lane + LANES)
        for first, key_first, key_count in blocks_of(rows, short):
            queries = mixed[0, first : first + BLOCK, lanes]
            keys = mixed[1, key_first : key_first + key_count, lanes]
            values = mixed[2, key_first : key_first + key_count, lanes]
            row = lax.broadcasted_iota(jnp.int32, (BLOCK, key_count), 0) + (first - key_first)
            causal = lax.broadcasted_iota(jnp.int32, (BLOCK, key_count), 1) <= row
            total = None
            for half in range(2):
                scale = jnp.where(head_mask(half), HEAD_SCALE, 0.0).astype(BF)
                keep = jnp.where(head_mask(half), 1.0, 0.0).astype(BF)
                scores = jnp.where(causal, dot_bt(queries * scale, keys), NEG)
                peak = jnp.max(scores, axis=-1, keepdims=True)
                exponent = jnp.exp(scores - peak)
                weights = exponent * (1.0 / jnp.sum(exponent, axis=-1, keepdims=True))
                part = dot(weights.astype(BF), values * keep)
                total = part if total is None else total + part
            attended[first : first + BLOCK, lanes] = total.astype(BF)


def pack_kernel(attn, taps, gains, out, scratch):
    r = attn.shape[1]
    scratch[...] = jnp.zeros_like(scratch)
    for k in range(3):
        out[:, k * D : (k + 1) * D] = attn[k]
        scratch[3 * k : 3 * k + 3, :r] = taps[k].astype(F32)
    scratch[9:11, :r] = gains[...].astype(F32)
    out[:, 3 * D :] = jnp.transpose(scratch[...])[:r].astype(BF)


def up_tile(tile, column, owner_rows, normed, upstream, w, squared, kept, sent):
    columns = slice(column * D, (column + 1) * D)
    hidden = jnp.maximum(dot(normed[...], w[:, (1 + tile) * D : (2 + tile) * D]), 0.0)
    low = (hidden * hidden).astype(BF)
    squared[:, columns] = low
    half = D // (2 * owner_rows)
    mine = slice(tile * half, (tile + 1) * half)
    store_split(dot_at(low, upstream[...]), owner_rows, kept.at[mine], sent.at[mine])


def up_kernel(
    short, owner_rows, tiles, ls, ll, xs, xl, cs, cl, attended, w, small,
    middle, normed, upstream, squared, kept, sent,
):
    rows = normed.shape[0]
    gain = small[10:11]
    branch = dot(attended[...], w[:, :D])
    for ref, cot, limit, first, count in (
        (xs, cs, ls, 0, short),
        (xl, cl, ll, short, rows - short),
    ):
        part = slice(first, first + count)
        mid = ref[...].astype(F32) + branch[part]
        middle[part] = mid
        normed[part] = (mid * rms_scale(mid) * gain).astype(BF)
        position = lax.broadcasted_iota(jnp.int32, (count, D), 0)
        wide = jnp.where(position < limit[0], cot[...].astype(F32), 0.0)
        upstream[part] = wide.astype(BF)
    for i, tile in enumerate(tiles):
        up_tile(tile, i, owner_rows, normed, upstream, w, squared, kept, sent)


def up_more_kernel(owner_rows, tiles, normed, upstream, w, *refs):
    kept, sent, squared = refs[-3:]
    for i, tile in enumerate(tiles):
        up_tile(tile, i, owner_rows, normed, upstream, w, squared, kept, sent)


def down_tiles(tiles, owner_rows, upstream, w_down, squares, w_up, normed, kept, sent, total):
    count = squares[0].shape[1] // D
    for tile in tiles:
        squared, i = squares[tile // count], tile % count
        rows = slice(tile * D, (tile + 1) * D)
        lanes = slice((1 + tile) * D, (2 + tile) * D)
        grad_squared = dot_bt(upstream[...], w_down[rows])
        active = jnp.sqrt(squared[:, i * D : (i + 1) * D].astype(F32))
        grad_hidden = (grad_squared * (2.0 * active)).astype(BF)
        store_split(dot_at(normed[...], grad_hidden), owner_rows, kept, sent, lanes)
        part = dot_bt(grad_hidden, w_up[:, lanes])
        total = part if total is None else total + part
    return total


def down_kernel(owner_rows, tiles, upstream, w_down, squared, w_up, normed, kept, sent, total):
    total[...] = down_tiles(
        tiles, owner_rows, upstream, w_down, [squared], w_up, normed, kept, sent, None
    )


def down_more_kernel(
    owner_rows, tiles, upstream, w_down, squared, more, w_up, normed, attended, middle, small,
    before, *refs
):
    kept, sent, grad_middle, grad_branch, grad_gain = refs[-5:]
    total = down_tiles(
        tiles, owner_rows, upstream, w_down, [squared, more], w_up, normed, kept, sent, before[...]
    )
    pulled, gain = norm_back(middle[...], small[10:11], total)
    grad_gain[...] = jnp.broadcast_to(gain, grad_gain.shape)
    wide = upstream[...].astype(F32) + pulled
    grad_middle[...] = wide
    low = wide.astype(BF)
    grad_branch[...] = low
    store_split(dot_at(attended[...], low), owner_rows, kept, sent, slice(0, D))


def mixer_kernel(
    short, owner_rows, group, mixed, projected, branch, w_up, small, normed, w, *refs
):
    scratch, w_out, ready = refs[-3:]
    refs = refs[:-2]
    columns = slice(group * GROUP, (group + 1) * GROUP)
    fetch = pltpu.make_async_copy(w_up.at[columns, :D], w_out, ready)
    fetch.start()
    if group == 0:
        before = None
    else:
        before, refs = refs[0], refs[1:]
    if group < GROUPS - 1:
        kept, sent, taps_out, total = refs[-5:-1]
    else:
        xs, xl, grad_middle, taps_before, grad_gain_two = refs[:5]
        kept, sent, back_short, back_long = refs[-5:-1]
    rows = branch.shape[0]
    fetch.wait()
    grad_attended = dot_bt(branch[...], w_out[...]).astype(BF)
    for pair in range(GROUP // LANES):
        lanes = slice(pair * LANES, (pair + 1) * LANES)
        lane = group * GROUP + pair * LANES
        far = slice(lane, lane + LANES)
        started = set()
        for first, key_first, key_count in blocks_of(rows, short):
            block = slice(first, first + BLOCK)
            spread = slice(key_first, key_first + key_count)
            queries = mixed[0, block, far]
            keys = mixed[1, spread, far]
            values = mixed[2, spread, far]
            grads = grad_attended[block, lanes]
            row = lax.broadcasted_iota(jnp.int32, (key_count, BLOCK), 1) + (first - key_first)
            causal = lax.broadcasted_iota(jnp.int32, (key_count, BLOCK), 0) <= row
            for_queries = for_keys = for_values = None
            for half in range(2):
                scale = jnp.where(head_mask(half), HEAD_SCALE, 0.0).astype(BF)
                keep = jnp.where(head_mask(half), 1.0, 0.0).astype(BF)
                scaled = queries * scale
                own = grads * keep
                scores = jnp.where(causal, dot_bt(keys, scaled), NEG)
                peak = jnp.max(scores, axis=0, keepdims=True)
                exponent = jnp.exp(scores - peak)
                probs = exponent * (1.0 / jnp.sum(exponent, axis=0, keepdims=True))
                grad_probs = dot_bt(values, own)
                inner = jnp.sum(probs * grad_probs, axis=0, keepdims=True)
                grad_scores = (probs * (grad_probs - inner)).astype(BF)
                to_values = dot(probs.astype(BF), own)
                to_keys = dot(grad_scores, scaled)
                to_queries = dot_at(grad_scores, keys * scale)
                if half == 0:
                    for_queries, for_keys, for_values = to_queries, to_keys, to_values
                else:
                    for_queries = for_queries + to_queries
                    for_keys = for_keys + to_keys
                    for_values = for_values + to_values
            scratch[0, block, lanes] = for_queries
            for block_key in range(key_count // BLOCK):
                at = key_first + block_key * BLOCK
                inside = slice(block_key * BLOCK, (block_key + 1) * BLOCK)
                if at in started:
                    scratch[1, at : at + BLOCK, lanes] += for_keys[inside]
                    scratch[2, at : at + BLOCK, lanes] += for_values[inside]
                else:
                    started.add(at)
                    scratch[1, at : at + BLOCK, lanes] = for_keys[inside]
                    scratch[2, at : at + BLOCK, lanes] = for_values[inside]
    position, in_short = positions_of(rows, short, GROUP)
    room = jnp.where(in_short, short, rows - short) - 1 - position
    taps = small[:, columns]
    tap_rows = []
    grad_normed = None if before is None else before[...]
    for k in range(3):
        g = scratch[k]
        p = projected[k, :, columns].astype(F32)
        low = (
            taps[3 * k : 3 * k + 1] * g
            + taps[3 * k + 1 : 3 * k + 2] * shift_up(g, 1, room)
            + taps[3 * k + 2 : 3 * k + 3] * shift_up(g, 2, room)
        ).astype(BF)
        lane = (0 if group == GROUPS - 1 else group * D) + k * GROUP
        lanes = slice(lane, lane + GROUP)
        store_split(dot_at(normed[...], low), owner_rows, kept, sent, lanes)
        part = dot_bt(low, w[:, k * D + group * GROUP : k * D + (group + 1) * GROUP])
        grad_normed = part if grad_normed is None else grad_normed + part
        tap_rows.append(jnp.sum(g * p, axis=0, keepdims=True))
        for j in (1, 2):
            tap_rows.append(jnp.sum(g * shift_down(p, j, position), axis=0, keepdims=True))
    if group < GROUPS - 1:
        for i, row in enumerate(tap_rows):
            taps_out[i : i + 1, columns] = row
        total[...] = grad_normed
        return
    gain_sum = None
    for ref, out, first, count in (
        (xs, back_short, 0, short),
        (xl, back_long, short, rows - short),
    ):
        rows_of = slice(first, first + count)
        pulled, gain = norm_back(ref[...].astype(F32), small[9:10], grad_normed[rows_of])
        out[...] = grad_middle[rows_of] + pulled
        gain_sum = gain if gain_sum is None else gain_sum + gain
    row = lax.broadcasted_iota(jnp.int32, (LANES, GROUP), 0)
    for g in range(GROUPS):
        lanes = slice(g * GROUP, (g + 1) * GROUP)
        packed = jnp.where(row == 9, gain_sum[:, lanes], jnp.zeros((LANES, GROUP), F32))
        packed = jnp.where(row == 10, grad_gain_two[0:1, lanes], packed)
        for i, tap_row in enumerate(tap_rows):
            tap = tap_row if g == group else taps_before[i : i + 1, lanes]
            packed = jnp.where(row == i, tap, packed)
        packed_all = packed if g == 0 else jnp.concatenate([packed_all, packed], axis=1)
    store_split(jnp.transpose(packed_all), owner_rows, kept, sent, slice(D, D + LANES))


def output_kernel(short, first, squared, more, wdown, middle, out_short, out_long, total):
    step = pl.program_id(0)

    @pl.when(step == 0)
    def _():
        total[...] = middle[...] + dot(squared[...], wdown[...])

    @pl.when(jnp.logical_and(step > 0, step < first))
    def _():
        total[...] += dot(squared[...], wdown[...])

    @pl.when(step >= first)
    def _():
        total[...] += dot(more[...], wdown[...])

    @pl.when(step == pl.num_programs(0) - 1)
    def _():
        out_short[...] = total[:short].astype(BF)
        out_long[...] = total[short:].astype(BF)


def whole(shape):
    zeros = (0,) * len(shape)
    return pl.BlockSpec(shape, lambda i: zeros, pipeline_mode=pl.Buffered(1))


def smem():
    return pl.BlockSpec(memory_space=pltpu.SMEM)


def vmem():
    return pl.BlockSpec(memory_space=pltpu.VMEM)


def vmem_call(
    kernel, name, ins, out_shape, mib, weight, scratch=(), aliases=None, far=(), scalars=()
):
    specs = [
        pl.BlockSpec(memory_space=pl.ANY) if i in far else smem() if i in scalars else vmem()
        for i in range(len(ins))
    ]
    return pl.pallas_call(
        kernel,
        in_specs=specs,
        out_specs=[vmem()] * len(out_shape),
        out_shape=out_shape,
        input_output_aliases=aliases or {},
        scratch_shapes=list(scratch),
        cost_estimate=cost(weight),
        compiler_params=pltpu.CompilerParams(vmem_limit_bytes=mib * MIB),
        name=name,
    )(*ins)


def struct(shape, dtype):
    return jax.ShapeDtypeStruct(shape, dtype)


def params(mib):
    return pltpu.CompilerParams(
        vmem_limit_bytes=mib * MIB, dimension_semantics=("arbitrary",)
    )


def cost(us):
    return pl.CostEstimate(
        flops=int(us * PEAK_PER_US * WEIGHT), bytes_accessed=0, transcendentals=0
    )


def update(grad, rate, weight, moment, average, outs, at=Ellipsis):
    moment_new = MOMENTUM * moment[at] + grad
    weight_new = weight.astype(F32) - rate * (grad + MOMENTUM * moment_new)
    outs[0][at] = grad
    outs[1][at] = moment_new
    outs[2][at] = weight_new
    outs[3][at] = AVERAGE * average[at] + (1.0 - AVERAGE) * weight_new


def total_of(pieces):
    total = pieces[0][...]
    for piece in pieces[1:]:
        total = total + piece[...].astype(F32)
    return total


def finish_kernel(kind, count, rates, *refs):
    pieces, rest = refs[:count], refs[count:]
    sets = len(rates)
    held = [rest[3 * i : 3 * i + 3] for i in range(sets)]
    outs = [rest[3 * sets + 4 * i : 3 * sets + 4 * i + 4] for i in range(sets)]
    if kind == "up":
        total = total_of(pieces)
        update(total[:, :D], rates[0], held[0][0][...], *held[0][1:], outs[0])
        update(total[:, D:], rates[1], held[1][0][...], *held[1][1:], outs[1])
    elif kind == "down":
        total = total_of(pieces)
        r = total.shape[0]
        weight = held[0][0][...].astype(F32)
        for slab in range(weight.shape[0] // r):
            at = slice(slab * r, (slab + 1) * r)
            grad = total[:, slab * D : (slab + 1) * D]
            update(grad, rates[0], weight[at], *held[0][1:], outs[0], at)
    else:
        total = total_of(pieces)
        r = total.shape[0]
        for k in range(3):
            for g in range(GROUPS):
                at = (k, slice(None), slice(g * GROUP, (g + 1) * GROUP))
                low = g * D + k * GROUP
                update(
                    total[:, low : low + GROUP], rates[0], held[0][0][at], *held[0][1:], outs[0], at
                )
        rest_rows = jnp.zeros((LANES - r, LANES), F32)
        turned = jnp.transpose(jnp.concatenate([total[:, GROUPS * D :], rest_rows], axis=0))
        for k in range(3):
            grad = turned[3 * k : 3 * k + 3, :r]
            update(grad, rates[1], held[1][0][k], *held[1][1:], outs[1], k)
        update(turned[9:11, :r], rates[2], held[2][0][...], *held[2][1:], outs[2])


def finish(kind, pieces, sets, rates, weight=1.5):
    flat = [array for one in sets for array in one]
    shapes = [one[0].shape for one in sets for _ in range(4)]
    outs = pl.pallas_call(
        functools.partial(finish_kernel, kind, len(pieces), rates),
        grid=(1,),
        in_specs=[whole(array.shape) for array in list(pieces) + flat],
        out_specs=[whole(shape) for shape in shapes],
        out_shape=[struct(shape, F32) for shape in shapes],
        cost_estimate=cost(weight),
        compiler_params=params(8),
        name="finish",
    )(*pieces, *flat)
    return [outs[4 * i : 4 * i + 4] for i in range(len(sets))]


def pack(attn_rows, conv_cols, gain_cols):
    shape = (attn_rows.shape[1], 3 * D + LANES)
    return pl.pallas_call(
        pack_kernel,
        grid=(1,),
        in_specs=[whole(array.shape) for array in (attn_rows, conv_cols, gain_cols)],
        out_specs=whole(shape),
        out_shape=struct(shape, BF),
        scratch_shapes=[pltpu.VMEM((LANES, LANES), F32)],
        cost_estimate=cost(1),
        compiler_params=params(56),
        name="pack",
    )(attn_rows, conv_cols, gain_cols)


def front(act_short, act_long, w_attn):
    short, rows = act_short.shape[0], act_short.shape[0] + act_long.shape[0]
    shapes = [
        struct((rows, D), BF),
        struct((16, D), F32),
        struct((3, rows, D), BF),
        struct((3, rows, D), BF),
        struct((rows, D), BF),
    ]
    kernel = functools.partial(front_kernel, short)
    return vmem_call(kernel, "front", [act_short, act_long, w_attn], shapes, 16, HEAVY)


def front_more(short, group, normed, small, w_attn, before):
    shapes = [struct(array.shape, array.dtype) for array in before]
    return vmem_call(
        functools.partial(front_more_kernel, short, group),
        "front_more",
        [normed, small, w_attn, *before],
        shapes,
        16,
        1,
        aliases={3 + i: i for i in range(len(before))},
    )


def up(act_short, act_long, cot_short, cot_long, len_short, len_long, attended, w_up, small, s):
    short, rows = act_short.shape[0], act_short.shape[0] + act_long.shape[0]
    tiles = range((w_up.shape[1] - D) // D // 2)
    halves_shape = struct(((w_up.shape[1] - D) // (2 * s), s, D), BF)
    return vmem_call(
        functools.partial(up_kernel, short, s, tiles),
        "up",
        [len_short, len_long, act_short, act_long, cot_short, cot_long, attended, w_up, small],
        [
            struct((rows, D), F32),
            struct((rows, D), BF),
            struct((rows, D), BF),
            struct((rows, len(tiles) * D), BF),
            halves_shape,
            halves_shape,
        ],
        16,
        HEAVY,
        scalars=(0, 1),
    )


def up_more(normed_two, upstream, w_up, s, before):
    rows = upstream.shape[0]
    count = (w_up.shape[1] - D) // D
    tiles = range(count // 2, count)
    return vmem_call(
        functools.partial(up_more_kernel, s, tiles),
        "up_more",
        [normed_two, upstream, w_up, *before],
        [struct(array.shape, array.dtype) for array in before]
        + [struct((rows, len(tiles) * D), BF)],
        16,
        HEAVY,
        aliases={3 + i: i for i in range(len(before))},
    )


def down(upstream, w_down, squared, w_up, normed_two, r):
    rows = upstream.shape[0]
    part = struct((D // (2 * r), r, w_up.shape[1]), BF)
    return vmem_call(
        functools.partial(down_kernel, r, range(1)),
        "down",
        [upstream, w_down, squared, w_up, normed_two],
        [part, part, struct((rows, D), F32)],
        16,
        HEAVY,
    )


def down_more(
    upstream, w_down, squared, more, w_up, normed_two, attended, middle, small, r, total, before
):
    rows = upstream.shape[0]
    count = w_down.shape[0] // D
    ins = [upstream, w_down, squared, more, w_up, normed_two, attended, middle, small, total]
    return vmem_call(
        functools.partial(down_more_kernel, r, range(1, count)),
        "down_more",
        ins + list(before),
        [struct(array.shape, array.dtype) for array in before]
        + [struct((rows, D), F32), struct((rows, D), BF), struct((8, D), F32)],
        16,
        HEAVY,
        aliases={len(ins) + i: i for i in range(len(before))},
    )


def mixer(
    short, r, group, mixed, projected, grad_branch, w_up, small, normed, w_attn, total=None,
    before=(), last=(),
):
    rows = grad_branch.shape[0]
    half = D // (2 * r)
    ins = [mixed, projected, grad_branch, w_up, small, normed, w_attn]
    if group > 0:
        ins = ins + [total]
    aliases = {}
    if group < GROUPS - 1:
        aliases = {len(ins) + i: i for i in range(len(before))}
        ins = ins + list(before)
        part = struct((half, r, (GROUPS - 1) * D), BF)
        out_shape = [part, part, struct((16, D), F32), struct((rows, D), F32)]
    else:
        act_short, act_long = last[:2]
        ins = ins + list(last)
        part = struct((half, r, D + LANES), BF)
        out_shape = [part, part, struct(act_short.shape, F32), struct(act_long.shape, F32)]
    return vmem_call(
        functools.partial(mixer_kernel, short, r, group),
        "mixer",
        ins,
        out_shape,
        16,
        2 if group == 1 else HEAVY,
        scratch=[
            pltpu.VMEM((3, rows, GROUP), F32),
            pltpu.VMEM((GROUP, D), BF),
            pltpu.SemaphoreType.DMA,
        ],
        aliases=aliases,
        far=(3,),
    )


def output(act_short, act_long, squared, more, w_down, middle):
    short, rows = act_short.shape[0], middle.shape[0]
    ff = w_down.shape[0]
    first = squared.shape[1] // D
    return pl.pallas_call(
        functools.partial(output_kernel, short, first),
        grid=(ff // D,),
        in_specs=[
            pl.BlockSpec((rows, D), lambda i: (0, jnp.minimum(i, first - 1))),
            pl.BlockSpec((rows, D), lambda i: (0, jnp.maximum(i - first, 0))),
            pl.BlockSpec((D, D), lambda i: (i, 0)),
            whole((rows, D)),
        ],
        out_specs=[whole(act_short.shape), whole(act_long.shape)],
        out_shape=[struct(act_short.shape, BF), struct(act_long.shape, BF)],
        scratch_shapes=[pltpu.VMEM((rows, D), F32)],
        cost_estimate=cost(HEAVY),
        compiler_params=params(12),
        name="output",
    )(squared, more, w_down, middle)


def shards(grid, *args):
    act_short, act_long, cot_short, cot_long, len_short, len_long = args[:6]
    owned = args[6:12]
    moments = args[12:18]
    averages = args[18:24]
    attn_rows, conv_cols, out_rows, up_rows, down_rows, gain_cols = owned
    r = out_rows.shape[0]
    s = down_rows.shape[0]
    short = act_short.shape[0]
    rows = short + act_long.shape[0]

    chunk_attn = pack(attn_rows, conv_cols, gain_cols)
    parts = s // r
    chunk_up = jnp.concatenate([out_rows, up_rows], axis=1)
    chunk_down = jnp.concatenate([down_rows[i * r : (i + 1) * r] for i in range(parts)], axis=1)
    wide, wide_up, wide_down = chunk_attn.shape[1], chunk_up.shape[1], chunk_down.shape[1]
    over_a, over_x, over_z = a_moves(grid), x_moves(grid), z_moves(grid)

    pieces = exchange(chunk_attn, over_z)
    (col_attn,) = place_z(grid, pieces, [(0, wide)])
    pieces_attn = exchange(col_attn, both_moves(grid))
    pieces_up = exchange(after(chunk_up, col_attn), over_z)
    plane_attn = place_both(grid, held_back(pieces_attn, *pieces_up[1:]))
    other_attn = swap(grid, plane_attn)
    up_low, up_high = halves(grid, held_back(pieces_up, plane_attn), wide_up)
    up_low, up_high = exchange(up_low, over_a), exchange(up_high, over_x)
    w_attn = join(grid, plane_attn, other_attn, wide)
    normed, small, *begun = front(act_short, act_long, w_attn)
    up_low, up_high = place_first(grid, held_back(up_low, normed), held_back(up_high, normed))
    pieces_down = exchange(after(chunk_down, up_low), over_z)
    up_low, up_high = exchange(up_low, over_x), exchange(up_high, over_a)
    begun = front_more(short, 1, after(normed, up_low[0]), small, w_attn, begun)
    down_low, down_high = halves(grid, held_back(pieces_down, begun[2]), wide_down)
    down_low, down_high = exchange(down_low, over_a), exchange(down_high, over_x)
    projected, mixed, attended = front_more(
        short, 2, after(normed, down_low[0]), small, w_attn, begun
    )
    plane_up = place_second(grid, held_back(up_low, attended), held_back(up_high, attended))
    other_up = swap(grid, plane_up)
    down_low, down_high = place_first(
        grid, held_back(down_low, plane_up), held_back(down_high, plane_up), HEAVY
    )
    down_low, down_high = exchange(down_low, over_x), exchange(down_high, over_a)
    w_up = join(grid, plane_up, after(other_up, down_low[0]), wide_up)
    middle, normed_two, upstream, squared, *begun = up(
        act_short, act_long, cot_short, cot_long, len_short, len_long, attended, w_up, small, s
    )
    plane_down = place_second(
        grid, held_back(down_low, normed_two), held_back(down_high, normed_two)
    )
    other_down = swap(grid, plane_down)
    kept_down, sent_down, more = up_more(
        after(normed_two, plane_down), upstream, w_up, s, begun
    )
    w_down = join(grid, plane_down, after(other_down, more), D)

    sent_down = swap(grid, sent_down)
    *begun, total = down(upstream, w_down, squared, w_up, normed_two, r)
    low_down, high_down = add_core(grid, kept_down, after(sent_down, total), D // 2)
    kept_up, sent_up, grad_middle, grad_branch, grad_gain_two = down_more(
        after(upstream, low_down[0]), w_down, squared, more, w_up, normed_two, attended, middle,
        small, r, total, begun,
    )
    sent_up = swap(grid, sent_up)
    low_down, high_down = add_plane(
        grid, held_back(low_down, grad_branch), held_back(high_down, grad_branch)
    )
    low_up, high_up = add_core(grid, kept_up, after(sent_up, low_down[0]), wide_up // 2)
    shared = (mixed, projected, grad_branch, w_up, small, normed, w_attn)
    *begun, total = mixer(
        short, r, 0, mixed, projected, after(grad_branch, low_up[0]), *shared[3:]
    )
    pieces_down = add_z(
        grid, r, [(held_back(low_down, total), held_back(high_down, total))]
    )
    kept_a, sent_a, grad_taps, total = mixer(
        short, r, 1, *shared, total=after(total, pieces_down[0]), before=begun
    )
    sent_a = swap(grid, sent_a)
    pieces_down = add_rest(grid, held_back(pieces_down, total))
    low_up, high_up = add_plane(
        grid, held_back(low_up, pieces_down[0]), held_back(high_up, pieces_down[0])
    )
    low_a, high_a = add_core(grid, kept_a, after(sent_a, low_up[0]), D)
    kept_b, sent_b, back_short, back_long = mixer(
        short, r, 2, *shared, total=after(total, low_a[0]),
        last=(act_short, act_long, grad_middle, grad_taps, grad_gain_two),
    )
    low_up, high_up = held_back(low_up, back_short), held_back(high_up, back_short)
    sent_b = swap(grid, sent_b)
    pieces_up = add_z(grid, r, [(held_back(low_up, back_short), held_back(high_up, back_short))])
    pieces_down = held_back(pieces_down, back_short)
    low_a, high_a = add_plane(
        grid,
        held_back(low_a, pieces_up[0], pieces_down[1]),
        held_back(high_a, pieces_up[0], pieces_down[1]),
    )
    pieces_b = add_both(grid, kept_b, after(sent_b, low_a[0]))
    out_short, out_long = output(
        act_short, act_long, squared, more, w_down, after(middle, pieces_b[0])
    )
    low_a, high_a = held_back(low_a, out_short), held_back(high_a, out_short)
    pieces_up = add_rest(grid, held_back(pieces_up, out_short))
    pieces_b = held_back(pieces_b, pieces_up[0])
    pieces_attn = add_z(grid, r, [(low_a, high_a), (pieces_b,)])
    pieces_up = held_back(pieces_up, pieces_attn[0])
    pieces_attn = add_rest(grid, held_back(pieces_attn, pieces_up[1]))
    scale_tokens = math.sqrt(rows * grid.a * grid.f)
    rates = [rate / scale_tokens for rate in RATES]
    sets = list(zip(owned, moments, averages))
    (done_down,) = finish("down", pieces_down, sets[4:5], rates[4:5])
    done_out, done_up = finish("up", pieces_up, sets[2:4], rates[2:4])
    done_attn, done_taps, done_gains = finish(
        "attn", pieces_attn, [sets[0], sets[1], sets[5]], [rates[0], rates[1], rates[5]]
    )
    results = [out_short, out_long, back_short, back_long]
    for done in (done_attn, done_taps, done_out, done_up, done_down, done_gains):
        results.extend(done)
    return tuple(results)


def solution(mesh):
    rows = P(AXES, None)
    weights = [P(None, AXES, None), P(None, None, AXES), rows, rows, rows, P(None, AXES)]
    in_specs = tuple([rows] * 4 + [P(AXES)] * 2 + weights * 3)
    out_specs = tuple([rows] * 4 + [spec for spec in weights for _ in range(4)])
    grid = Grid(mesh)

    def program(*args):
        return shards(grid, *args)

    return jax.shard_map(
        program, mesh=mesh, in_specs=in_specs, out_specs=out_specs, check_vma=False
    )
```

```python
import functools
import math

import jax
import jax.numpy as jnp
from jax import lax
from jax.experimental import pallas as pl
from jax.experimental.pallas import tpu as pltpu
from jax.sharding import PartitionSpec as P

D = 768
HEAD_DIM = 64
GROUP = 256
GROUPS = D // GROUP
BLOCK = 256
LANES = 128

EPS = 1e-06
MOMENTUM = 0.9
AVERAGE = 0.5
RATES = (0.03, 0.5, 0.6, 0.025, 0.007, 0.05)
NEG = -1e30
HEAD_SCALE = 0.125
AXES = ("dp", "fsdp")
BF = jnp.bfloat16
F32 = jnp.float32
MIB = 1024 * 1024
PEAK_PER_US = 1.15e9
WEIGHT = 1.0
HEAVY = 100


class Grid:
    def __init__(self, mesh):
        self.a = mesh.shape["dp"]
        self.f = mesh.shape["fsdp"]
        self.x = 2
        self.z = self.f // 4

    def index(self, a, z, x, c):
        return a * self.f + (z * self.x + x) * 2 + c

    def perm(self, move):
        pairs = []
        for a in range(self.a):
            for z in range(self.z):
                for x in range(self.x):
                    for c in range(2):
                        pairs.append((self.index(a, z, x, c), self.index(*move(a, z, x, c))))
        return pairs

    def swap_core(self):
        return self.perm(lambda a, z, x, c: (a, z, x, 1 - c))

    def shift_plane(self, da, dx):
        return self.perm(lambda a, z, x, c: ((a + da) % self.a, z, (x + dx) % self.x, c))

    def shift_z(self, dz):
        return self.perm(lambda a, z, x, c: (a, (z + dz) % self.z, x, c))

    def flip_z(self, bit):
        return self.perm(lambda a, z, x, c: (a, z ^ bit, x, c))

    def z_bits(self):
        bits, bit = [], 1
        while bit < self.z:
            bits.append(bit)
            bit *= 2
        return bits

    def here(self):
        f = lax.axis_index("fsdp")
        return lax.axis_index("dp"), f // 4, (f // 2) % 2, f % 2

    def plane_moves(self):
        return [(da, dx) for da in range(self.a) for dx in range(self.x) if da or dx]


def after(value, *others):
    return lax.optimization_barrier((value,) + others)[0]


def relay_kernel(grid, body, count, *refs):
    body(grid.here(), refs[:count], refs[count:])


def near_kernel(grid, body, steps, axes, count, *refs):
    for step in range(steps):
        views = [
            ref.at[(slice(None),) * axis + (slice(step, step + 1),)]
            for ref, axis in zip(refs, axes)
        ]
        body(grid.here(), views[:count], views[count:])


def near(grid, name, body, steps, ins, outs, weight=1):
    axes = [axis for _, axis in ins] + [axis for _, _, axis in outs]
    return vmem_call(
        functools.partial(near_kernel, grid, body, steps, axes, len(ins)),
        name,
        [array for array, _ in ins],
        [jax.ShapeDtypeStruct(shape, kind) for shape, kind, _ in outs],
        4,
        weight,
    )


def along(shape, axis):
    if axis is None:
        return pl.BlockSpec(shape, lambda i: (0,) * len(shape))
    block = tuple(1 if j == axis else size for j, size in enumerate(shape))
    return pl.BlockSpec(block, lambda i: tuple(i if j == axis else 0 for j in range(len(shape))))


def relay(grid, name, body, steps, ins, outs, weight=1):
    return pl.pallas_call(
        functools.partial(relay_kernel, grid, body, len(ins)),
        grid=(steps,),
        in_specs=[along(array.shape, axis) for array, axis in ins],
        out_specs=[along(shape, axis) for shape, _, axis in outs],
        out_shape=[jax.ShapeDtypeStruct(shape, kind) for shape, kind, _ in outs],
        cost_estimate=cost(weight),
        compiler_params=params(8),
        name=name,
    )(*[array for array, _ in ins])


def z_moves(grid):
    return [
        (
            grid.shift_z(dz),
            lambda a, z, x, c, dz=dz: ((z + dz) % grid.z,),
            lambda a, z, x, c, dz=dz: ((z - dz) % grid.z,),
        )
        for dz in range(1, grid.z)
    ]


def a_moves(grid):
    return [
        (
            grid.shift_plane(da, 0),
            lambda a, z, x, c, da=da: ((a + da) % grid.a,),
            lambda a, z, x, c, da=da: ((a - da) % grid.a,),
        )
        for da in range(1, grid.a)
    ]


def x_moves(grid):
    return [
        (
            grid.shift_plane(0, 1),
            lambda a, z, x, c: (1 - x,),
            lambda a, z, x, c: (1 - x,),
        )
    ]


def both_moves(grid):
    return [
        (
            grid.shift_plane(da, dx),
            lambda a, z, x, c, da=da, dx=dx: ((a + da) % grid.a, (x + dx) % grid.x),
            lambda a, z, x, c, da=da, dx=dx: ((a - da) % grid.a, (x - dx) % grid.x),
        )
        for da, dx in grid.plane_moves()
    ]


OWN_Z = lambda a, z, x, c: (z,)
OWN_A = lambda a, z, x, c: (a,)
OWN_X = lambda a, z, x, c: (x,)
OWN_AX = lambda a, z, x, c: (a, x)


def exchange(value, moves):
    return [value] + [lax.ppermute(value, AXES, pairs) for pairs, _, _ in moves]


def send(parts, moves):
    return [parts[0]] + [
        lax.ppermute(part, AXES, pairs) for part, (pairs, _, _) in zip(parts[1:], moves)
    ]


def swap(grid, value):
    return lax.ppermute(value, AXES, grid.swap_core())


def arrived(own, moves):
    return [own] + [brought for _, _, brought in moves]


def leaving(own, moves):
    return [own] + [sent for _, sent, _ in moves]


def held_back(pieces, *others):
    return [pieces[0]] + [after(piece, *others) for piece in pieces[1:]]


def place_z(grid, pieces, cuts):
    spots = arrived(OWN_Z, z_moves(grid))
    r = pieces[0].shape[0]

    def body(here, ins, outs):
        for piece, spot in zip(ins, spots):
            at = spot(*here)[0]
            for out, (low, high) in zip(outs, cuts):
                out[at] = piece[:, low:high]

    outs = [((grid.z, r, high - low), BF, None) for low, high in cuts]
    return relay(grid, "place_z", body, 1, [(piece, None) for piece in pieces], outs)


def flip(grid, value, bit):
    return lax.ppermute(value, AXES, grid.flip_z(bit))


def halves(grid, pieces, width):
    return place_z(grid, pieces, [(0, width // 2), (width // 2, width)])


def place_both(grid, pieces):
    spots = arrived(OWN_AX, both_moves(grid))

    def body(here, ins, outs):
        for piece, spot in zip(ins, spots):
            ia, ix = spot(*here)
            outs[0][ia, 0, ix] = piece[0]

    z, r, n = pieces[0].shape
    outs = [((grid.a, z, grid.x, r, n), BF, 1)]
    return relay(grid, "place_both", body, z, [(piece, 0) for piece in pieces], outs)[0]


def place_first(grid, over_a, over_x, weight=1):
    a_spots = arrived(OWN_A, a_moves(grid))
    x_spots = arrived(OWN_X, x_moves(grid))

    def body(here, ins, outs):
        for piece, spot in zip(ins, a_spots):
            outs[0][spot(*here)[0], 0] = piece[0]
        for piece, spot in zip(ins[len(a_spots) :], x_spots):
            outs[1][0, spot(*here)[0]] = piece[0]

    z, r, n = over_a[0].shape
    m = over_x[0].shape[-1]
    ins = [(piece, 0) for piece in over_a + over_x]
    outs = [((grid.a, z, r, n), BF, 1), ((z, grid.x, r, m), BF, 0)]
    return near(grid, "place_first", body, z, ins, outs, weight)


def place_second(grid, over_x, over_a):
    x_spots = arrived(OWN_X, x_moves(grid))
    a_spots = arrived(OWN_A, a_moves(grid))
    z, r, n = over_x[0].shape[1:]
    m = over_a[0].shape[-1]

    def body(here, ins, outs):
        for piece, spot in zip(ins, x_spots):
            for ia in range(grid.a):
                outs[0][ia, 0, spot(*here)[0], :, :n] = piece[ia, 0]
        for piece, spot in zip(ins[len(x_spots) :], a_spots):
            for ix in range(grid.x):
                outs[0][spot(*here)[0], 0, ix, :, n:] = piece[0, ix]

    ins = [(piece, 1) for piece in over_x] + [(piece, 0) for piece in over_a]
    outs = [((grid.a, z, grid.x, r, n + m), BF, 1)]
    return near(grid, "place_second", body, z, ins, outs)[0]


def join(grid, plane, other, width):
    r, n = plane.shape[-2:]
    parts = n // width
    owners = grid.a * grid.x

    def body(here, ins, outs):
        core = here[3]
        for source, at in ((ins[0], core), (ins[1], 1 - core)):
            for i in range(owners):
                for part in range(parts):
                    outs[0][0, i, at, part] = source[0, i, :, part * width : (part + 1) * width]

    plane, other = (
        array.reshape(grid.z, owners, r, n) for array in (plane, other)
    )
    outs = [((grid.z, owners, 2, parts, r, width), BF, 0)]
    (whole_array,) = relay(grid, "join", body, grid.z, [(plane, 0), (other, 0)], outs)
    return whole_array.reshape(-1, width)


def add_at(pieces, where):
    total = pieces[0][where].astype(F32)
    for piece in pieces[1:]:
        total = total + piece[where].astype(F32)
    return total


def add_core(grid, kept, got, cut):
    a_spots = leaving(OWN_A, a_moves(grid))
    x_spots = leaving(OWN_X, x_moves(grid))
    shape = (grid.a, grid.z, grid.x) + kept.shape[-2:]
    kept, got = kept.reshape(shape), got.reshape(shape)
    r, n = shape[-2:]
    low, high = slice(0, cut), slice(cut, n)

    def body(here, ins, outs):
        for out, spot in zip(outs, a_spots):
            for ix in range(grid.x):
                out[0, ix] = add_at(ins, (spot(*here)[0], 0, ix, slice(None), low)).astype(BF)
        for out, spot in zip(outs[len(a_spots) :], x_spots):
            for ia in range(grid.a):
                out[ia, 0] = add_at(ins, (ia, 0, spot(*here)[0], slice(None), high)).astype(BF)

    outs = [((grid.z, grid.x, r, cut), BF, 0)] * len(a_spots)
    outs += [((grid.a, grid.z, r, n - cut), BF, 1)] * len(x_spots)
    parts = near(grid, "add_core", body, grid.z, [(kept, 1), (got, 1)], outs)
    return (
        send(parts[: len(a_spots)], a_moves(grid)),
        send(parts[len(a_spots) :], x_moves(grid)),
    )


def add_plane(grid, low, high):
    x_spots = leaving(OWN_X, x_moves(grid))
    a_spots = leaving(OWN_A, a_moves(grid))
    z, _, r, n = low[0].shape
    m = high[0].shape[-1]

    def body(here, ins, outs):
        for out, spot in zip(outs, x_spots):
            out[0] = add_at(ins[: len(low)], (0, spot(*here)[0])).astype(BF)
        for out, spot in zip(outs[len(x_spots) :], a_spots):
            out[0] = add_at(ins[len(low) :], (spot(*here)[0], 0)).astype(BF)

    ins = [(piece, 0) for piece in low] + [(piece, 1) for piece in high]
    outs = [((z, r, n), BF, 0)] * len(x_spots) + [((z, r, m), BF, 0)] * len(a_spots)
    parts = near(grid, "add_plane", body, z, ins, outs, HEAVY)
    return (
        send(parts[: len(x_spots)], x_moves(grid)),
        send(parts[len(x_spots) :], a_moves(grid)),
    )


def add_both(grid, kept, got, weight=1):
    spots = leaving(OWN_AX, both_moves(grid))
    shape = (grid.a, grid.z, grid.x) + kept.shape[-2:]

    def body(here, ins, outs):
        for out, spot in zip(outs, spots):
            ia, ix = spot(*here)
            out[0] = add_at(ins, (ia, 0, ix)).astype(BF)

    ins = [(kept.reshape(shape), 1), (got.reshape(shape), 1)]
    outs = [((grid.z,) + shape[-2:], BF, 0)] * len(spots)
    return send(relay(grid, "add_both", body, grid.z, ins, outs, weight), both_moves(grid))


def add_z(grid, r, parts):
    lanes, end = [], 0
    for part in parts:
        widths = [half[0].shape[-1] for half in part]
        lanes.append((end, widths))
        end += sum(widths) * (part[0][0].shape[1] // r)
    count = grid.z // 2

    def body(here, ins, outs):
        mine = here[1] % 2
        for out, bit in ((outs[0], mine), (outs[1], 1 - mine)):
            for place in range(count):
                at, first = 2 * place + bit, 0
                for part, (start, widths) in zip(parts, lanes):
                    for i, half in enumerate(part):
                        total = add_at(ins[first : first + len(half)], at)
                        for slab in range(total.shape[0] // r):
                            low = start + slab * sum(widths) + sum(widths[:i])
                            piece = total[slab * r : (slab + 1) * r]
                            out[place, :, low : low + widths[i]] = piece.astype(BF)
                        first += len(half)

    ins = [(piece, None) for part in parts for half in part for piece in half]
    outs = [((count, r, end), BF, None)] * 2
    kept, sent = relay(grid, "add_z", body, 1, ins, outs)
    return [kept, flip(grid, sent, 1)]


def add_rest(grid, pieces):
    for bit in grid.z_bits()[1:]:
        count, r, n = pieces[0].shape
        last = count == 2

        def body(here, ins, outs):
            mine = (here[1] // bit) % 2
            for out, at in ((outs[0], mine), (outs[1], 1 - mine)):
                for place in range(count // 2):
                    where = Ellipsis if last else place
                    out[where] = add_at(ins, 2 * place + at).astype(out.dtype)

        shape = (r, n) if last else (count // 2, r, n)
        outs = [(shape, F32 if last else BF, None), (shape, BF, None)]
        kept, sent = relay(grid, "add_rest", body, 1, [(piece, None) for piece in pieces], outs)
        pieces = [kept, flip(grid, sent, bit)]
    return pieces


def dot(left, right):
    return lax.dot_general(left, right, (((1,), (0,)), ((), ())), preferred_element_type=F32)


def dot_bt(left, right):
    return lax.dot_general(left, right, (((1,), (1,)), ((), ())), preferred_element_type=F32)


def dot_at(left, right):
    return lax.dot_general(left, right, (((0,), (0,)), ((), ())), preferred_element_type=F32)


def rms_scale(values):
    return lax.rsqrt(jnp.mean(values * values, axis=-1, keepdims=True) + EPS)


def norm_back(values, gain, grad):
    scale = rms_scale(values)
    scaled = grad * gain
    inner = jnp.mean(scaled * values, axis=-1, keepdims=True)
    grad_gain = jnp.sum(grad * (values * scale), axis=0, keepdims=True)
    return scale * scaled - values * (scale * scale * scale * inner), grad_gain


def positions_of(rows, short, width):
    row = lax.broadcasted_iota(jnp.int32, (rows, width), 0)
    return jnp.where(row < short, row, row - short), row < short


def shift_down(values, offset, position):
    return jnp.where(position >= offset, pltpu.roll(values, offset, 0), 0.0)


def shift_up(values, offset, room):
    rows = values.shape[0]
    return jnp.where(room >= offset, pltpu.roll(values, rows - offset, 0), 0.0)


def head_mask(half):
    lane = lax.broadcasted_iota(jnp.int32, (1, LANES), 1)
    return (lane // HEAD_DIM) == half


def blocks_of(rows, short):
    found = []
    for start, length in ((0, short), (short, rows - short)):
        for block in range(length // BLOCK):
            found.append((start + block * BLOCK, start, (block + 1) * BLOCK))
    return found


def store_split(value, owner_rows, kept, sent, lanes=slice(None)):
    first = lax.axis_index("fsdp") % 2 == 0
    for pair in range(value.shape[0] // (2 * owner_rows)):
        at = 2 * pair * owner_rows
        even, odd = value[at : at + owner_rows], value[at + owner_rows : at + 2 * owner_rows]
        kept[pair, :, lanes] = jnp.where(first, even, odd).astype(BF)
        sent[pair, :, lanes] = jnp.where(first, odd, even).astype(BF)


def _():
            for pair in range(value.shape[0] // (2 * owner_rows)):
                at = 2 * pair * owner_rows
                first[pair, :, lanes] = value[at : at + owner_rows].astype(BF)
                second[pair, :, lanes] = value[at + owner_rows : at + 2 * owner_rows].astype(BF)


def front_kernel(short, xs, xl, w, normed, small, *refs):
    rows = normed.shape[0]
    turned = jnp.transpose(w[:, 3 * D : 3 * D + LANES].astype(F32))[:16]
    small[...] = turned
    gain = turned[9:10]
    for ref, first, count in ((xs, 0, short), (xl, short, rows - short)):
        x = ref[...].astype(F32)
        normed[first : first + count] = (x * rms_scale(x) * gain).astype(BF)
    front_group(short, 0, normed, small, w, *refs)


def front_more_kernel(short, group, normed, small, w, *refs):
    front_group(short, group, normed, small, w, *refs[-3:])


def front_group(short, group, normed, small, w, projected, mixed, attended):
    rows = normed.shape[0]
    columns = slice(group * GROUP, (group + 1) * GROUP)
    taps = small[:, columns]
    position, _ = positions_of(rows, short, GROUP)
    base = normed[...]
    for k in range(3):
        p = dot(base, w[:, k * D + group * GROUP : k * D + (group + 1) * GROUP])
        projected[k, :, columns] = p.astype(BF)
        mixed[k, :, columns] = (
            taps[3 * k : 3 * k + 1] * p
            + taps[3 * k + 1 : 3 * k + 2] * shift_down(p, 1, position)
            + taps[3 * k + 2 : 3 * k + 3] * shift_down(p, 2, position)
        ).astype(BF)
    for pair in range(GROUP // LANES):
        lane = group * GROUP + pair * LANES
        lanes = slice(lane, lane + LANES)
        for first, key_first, key_count in blocks_of(rows, short):
            queries = mixed[0, first : first + BLOCK, lanes]
            keys = mixed[1, key_first : key_first + key_count, lanes]
            values = mixed[2, key_first : key_first + key_count, lanes]
            row = lax.broadcasted_iota(jnp.int32, (BLOCK, key_count), 0) + (first - key_first)
            causal = lax.broadcasted_iota(jnp.int32, (BLOCK, key_count), 1) <= row
            total = None
            for half in range(2):
                scale = jnp.where(head_mask(half), HEAD_SCALE, 0.0).astype(BF)
                keep = jnp.where(head_mask(half), 1.0, 0.0).astype(BF)
                scores = jnp.where(causal, dot_bt(queries * scale, keys), NEG)
                peak = jnp.max(scores, axis=-1, keepdims=True)
                exponent = jnp.exp(scores - peak)
                weights = exponent * (1.0 / jnp.sum(exponent, axis=-1, keepdims=True))
                part = dot(weights.astype(BF), values * keep)
                total = part if total is None else total + part
            attended[first : first + BLOCK, lanes] = total.astype(BF)


def pack_kernel(attn, taps, gains, out, scratch):
    r = attn.shape[1]
    scratch[...] = jnp.zeros_like(scratch)
    for k in range(3):
        out[:, k * D : (k + 1) * D] = attn[k]
        scratch[3 * k : 3 * k + 3, :r] = taps[k].astype(F32)
    scratch[9:11, :r] = gains[...].astype(F32)
    out[:, 3 * D :] = jnp.transpose(scratch[...])[:r].astype(BF)


def up_tile(tile, column, owner_rows, normed, upstream, w, squared, kept, sent):
    columns = slice(column * D, (column + 1) * D)
    hidden = jnp.maximum(dot(normed[...], w[:, (1 + tile) * D : (2 + tile) * D]), 0.0)
    low = (hidden * hidden).astype(BF)
    squared[:, columns] = low
    half = D // (2 * owner_rows)
    mine = slice(tile * half, (tile + 1) * half)
    store_split(dot_at(low, upstream[...]), owner_rows, kept.at[mine], sent.at[mine])


def up_kernel(
    short, owner_rows, tiles, ls, ll, xs, xl, cs, cl, attended, w, small,
    middle, normed, upstream, squared, kept, sent,
):
    rows = normed.shape[0]
    gain = small[10:11]
    branch = dot(attended[...], w[:, :D])
    for ref, cot, limit, first, count in (
        (xs, cs, ls, 0, short),
        (xl, cl, ll, short, rows - short),
    ):
        part = slice(first, first + count)
        mid = ref[...].astype(F32) + branch[part]
        middle[part] = mid
        normed[part] = (mid * rms_scale(mid) * gain).astype(BF)
        position = lax.broadcasted_iota(jnp.int32, (count, D), 0)
        wide = jnp.where(position < limit[0], cot[...].astype(F32), 0.0)
        upstream[part] = wide.astype(BF)
    for i, tile in enumerate(tiles):
        up_tile(tile, i, owner_rows, normed, upstream, w, squared, kept, sent)


def up_more_kernel(owner_rows, tiles, normed, upstream, w, *refs):
    kept, sent, squared = refs[-3:]
    for i, tile in enumerate(tiles):
        up_tile(tile, i, owner_rows, normed, upstream, w, squared, kept, sent)


def down_tiles(tiles, owner_rows, upstream, w_down, squares, w_up, normed, kept, sent, total):
    count = squares[0].shape[1] // D
    for tile in tiles:
        squared, i = squares[tile // count], tile % count
        rows = slice(tile * D, (tile + 1) * D)
        lanes = slice((1 + tile) * D, (2 + tile) * D)
        grad_squared = dot_bt(upstream[...], w_down[rows])
        active = jnp.sqrt(squared[:, i * D : (i + 1) * D].astype(F32))
        grad_hidden = (grad_squared * (2.0 * active)).astype(BF)
        store_split(dot_at(normed[...], grad_hidden), owner_rows, kept, sent, lanes)
        part = dot_bt(grad_hidden, w_up[:, lanes])
        total = part if total is None else total + part
    return total


def down_kernel(owner_rows, tiles, upstream, w_down, squared, w_up, normed, kept, sent, total):
    total[...] = down_tiles(
        tiles, owner_rows, upstream, w_down, [squared], w_up, normed, kept, sent, None
    )


def down_more_kernel(
    owner_rows, tiles, upstream, w_down, squared, more, w_up, normed, attended, middle, small,
    before, *refs
):
    kept, sent, grad_middle, grad_branch, grad_gain = refs[-5:]
    total = down_tiles(
        tiles, owner_rows, upstream, w_down, [squared, more], w_up, normed, kept, sent, before[...]
    )
    pulled, gain = norm_back(middle[...], small[10:11], total)
    grad_gain[...] = jnp.broadcast_to(gain, grad_gain.shape)
    wide = upstream[...].astype(F32) + pulled
    grad_middle[...] = wide
    low = wide.astype(BF)
    grad_branch[...] = low
    store_split(dot_at(attended[...], low), owner_rows, kept, sent, slice(0, D))


def mixer_kernel(
    short, owner_rows, group, mixed, projected, branch, w_up, small, normed, w, *refs
):
    scratch, w_out, ready = refs[-3:]
    refs = refs[:-2]
    columns = slice(group * GROUP, (group + 1) * GROUP)
    fetch = pltpu.make_async_copy(w_up.at[columns, :D], w_out, ready)
    fetch.start()
    if group == 0:
        before = None
    else:
        before, refs = refs[0], refs[1:]
    if group < GROUPS - 1:
        kept, sent, taps_out, total = refs[-5:-1]
    else:
        xs, xl, grad_middle, taps_before, grad_gain_two = refs[:5]
        kept, sent, back_short, back_long = refs[-5:-1]
    rows = branch.shape[0]
    fetch.wait()
    grad_attended = dot_bt(branch[...], w_out[...]).astype(BF)
    for pair in range(GROUP // LANES):
        lanes = slice(pair * LANES, (pair + 1) * LANES)
        lane = group * GROUP + pair * LANES
        far = slice(lane, lane + LANES)
        started = set()
        for first, key_first, key_count in blocks_of(rows, short):
            block = slice(first, first + BLOCK)
            spread = slice(key_first, key_first + key_count)
            queries = mixed[0, block, far]
            keys = mixed[1, spread, far]
            values = mixed[2, spread, far]
            grads = grad_attended[block, lanes]
            row = lax.broadcasted_iota(jnp.int32, (key_count, BLOCK), 1) + (first - key_first)
            causal = lax.broadcasted_iota(jnp.int32, (key_count, BLOCK), 0) <= row
            for_queries = for_keys = for_values = None
            for half in range(2):
                scale = jnp.where(head_mask(half), HEAD_SCALE, 0.0).astype(BF)
                keep = jnp.where(head_mask(half), 1.0, 0.0).astype(BF)
                scaled = queries * scale
                own = grads * keep
                scores = jnp.where(causal, dot_bt(keys, scaled), NEG)
                peak = jnp.max(scores, axis=0, keepdims=True)
                exponent = jnp.exp(scores - peak)
                probs = exponent * (1.0 / jnp.sum(exponent, axis=0, keepdims=True))
                grad_probs = dot_bt(values, own)
                inner = jnp.sum(probs * grad_probs, axis=0, keepdims=True)
                grad_scores = (probs * (grad_probs - inner)).astype(BF)
                to_values = dot(probs.astype(BF), own)
                to_keys = dot(grad_scores, scaled)
                to_queries = dot_at(grad_scores, keys * scale)
                if half == 0:
                    for_queries, for_keys, for_values = to_queries, to_keys, to_values
                else:
                    for_queries = for_queries + to_queries
                    for_keys = for_keys + to_keys
                    for_values = for_values + to_values
            scratch[0, block, lanes] = for_queries
            for block_key in range(key_count // BLOCK):
                at = key_first + block_key * BLOCK
                inside = slice(block_key * BLOCK, (block_key + 1) * BLOCK)
                if at in started:
                    scratch[1, at : at + BLOCK, lanes] += for_keys[inside]
                    scratch[2, at : at + BLOCK, lanes] += for_values[inside]
                else:
                    started.add(at)
                    scratch[1, at : at + BLOCK, lanes] = for_keys[inside]
                    scratch[2, at : at + BLOCK, lanes] = for_values[inside]
    position, in_short = positions_of(rows, short, GROUP)
    room = jnp.where(in_short, short, rows - short) - 1 - position
    taps = small[:, columns]
    tap_rows = []
    grad_normed = None if before is None else before[...]
    for k in range(3):
        g = scratch[k]
        p = projected[k, :, columns].astype(F32)
        low = (
            taps[3 * k : 3 * k + 1] * g
            + taps[3 * k + 1 : 3 * k + 2] * shift_up(g, 1, room)
            + taps[3 * k + 2 : 3 * k + 3] * shift_up(g, 2, room)
        ).astype(BF)
        lane = (0 if group == GROUPS - 1 else group * D) + k * GROUP
        lanes = slice(lane, lane + GROUP)
        store_split(dot_at(normed[...], low), owner_rows, kept, sent, lanes)
        part = dot_bt(low, w[:, k * D + group * GROUP : k * D + (group + 1) * GROUP])
        grad_normed = part if grad_normed is None else grad_normed + part
        tap_rows.append(jnp.sum(g * p, axis=0, keepdims=True))
        for j in (1, 2):
            tap_rows.append(jnp.sum(g * shift_down(p, j, position), axis=0, keepdims=True))
    if group < GROUPS - 1:
        for i, row in enumerate(tap_rows):
            taps_out[i : i + 1, columns] = row
        total[...] = grad_normed
        return
    gain_sum = None
    for ref, out, first, count in (
        (xs, back_short, 0, short),
        (xl, back_long, short, rows - short),
    ):
        rows_of = slice(first, first + count)
        pulled, gain = norm_back(ref[...].astype(F32), small[9:10], grad_normed[rows_of])
        out[...] = grad_middle[rows_of] + pulled
        gain_sum = gain if gain_sum is None else gain_sum + gain
    row = lax.broadcasted_iota(jnp.int32, (LANES, GROUP), 0)
    for g in range(GROUPS):
        lanes = slice(g * GROUP, (g + 1) * GROUP)
        packed = jnp.where(row == 9, gain_sum[:, lanes], jnp.zeros((LANES, GROUP), F32))
        packed = jnp.where(row == 10, grad_gain_two[0:1, lanes], packed)
        for i, tap_row in enumerate(tap_rows):
            tap = tap_row if g == group else taps_before[i : i + 1, lanes]
            packed = jnp.where(row == i, tap, packed)
        packed_all = packed if g == 0 else jnp.concatenate([packed_all, packed], axis=1)
    store_split(jnp.transpose(packed_all), owner_rows, kept, sent, slice(D, D + LANES))


def output_kernel(short, first, squared, more, wdown, middle, out_short, out_long, total):
    step = pl.program_id(0)

    @pl.when(step == 0)
    def _():
        total[...] = middle[...] + dot(squared[...], wdown[...])

    @pl.when(jnp.logical_and(step > 0, step < first))
    def _():
        total[...] += dot(squared[...], wdown[...])

    @pl.when(step >= first)
    def _():
        total[...] += dot(more[...], wdown[...])

    @pl.when(step == pl.num_programs(0) - 1)
    def _():
        out_short[...] = total[:short].astype(BF)
        out_long[...] = total[short:].astype(BF)


def whole(shape):
    zeros = (0,) * len(shape)
    return pl.BlockSpec(shape, lambda i: zeros, pipeline_mode=pl.Buffered(1))


def smem():
    return pl.BlockSpec(memory_space=pltpu.SMEM)


def vmem():
    return pl.BlockSpec(memory_space=pltpu.VMEM)


def vmem_call(
    kernel, name, ins, out_shape, mib, weight, scratch=(), aliases=None, far=(), scalars=()
):
    specs = [
        pl.BlockSpec(memory_space=pl.ANY) if i in far else smem() if i in scalars else vmem()
        for i in range(len(ins))
    ]
    return pl.pallas_call(
        kernel,
        in_specs=specs,
        out_specs=[vmem()] * len(out_shape),
        out_shape=out_shape,
        input_output_aliases=aliases or {},
        scratch_shapes=list(scratch),
        cost_estimate=cost(weight),
        compiler_params=pltpu.CompilerParams(vmem_limit_bytes=mib * MIB),
        name=name,
    )(*ins)


def struct(shape, dtype):
    return jax.ShapeDtypeStruct(shape, dtype)


def params(mib):
    return pltpu.CompilerParams(
        vmem_limit_bytes=mib * MIB, dimension_semantics=("arbitrary",)
    )


def cost(us):
    return pl.CostEstimate(
        flops=int(us * PEAK_PER_US * WEIGHT), bytes_accessed=0, transcendentals=0
    )


def update(grad, rate, weight, moment, average, outs, at=Ellipsis):
    moment_new = MOMENTUM * moment[at] + grad
    weight_new = weight.astype(F32) - rate * (grad + MOMENTUM * moment_new)
    outs[0][at] = grad
    outs[1][at] = moment_new
    outs[2][at] = weight_new
    outs[3][at] = AVERAGE * average[at] + (1.0 - AVERAGE) * weight_new


def total_of(pieces):
    total = pieces[0][...]
    for piece in pieces[1:]:
        total = total + piece[...].astype(F32)
    return total


def finish_kernel(kind, count, rates, *refs):
    pieces, rest = refs[:count], refs[count:]
    sets = len(rates)
    held = [rest[3 * i : 3 * i + 3] for i in range(sets)]
    outs = [rest[3 * sets + 4 * i : 3 * sets + 4 * i + 4] for i in range(sets)]
    if kind == "up":
        total = total_of(pieces)
        update(total[:, :D], rates[0], held[0][0][...], *held[0][1:], outs[0])
        update(total[:, D:], rates[1], held[1][0][...], *held[1][1:], outs[1])
    elif kind == "down":
        total = total_of(pieces)
        r = total.shape[0]
        weight = held[0][0][...].astype(F32)
        for slab in range(weight.shape[0] // r):
            at = slice(slab * r, (slab + 1) * r)
            grad = total[:, slab * D : (slab + 1) * D]
            update(grad, rates[0], weight[at], *held[0][1:], outs[0], at)
    else:
        total = total_of(pieces)
        r = total.shape[0]
        for k in range(3):
            for g in range(GROUPS):
                at = (k, slice(None), slice(g * GROUP, (g + 1) * GROUP))
                low = g * D + k * GROUP
                update(
                    total[:, low : low + GROUP], rates[0], held[0][0][at], *held[0][1:], outs[0], at
                )
        rest_rows = jnp.zeros((LANES - r, LANES), F32)
        turned = jnp.transpose(jnp.concatenate([total[:, GROUPS * D :], rest_rows], axis=0))
        for k in range(3):
            grad = turned[3 * k : 3 * k + 3, :r]
            update(grad, rates[1], held[1][0][k], *held[1][1:], outs[1], k)
        update(turned[9:11, :r], rates[2], held[2][0][...], *held[2][1:], outs[2])


def finish(kind, pieces, sets, rates, weight=1.5):
    flat = [array for one in sets for array in one]
    shapes = [one[0].shape for one in sets for _ in range(4)]
    outs = pl.pallas_call(
        functools.partial(finish_kernel, kind, len(pieces), rates),
        grid=(1,),
        in_specs=[whole(array.shape) for array in list(pieces) + flat],
        out_specs=[whole(shape) for shape in shapes],
        out_shape=[struct(shape, F32) for shape in shapes],
        cost_estimate=cost(weight),
        compiler_params=params(8),
        name="finish",
    )(*pieces, *flat)
    return [outs[4 * i : 4 * i + 4] for i in range(len(sets))]


def pack(attn_rows, conv_cols, gain_cols):
    shape = (attn_rows.shape[1], 3 * D + LANES)
    return pl.pallas_call(
        pack_kernel,
        grid=(1,),
        in_specs=[whole(array.shape) for array in (attn_rows, conv_cols, gain_cols)],
        out_specs=whole(shape),
        out_shape=struct(shape, BF),
        scratch_shapes=[pltpu.VMEM((LANES, LANES), F32)],
        cost_estimate=cost(1),
        compiler_params=params(56),
        name="pack",
    )(attn_rows, conv_cols, gain_cols)


def front(act_short, act_long, w_attn):
    short, rows = act_short.shape[0], act_short.shape[0] + act_long.shape[0]
    shapes = [
        struct((rows, D), BF),
        struct((16, D), F32),
        struct((3, rows, D), BF),
        struct((3, rows, D), BF),
        struct((rows, D), BF),
    ]
    kernel = functools.partial(front_kernel, short)
    return vmem_call(kernel, "front", [act_short, act_long, w_attn], shapes, 16, HEAVY)


def front_more(short, group, normed, small, w_attn, before):
    shapes = [struct(array.shape, array.dtype) for array in before]
    return vmem_call(
        functools.partial(front_more_kernel, short, group),
        "front_more",
        [normed, small, w_attn, *before],
        shapes,
        8,
        1,
        aliases={3 + i: i for i in range(len(before))},
    )


def up(act_short, act_long, cot_short, cot_long, len_short, len_long, attended, w_up, small, s):
    short, rows = act_short.shape[0], act_short.shape[0] + act_long.shape[0]
    tiles = range((w_up.shape[1] - D) // D // 2)
    halves_shape = struct(((w_up.shape[1] - D) // (2 * s), s, D), BF)
    return vmem_call(
        functools.partial(up_kernel, short, s, tiles),
        "up",
        [len_short, len_long, act_short, act_long, cot_short, cot_long, attended, w_up, small],
        [
            struct((rows, D), F32),
            struct((rows, D), BF),
            struct((rows, D), BF),
            struct((rows, len(tiles) * D), BF),
            halves_shape,
            halves_shape,
        ],
        8,
        HEAVY,
        scalars=(0, 1),
    )


def up_more(normed_two, upstream, w_up, s, before):
    rows = upstream.shape[0]
    count = (w_up.shape[1] - D) // D
    tiles = range(count // 2, count)
    return vmem_call(
        functools.partial(up_more_kernel, s, tiles),
        "up_more",
        [normed_two, upstream, w_up, *before],
        [struct(array.shape, array.dtype) for array in before]
        + [struct((rows, len(tiles) * D), BF)],
        8,
        HEAVY,
        aliases={3 + i: i for i in range(len(before))},
    )


def down(upstream, w_down, squared, w_up, normed_two, r):
    rows = upstream.shape[0]
    part = struct((D // (2 * r), r, w_up.shape[1]), BF)
    return vmem_call(
        functools.partial(down_kernel, r, range(1)),
        "down",
        [upstream, w_down, squared, w_up, normed_two],
        [part, part, struct((rows, D), F32)],
        8,
        HEAVY,
    )


def down_more(
    upstream, w_down, squared, more, w_up, normed_two, attended, middle, small, r, total, before
):
    rows = upstream.shape[0]
    count = w_down.shape[0] // D
    ins = [upstream, w_down, squared, more, w_up, normed_two, attended, middle, small, total]
    return vmem_call(
        functools.partial(down_more_kernel, r, range(1, count)),
        "down_more",
        ins + list(before),
        [struct(array.shape, array.dtype) for array in before]
        + [struct((rows, D), F32), struct((rows, D), BF), struct((8, D), F32)],
        8,
        HEAVY,
        aliases={len(ins) + i: i for i in range(len(before))},
    )


def mixer(
    short, r, group, mixed, projected, grad_branch, w_up, small, normed, w_attn, total=None,
    before=(), last=(),
):
    rows = grad_branch.shape[0]
    half = D // (2 * r)
    ins = [mixed, projected, grad_branch, w_up, small, normed, w_attn]
    if group > 0:
        ins = ins + [total]
    aliases = {}
    if group < GROUPS - 1:
        aliases = {len(ins) + i: i for i in range(len(before))}
        ins = ins + list(before)
        part = struct((half, r, (GROUPS - 1) * D), BF)
        out_shape = [part, part, struct((16, D), F32), struct((rows, D), F32)]
    else:
        act_short, act_long = last[:2]
        ins = ins + list(last)
        part = struct((half, r, D + LANES), BF)
        out_shape = [part, part, struct(act_short.shape, F32), struct(act_long.shape, F32)]
    return vmem_call(
        functools.partial(mixer_kernel, short, r, group),
        "mixer",
        ins,
        out_shape,
        14,
        2 if group == 1 else HEAVY,
        scratch=[
            pltpu.VMEM((3, rows, GROUP), F32),
            pltpu.VMEM((GROUP, D), BF),
            pltpu.SemaphoreType.DMA,
        ],
        aliases=aliases,
        far=(3,),
    )


def output(act_short, act_long, squared, more, w_down, middle):
    short, rows = act_short.shape[0], middle.shape[0]
    ff = w_down.shape[0]
    first = squared.shape[1] // D
    return pl.pallas_call(
        functools.partial(output_kernel, short, first),
        grid=(ff // D,),
        in_specs=[
            pl.BlockSpec((rows, D), lambda i: (0, jnp.minimum(i, first - 1))),
            pl.BlockSpec((rows, D), lambda i: (0, jnp.maximum(i - first, 0))),
            pl.BlockSpec((D, D), lambda i: (i, 0)),
            whole((rows, D)),
        ],
        out_specs=[whole(act_short.shape), whole(act_long.shape)],
        out_shape=[struct(act_short.shape, BF), struct(act_long.shape, BF)],
        scratch_shapes=[pltpu.VMEM((rows, D), F32)],
        cost_estimate=cost(HEAVY),
        compiler_params=params(12),
        name="output",
    )(squared, more, w_down, middle)


def shards(grid, *args):
    act_short, act_long, cot_short, cot_long, len_short, len_long = args[:6]
    owned = args[6:12]
    moments = args[12:18]
    averages = args[18:24]
    attn_rows, conv_cols, out_rows, up_rows, down_rows, gain_cols = owned
    r = out_rows.shape[0]
    s = down_rows.shape[0]
    short = act_short.shape[0]
    rows = short + act_long.shape[0]

    chunk_attn = pack(attn_rows, conv_cols, gain_cols)
    parts = s // r
    chunk_up = jnp.concatenate([out_rows, up_rows], axis=1)
    chunk_down = jnp.concatenate([down_rows[i * r : (i + 1) * r] for i in range(parts)], axis=1)
    wide, wide_up, wide_down = chunk_attn.shape[1], chunk_up.shape[1], chunk_down.shape[1]
    over_a, over_x, over_z = a_moves(grid), x_moves(grid), z_moves(grid)

    pieces = exchange(chunk_attn, over_z)
    (col_attn,) = place_z(grid, pieces, [(0, wide)])
    pieces_attn = exchange(col_attn, both_moves(grid))
    pieces_up = exchange(after(chunk_up, col_attn), over_z)
    plane_attn = place_both(grid, held_back(pieces_attn, *pieces_up[1:]))
    other_attn = swap(grid, plane_attn)
    up_low, up_high = halves(grid, held_back(pieces_up, plane_attn), wide_up)
    up_low, up_high = exchange(up_low, over_a), exchange(up_high, over_x)
    w_attn = join(grid, plane_attn, other_attn, wide)
    normed, small, *begun = front(act_short, act_long, w_attn)
    up_low, up_high = place_first(grid, held_back(up_low, normed), held_back(up_high, normed))
    pieces_down = exchange(after(chunk_down, up_low), over_z)
    up_low, up_high = exchange(up_low, over_x), exchange(up_high, over_a)
    begun = front_more(short, 1, after(normed, up_low[0]), small, w_attn, begun)
    projected, mixed, attended = front_more(short, 2, normed, small, w_attn, begun)
    plane_up = place_second(grid, held_back(up_low, attended), held_back(up_high, attended))
    other_up = swap(grid, plane_up)
    down_low, down_high = halves(grid, held_back(pieces_down, plane_up), wide_down)
    down_low, down_high = exchange(down_low, over_a), exchange(down_high, over_x)
    down_low, down_high = place_first(grid, down_low, down_high, HEAVY)
    down_low, down_high = exchange(down_low, over_x), exchange(down_high, over_a)
    w_up = join(grid, plane_up, after(other_up, down_low[0]), wide_up)
    middle, normed_two, upstream, squared, *begun = up(
        act_short, act_long, cot_short, cot_long, len_short, len_long, attended, w_up, small, s
    )
    kept_down, sent_down, more = up_more(normed_two, upstream, w_up, s, begun)
    sent_down = swap(grid, sent_down)
    plane_down = place_second(grid, held_back(down_low, more), held_back(down_high, more))
    other_down = swap(grid, plane_down)

    low_down, high_down = add_core(grid, kept_down, after(sent_down, plane_down), D // 2)
    w_down = join(grid, plane_down, after(other_down, low_down[0]), D)
    *begun, total = down(upstream, w_down, squared, w_up, normed_two, r)
    kept_up, sent_up, grad_middle, grad_branch, grad_gain_two = down_more(
        after(upstream, low_down[0]), w_down, squared, more, w_up, normed_two, attended, middle,
        small, r, total, begun,
    )
    sent_up = swap(grid, sent_up)
    low_down, high_down = add_plane(
        grid, held_back(low_down, grad_branch), held_back(high_down, grad_branch)
    )
    low_up, high_up = add_core(grid, kept_up, after(sent_up, low_down[0]), wide_up // 2)
    shared = (mixed, projected, grad_branch, w_up, small, normed, w_attn)
    *begun, total = mixer(
        short, r, 0, mixed, projected, after(grad_branch, low_up[0]), *shared[3:]
    )
    pieces_down = add_z(
        grid, r, [(held_back(low_down, total), held_back(high_down, total))]
    )
    kept_a, sent_a, grad_taps, total = mixer(
        short, r, 1, *shared, total=after(total, pieces_down[0]), before=begun
    )
    sent_a = swap(grid, sent_a)
    pieces_down = add_rest(grid, held_back(pieces_down, total))
    low_up, high_up = add_plane(
        grid, held_back(low_up, pieces_down[0]), held_back(high_up, pieces_down[0])
    )
    low_a, high_a = add_core(grid, kept_a, after(sent_a, low_up[0]), D)
    kept_b, sent_b, back_short, back_long = mixer(
        short, r, 2, *shared, total=after(total, low_a[0]),
        last=(act_short, act_long, grad_middle, grad_taps, grad_gain_two),
    )
    low_up, high_up = held_back(low_up, back_short), held_back(high_up, back_short)
    sent_b = swap(grid, sent_b)
    pieces_up = add_z(grid, r, [(held_back(low_up, back_short), held_back(high_up, back_short))])
    pieces_down = held_back(pieces_down, back_short)
    low_a, high_a = add_plane(
        grid,
        held_back(low_a, pieces_up[0], pieces_down[1]),
        held_back(high_a, pieces_up[0], pieces_down[1]),
    )
    pieces_b = add_both(grid, kept_b, after(sent_b, low_a[0]))
    out_short, out_long = output(
        act_short, act_long, squared, more, w_down, after(middle, pieces_b[0])
    )
    low_a, high_a = held_back(low_a, out_short), held_back(high_a, out_short)
    pieces_up = add_rest(grid, held_back(pieces_up, out_short))
    pieces_b = held_back(pieces_b, pieces_up[0])
    pieces_attn = add_z(grid, r, [(low_a, high_a), (pieces_b,)])
    pieces_up = held_back(pieces_up, pieces_attn[0])
    pieces_attn = add_rest(grid, held_back(pieces_attn, pieces_up[1]))
    scale_tokens = math.sqrt(rows * grid.a * grid.f)
    rates = [rate / scale_tokens for rate in RATES]
    sets = list(zip(owned, moments, averages))
    (done_down,) = finish("down", pieces_down, sets[4:5], rates[4:5])
    done_out, done_up = finish("up", pieces_up, sets[2:4], rates[2:4])
    done_attn, done_taps, done_gains = finish(
        "attn", pieces_attn, [sets[0], sets[1], sets[5]], [rates[0], rates[1], rates[5]]
    )
    results = [out_short, out_long, back_short, back_long]
    for done in (done_attn, done_taps, done_out, done_up, done_down, done_gains):
        results.extend(done)
    return tuple(results)


def solution(mesh):
    rows = P(AXES, None)
    weights = [P(None, AXES, None), P(None, None, AXES), rows, rows, rows, P(None, AXES)]
    in_specs = tuple([rows] * 4 + [P(AXES)] * 2 + weights * 3)
    out_specs = tuple([rows] * 4 + [spec for spec in weights for _ in range(4)])
    grid = Grid(mesh)

    def program(*args):
        return shards(grid, *args)

    return jax.shard_map(
        program, mesh=mesh, in_specs=in_specs, out_specs=out_specs, check_vma=False
    )
```
